512 devices in a mesh: row: 16 (over z, core), col: 32 (over y, x).
Axes of the slice: x: 4, y: 8, z: 8, core: 2. Of those that a mesh axis runs over, the one named last changes fastest.
Arguments:
- train_embed: bfloat16 [8192, 256], P(('row', 'col')), may hold values from -16 to 16
- valid_embed: bfloat16 [65536, 256], P(('row', 'col')), may hold values from -16 to 16
- train_labels: int32 [8192], P(('row', 'col')), may hold values from 0 to 99
- valid_labels: int32 [65536], P(('row', 'col')), may hold values from 0 to 99
- pair_level: int32 [100, 100], replicated, may hold values from 0 to 3
- level_cost: float32 [4], replicated, may hold values from 0.05 to 1
Outputs:
- calibrated: float32 [8192], P('row')
The draws below stay inside these ranges and needn't reach their ends.
All inputs are finite; a program needn't handle non-finite values.
Results may differ from the reference program's by a relative error of at most 0.0003.
Values may be sent and summed in bfloat16 or wider, within the bound.
No kernel may reach another device: no remote copies, remote signals or barrier semaphores. Data moves between devices by JAX's collectives and lax.ppermute only.
A program may use at most 64 MiB of HBM per device.

```python
import math
import jax
import jax.numpy as jnp
import numpy as np
from jax import lax

EMBED = 256
CLASSES = 100
LEVELS = 4
ITERS = 4
TRAIN_PTS = 8192
VALID_PTS = 65536


def embed_pair(key):
    base = jax.random.fold_in(key, 7)
    train_draw = jax.random.normal(jax.random.fold_in(base, 1), (TRAIN_PTS, EMBED), jnp.float32)
    valid_draw = jax.random.normal(jax.random.fold_in(base, 2), (VALID_PTS, EMBED), jnp.float32)
    return (jnp.clip(train_draw, -16.0, 16.0), jnp.clip(valid_draw, -16.0, 16.0))


def draw_train_embed(key, part):
    return embed_pair(key)[0].astype(jnp.bfloat16)


def draw_valid_embed(key, part):
    return embed_pair(key)[1].astype(jnp.bfloat16)


def place_ends(entries, stream_key, smallest, largest):
    extent = entries.shape
    index_at = [jax.random.randint(jax.random.fold_in(stream_key, axis), (), 0, extent[axis]) for axis in range(len(extent))]
    entries = entries.at[tuple(index_at)].set(smallest)
    longest = extent.index(max(extent))
    index_at[longest] = (index_at[longest] + 1) % extent[longest]
    return entries.at[tuple(index_at)].set(largest)


def cumulative_ranks(amount, lean):
    portions = [(1 << 20) // math.isqrt(grade ** lean) + 1 for grade in range(1, amount + 1)]
    spread = 1 + sum(portions) // (1 << 30)
    return np.cumsum(np.array([max(1, weight // spread) for weight in portions]))


def ranked_ids(stream_key, extent, amount, lean):
    table = cumulative_ranks(amount, lean)
    lot = jax.random.randint(jax.random.fold_in(stream_key, 1), extent, 0, int(table[amount - 1]))
    rank = jnp.searchsorted(jnp.asarray(table, jnp.int32), lot, side="right")
    return jax.random.permutation(jax.random.fold_in(stream_key, 2), amount)[rank].astype(jnp.int32)


def setup_inputs(seed: int = 0) -> dict:
    arg_keys = jax.random.split(jax.random.key(seed), 7)
    return {
        "train_embed": draw_train_embed(jax.random.fold_in(arg_keys[6], 71), 0),
        "valid_embed": draw_valid_embed(jax.random.fold_in(arg_keys[6], 71), 0),
        "train_labels": place_ends(ranked_ids(arg_keys[2], (TRAIN_PTS,), CLASSES, 2), jax.random.fold_in(arg_keys[2], 3), 0, CLASSES - 1).astype(jnp.int32),
        "valid_labels": place_ends(ranked_ids(arg_keys[3], (VALID_PTS,), CLASSES, 2), jax.random.fold_in(arg_keys[3], 3), 0, CLASSES - 1).astype(jnp.int32),
        "pair_level": place_ends(jax.random.randint(arg_keys[4], (CLASSES, CLASSES), 0, LEVELS), jax.random.fold_in(arg_keys[4], 1), 0, LEVELS - 1).astype(jnp.int32),
        "level_cost": jnp.clip(jnp.exp(jax.random.uniform(arg_keys[5], (LEVELS,), jnp.float32, math.log(0.05), math.log(1.0))), 0.05, 1.0),
    }


entropy_scale = 0.05


def class_costs(pair_level, level_cost):
    selected = (pair_level[:, :, None] == jnp.arange(LEVELS, dtype=jnp.int32)[None, None, :]).astype(jnp.float32)
    return jnp.sum(selected * level_cost[None, None, :], axis=2)


def reference(train_embed, valid_embed, train_labels, valid_labels, pair_level, level_cost):
    class_table = class_costs(pair_level, level_cost)
    train_wide = train_embed.astype(jnp.float32)
    train_sq = jnp.sum(train_wide * train_wide, axis=1)
    row_labels = class_table[train_labels]
    block_cols = min(512, VALID_PTS)
    block_count = VALID_PTS // block_cols
    valid_blocks = valid_embed.reshape(block_count, block_cols, EMBED)
    label_blocks = valid_labels.reshape(block_count, block_cols)
    row_pot = jnp.zeros((TRAIN_PTS,), jnp.float32)
    col_pot = jnp.zeros((VALID_PTS,), jnp.float32)
    for iteration in range(ITERS):
        def visit(running, inputs, row_pot=row_pot):
            block_y, block_labels, block_pot = inputs
            block_wide = block_y.astype(jnp.float32)
            block_sq = jnp.sum(block_wide * block_wide, axis=1)
            products = jnp.dot(train_embed, block_y.T, preferred_element_type=jnp.float32)
            cost_tile = (train_sq[:, None] + block_sq[None, :] - 2.0 * products) / EMBED + row_labels[:, block_labels]
            row_side = (block_pot[None, :] - cost_tile) / entropy_scale
            col_side = (row_pot[:, None] - cost_tile) / entropy_scale
            return jnp.logaddexp(running, jax.nn.logsumexp(row_side, axis=1)), jax.nn.logsumexp(col_side, axis=0)

        start_lse = jnp.full((TRAIN_PTS,), -jnp.inf, jnp.float32)
        row_lse, col_lse = lax.scan(visit, start_lse, (valid_blocks, label_blocks, col_pot.reshape(block_count, block_cols)))
        col_lse = col_lse.reshape(VALID_PTS)
        row_new = entropy_scale * math.log(VALID_PTS) - entropy_scale * row_lse
        col_new = entropy_scale * math.log(TRAIN_PTS) - entropy_scale * col_lse
        row_pot = 0.5 * (row_pot + row_new)
        col_pot = 0.5 * (col_pot + col_new)
    potential_sum = jnp.sum(row_pot)
    return (row_pot * TRAIN_PTS - potential_sum) / (TRAIN_PTS - 1)
```

```python
import math

import jax
import jax.numpy as jnp
from jax import lax
from jax.experimental import pallas as pl
from jax.experimental.pallas import tpu as pltpu
from jax.sharding import PartitionSpec as P

ITERS = 4
LANES = 128
SUB = 8

entropy_scale = 0.05
UNIT = entropy_scale * math.log(2.0)

VMEM = pl.BlockSpec(memory_space=pltpu.VMEM)


def lse_lead(parts):
    high = jnp.max(parts, axis=0)
    return high + jnp.log2(jnp.sum(jnp.exp2(parts - high[None]), axis=0))


def spread_rows(values, out_ref):
    for a in range(values.shape[0]):
        block = jnp.broadcast_to(values[a : a + 1, :], (LANES, LANES))
        out_ref[a * LANES : (a + 1) * LANES, :] = block.T


def lanes_of(ref, combine):
    rows = []
    for a in range(ref.shape[0] // LANES):
        block = ref[a * LANES : (a + 1) * LANES, :].T
        rows.append(combine(block, axis=0, keepdims=True))
    return jnp.concatenate(rows, axis=0)


def col_partial(cost_ref, row_ref):
    rows, cols = cost_ref.shape
    chunks = cols // LANES

    def tile(g, k, base):
        cell = cost_ref[pl.ds(g * SUB, SUB), k * LANES : (k + 1) * LANES]
        return -cell if base is None else base - cell

    def base_of(g):
        return None if row_ref is None else row_ref[pl.ds(pl.multiple_of(g * SUB, SUB), SUB), :]

    def peaks(g, high):
        g = pl.multiple_of(g, 1)
        base = base_of(g)
        return tuple(jnp.maximum(high[k], tile(g, k, base)) for k in range(chunks))

    start = tuple(jnp.full((SUB, LANES), -jnp.inf, jnp.float32) for _ in range(chunks))
    high = lax.fori_loop(0, rows // SUB, peaks, start, unroll=4)
    high = tuple(jnp.max(h, axis=0, keepdims=True) for h in high)

    def totals(g, total):
        base = base_of(g)
        return tuple(total[k] + jnp.exp2(tile(g, k, base) - high[k]) for k in range(chunks))

    zero = tuple(jnp.zeros((SUB, LANES), jnp.float32) for _ in range(chunks))
    total = lax.fori_loop(0, rows // SUB, totals, zero, unroll=4)
    return jnp.concatenate(
        [high[k] + jnp.log2(jnp.sum(total[k], axis=0, keepdims=True)) for k in range(chunks)], axis=0
    )


def row_partial(cost_ref, col, high_ref, total_ref):
    rows, cols = cost_ref.shape
    chunks = cols // LANES

    def tile(g, k):
        cell = cost_ref[pl.ds(g * SUB, SUB), k * LANES : (k + 1) * LANES]
        return -cell if col is None else col[k : k + 1, :] - cell

    def peaks(g, carry):
        high = tile(g, 0)
        for k in range(1, chunks):
            high = jnp.maximum(high, tile(g, k))
        high_ref[pl.ds(pl.multiple_of(g * SUB, SUB), SUB), :] = jnp.broadcast_to(
            jnp.max(high, axis=1, keepdims=True), (SUB, LANES)
        )
        return carry

    lax.fori_loop(0, rows // SUB, peaks, 0, unroll=4)

    def totals(g, carry):
        here = pl.ds(pl.multiple_of(g * SUB, SUB), SUB)
        high = high_ref[here, :]
        total = jnp.exp2(tile(g, 0) - high)
        for k in range(1, chunks):
            total = total + jnp.exp2(tile(g, k) - high)
        total_ref[here, :] = total
        return carry

    lax.fori_loop(0, rows // SUB, totals, 0, unroll=4)
    return lanes_of(high_ref, jnp.max) + jnp.log2(lanes_of(total_ref, jnp.sum))


def split3(values):
    high = values.astype(jnp.bfloat16)
    rest = values - high.astype(jnp.float32)
    mid = rest.astype(jnp.bfloat16)
    low = (rest - mid.astype(jnp.float32)).astype(jnp.bfloat16)
    return high, mid, low


def dot(left, right, dims):
    return lax.dot_general(left, right, (dims, ((), ())), preferred_element_type=jnp.float32)


def start_kernel(
    train_ref, valid_ref, levels_ref, level_cost_ref, cost_ref, row_out, col_out, row_a, row_b, *, num_levels
):
    shards, shard_rows, width = train_ref.shape
    embed = width - LANES
    rows = shards * shard_rows
    packed = train_ref[...].reshape(rows, width)
    train = packed[:, :embed]
    wide = train.astype(jnp.float32)
    train_sq = jnp.sum(wide * wide, axis=1, keepdims=True)
    levels = levels_ref[...]
    table = jnp.zeros(levels.shape, jnp.float32)
    for level in range(num_levels):
        table = table + jnp.where(levels == level, level_cost_ref[level], 0.0)
    labels = packed[:, embed:].astype(jnp.float32)
    lane_ids = lax.broadcasted_iota(jnp.int32, labels.shape, 1).astype(jnp.float32)
    train_hot = jnp.where(labels == lane_ids, 1.0, 0.0).astype(jnp.bfloat16)
    parts = [dot(train_hot, part, ((1,), (0,))).astype(jnp.bfloat16) for part in split3(table)]
    left = jnp.concatenate([train * jnp.bfloat16(-2.0 / embed), *parts], axis=1)
    ones = jnp.ones((SUB, embed), jnp.bfloat16)
    blocks, block_rows, _ = valid_ref.shape
    points = LANES
    for pair in range(blocks // 2):
        halves = (2 * pair, 2 * pair + 1)
        block = jnp.concatenate([valid_ref[h, :points, :] for h in halves], axis=0)
        hots = []
        for h in halves:
            label_row = valid_ref[h, points:, :LANES].astype(jnp.float32)[:1, :]
            class_ids = lax.broadcasted_iota(jnp.int32, (LANES, LANES), 0).astype(jnp.float32)
            hots.append(jnp.where(class_ids == label_row, 1.0, 0.0).astype(jnp.bfloat16))
        hot = jnp.concatenate(hots, axis=1)
        block_wide = block.astype(jnp.float32)
        squares = block_wide * block_wide
        sq_high = squares.astype(jnp.bfloat16)
        sq_low = (squares - sq_high.astype(jnp.float32)).astype(jnp.bfloat16)
        block_sq = (dot(ones, sq_high, ((1,), (1,))) + dot(ones, sq_low, ((1,), (1,))))[:1, :]
        products = dot(left[:, :embed], block, ((1,), (1,)))
        label_part = dot(left[:, embed:], jnp.concatenate([hot] * 3, axis=0), ((1,), (0,)))
        cost = products + (train_sq + block_sq) * (1.0 / embed) + label_part
        cost_ref[:, pair * 2 * points : (pair + 1) * 2 * points] = cost * (1.0 / UNIT)
    col_out[...] = jnp.broadcast_to(col_partial(cost_ref, None)[None], col_out.shape)
    row_out[...] = jnp.broadcast_to(row_partial(cost_ref, None, row_a, row_b)[None], row_out.shape)


def col_kernel(cost_ref, parts_ref, pot_ref, out_ref, new_ref, spread_ref, *, offset):
    pot = 0.5 * (pot_ref[...] + (offset - lse_lead(parts_ref[...])))
    new_ref[...] = pot
    spread_rows(pot, spread_ref)
    out_ref[...] = jnp.broadcast_to(col_partial(cost_ref, spread_ref)[None], out_ref.shape)


def row_kernel(cost_ref, parts_ref, pot_ref, out_ref, new_ref, row_a, row_b, *, offset):
    pot = 0.5 * (pot_ref[...] + (offset - lse_lead(parts_ref[...])))
    new_ref[...] = pot
    out_ref[...] = jnp.broadcast_to(row_partial(cost_ref, pot, row_a, row_b)[None], out_ref.shape)


def last_kernel(parts_ref, pot_ref, out_ref, *, offset):
    pot = 0.5 * (pot_ref[...] + (offset - lse_lead(parts_ref[...])))
    out_ref[...] = jnp.broadcast_to(pot[None], out_ref.shape)


def calibrate_kernel(parts_ref, pot_ref, out_ref, *, count):
    total = jnp.sum(jnp.sum(parts_ref[...], axis=0), keepdims=True)
    out_ref[...] = (pot_ref[...] * count - total) * (UNIT / (count - 1))


def exchange(copies, axis):
    return lax.all_to_all(copies, axis, 0, 0, tiled=True)


def call(kernel, out_shape, scratch, *args, smem=(), flops=0, **static):
    body = kernel if not static else (lambda *refs: kernel(*refs, **static))
    specs = [pl.BlockSpec(memory_space=pltpu.SMEM) if i in smem else VMEM for i in range(len(args))]
    return pl.pallas_call(
        body,
        out_shape=out_shape,
        in_specs=specs,
        out_specs=jax.tree.map(lambda _: VMEM, out_shape),
        scratch_shapes=scratch,
        compiler_params=pltpu.CompilerParams(vmem_limit_bytes=48 * 2**20),
        cost_estimate=pl.CostEstimate(flops=flops, bytes_accessed=4 * 2**20, transcendentals=2**20),
    )(*args)


def shards(train_embed, valid_embed, train_labels, valid_labels, pair_level, level_cost):
    row_size, col_size = lax.axis_size("row"), lax.axis_size("col")
    embed = train_embed.shape[1]
    train_pack = jnp.concatenate(
        [
            train_embed,
            jnp.broadcast_to(train_labels.astype(jnp.bfloat16)[:, None], (train_embed.shape[0], LANES)),
        ],
        axis=1,
    )
    label_row = jnp.tile(valid_labels.astype(jnp.bfloat16), embed // LANES)[None, :]
    valid_pack = jnp.concatenate([valid_embed, jnp.broadcast_to(label_row, (16, embed))], axis=0)
    train_all = exchange(jnp.broadcast_to(train_pack[None], (col_size,) + train_pack.shape), "col")
    valid_all = exchange(jnp.broadcast_to(valid_pack[None], (row_size,) + valid_pack.shape), "row")
    rows = train_embed.shape[0] * col_size
    cols = valid_embed.shape[0] * row_size
    row_chunks, col_chunks = rows // LANES, cols // LANES
    classes = pair_level.shape[0]
    levels = jnp.pad(pair_level, ((0, LANES - classes), (0, LANES - classes)), constant_values=-1)
    f32 = jnp.float32
    row_copies = jax.ShapeDtypeStruct((col_size, row_chunks, LANES), f32)
    col_copies = jax.ShapeDtypeStruct((row_size, col_chunks, LANES), f32)
    row_shape = jax.ShapeDtypeStruct((row_chunks, LANES), f32)
    col_shape = jax.ShapeDtypeStruct((col_chunks, LANES), f32)
    tall = pltpu.VMEM((rows, LANES), f32)
    cost, row_part, col_part = call(
        start_kernel,
        (jax.ShapeDtypeStruct((rows, cols), f32), row_copies, col_copies),
        [tall, tall],
        train_all,
        valid_all,
        levels,
        level_cost,
        smem=(3,),
        num_levels=level_cost.shape[0],
    )
    full_rows = rows * row_size
    full_cols = cols * col_size
    row_offset, col_offset = math.log2(full_cols), math.log2(full_rows)
    row_pot = jnp.zeros(row_shape.shape, f32)
    col_pot = jnp.zeros(col_shape.shape, f32)
    for iteration in range(ITERS - 1):
        row_got = exchange(row_part, "col")
        col_got = exchange(col_part, "row")
        row_before, col_before = row_pot, col_pot
        if iteration < ITERS - 2:
            col_part, row_pot = call(
                col_kernel, (col_copies, row_shape), [tall], cost, row_got, row_before, offset=row_offset
            )
        row_part, col_pot = call(
            row_kernel, (row_copies, col_shape), [tall, tall], cost, col_got, col_before, offset=col_offset
        )
        if iteration == ITERS - 2:
            row_pot = call(
                last_kernel, jax.ShapeDtypeStruct((1,) + row_shape.shape, f32), [], row_got, row_before, offset=row_offset
            )[0]
    row_got = exchange(row_part, "col")
    final = call(
        last_kernel,
        jax.ShapeDtypeStruct((row_size,) + row_shape.shape, f32),
        [],
        row_got,
        row_pot,
        offset=row_offset,
    )
    finals = exchange(final, "row")
    out = call(calibrate_kernel, row_shape, [], finals, final[0], count=full_rows)
    return out.reshape(rows)


def solution(mesh):
    placed = (
        P(("row", "col"), None),
        P(("row", "col"), None),
        P(("row", "col")),
        P(("row", "col")),
        P(),
        P(),
    )
    return jax.shard_map(shards, mesh=mesh, in_specs=placed, out_specs=P("row"), check_vma=False)
```

```python
import math

import jax
import jax.numpy as jnp
from jax import lax
from jax.experimental import pallas as pl
from jax.experimental.pallas import tpu as pltpu
from jax.sharding import PartitionSpec as P

ITERS = 4
LANES = 128
SUB = 8

entropy_scale = 0.05
UNIT = entropy_scale * math.log(2.0)

ROW = ("zh", "zl", "core")

VMEM = pl.BlockSpec(memory_space=pltpu.VMEM)


def lse_lead(parts):
    high = jnp.max(parts, axis=0)
    return high + jnp.log2(jnp.sum(jnp.exp2(parts - high[None]), axis=0))


def spread_rows(values, out_ref):
    for a in range(values.shape[0]):
        block = jnp.broadcast_to(values[a : a + 1, :], (LANES, LANES))
        out_ref[a * LANES : (a + 1) * LANES, :] = block.T


def lanes_of(ref, combine):
    rows = []
    for a in range(ref.shape[0] // LANES):
        block = ref[a * LANES : (a + 1) * LANES, :].T
        rows.append(combine(block, axis=0, keepdims=True))
    return jnp.concatenate(rows, axis=0)


def col_partial(cost_ref, row_ref):
    rows, cols = cost_ref.shape
    chunks = cols // LANES

    def tile(g, k, base):
        cell = cost_ref[pl.ds(g * SUB, SUB), k * LANES : (k + 1) * LANES]
        return -cell if base is None else base - cell

    def base_of(g):
        return None if row_ref is None else row_ref[pl.ds(pl.multiple_of(g * SUB, SUB), SUB), :]

    def peaks(g, high):
        g = pl.multiple_of(g, 1)
        base = base_of(g)
        return tuple(jnp.maximum(high[k], tile(g, k, base)) for k in range(chunks))

    start = tuple(jnp.full((SUB, LANES), -jnp.inf, jnp.float32) for _ in range(chunks))
    high = lax.fori_loop(0, rows // SUB, peaks, start, unroll=4)
    high = tuple(jnp.max(h, axis=0, keepdims=True) for h in high)

    def totals(g, total):
        base = base_of(g)
        return tuple(total[k] + jnp.exp2(tile(g, k, base) - high[k]) for k in range(chunks))

    zero = tuple(jnp.zeros((SUB, LANES), jnp.float32) for _ in range(chunks))
    total = lax.fori_loop(0, rows // SUB, totals, zero, unroll=4)
    return jnp.concatenate(
        [high[k] + jnp.log2(jnp.sum(total[k], axis=0, keepdims=True)) for k in range(chunks)], axis=0
    )


def row_partial(cost_ref, col, high_ref, total_ref):
    rows, cols = cost_ref.shape
    chunks = cols // LANES

    def tile(g, k):
        cell = cost_ref[pl.ds(g * SUB, SUB), k * LANES : (k + 1) * LANES]
        return -cell if col is None else col[k : k + 1, :] - cell

    def peaks(g, carry):
        high = tile(g, 0)
        for k in range(1, chunks):
            high = jnp.maximum(high, tile(g, k))
        high_ref[pl.ds(pl.multiple_of(g * SUB, SUB), SUB), :] = jnp.broadcast_to(
            jnp.max(high, axis=1, keepdims=True), (SUB, LANES)
        )
        return carry

    lax.fori_loop(0, rows // SUB, peaks, 0, unroll=4)

    def totals(g, carry):
        here = pl.ds(pl.multiple_of(g * SUB, SUB), SUB)
        high = high_ref[here, :]
        total = jnp.exp2(tile(g, 0) - high)
        for k in range(1, chunks):
            total = total + jnp.exp2(tile(g, k) - high)
        total_ref[here, :] = total
        return carry

    lax.fori_loop(0, rows // SUB, totals, 0, unroll=4)
    return lanes_of(high_ref, jnp.max) + jnp.log2(lanes_of(total_ref, jnp.sum))


def split3(values):
    high = values.astype(jnp.bfloat16)
    rest = values - high.astype(jnp.float32)
    mid = rest.astype(jnp.bfloat16)
    low = (rest - mid.astype(jnp.float32)).astype(jnp.bfloat16)
    return high, mid, low


def dot(left, right, dims):
    return lax.dot_general(left, right, (dims, ((), ())), preferred_element_type=jnp.float32)


def start_kernel(
    train_ref, valid_ref, levels_ref, level_cost_ref, cost_ref, col_out, *, num_levels
):
    shards, shard_rows, width = train_ref.shape
    embed = width - LANES
    rows = shards * shard_rows
    packed = train_ref[...].reshape(rows, width)
    train = packed[:, :embed]
    wide = train.astype(jnp.float32)
    train_sq = jnp.sum(wide * wide, axis=1, keepdims=True)
    levels = levels_ref[...]
    table = jnp.zeros(levels.shape, jnp.float32)
    for level in range(num_levels):
        table = table + jnp.where(levels == level, level_cost_ref[level], 0.0)
    labels = packed[:, embed:].astype(jnp.float32)
    lane_ids = lax.broadcasted_iota(jnp.int32, labels.shape, 1).astype(jnp.float32)
    train_hot = jnp.where(labels == lane_ids, 1.0, 0.0).astype(jnp.bfloat16)
    parts = [dot(train_hot, part, ((1,), (0,))).astype(jnp.bfloat16) for part in split3(table)]
    left = jnp.concatenate([train * jnp.bfloat16(-2.0 / embed), *parts], axis=1)
    ones = jnp.ones((SUB, embed), jnp.bfloat16)
    blocks, block_rows, _ = valid_ref.shape
    points = LANES
    for pair in range(blocks // 2):
        halves = (2 * pair, 2 * pair + 1)
        block = jnp.concatenate([valid_ref[h, :points, :] for h in halves], axis=0)
        hots = []
        for h in halves:
            label_row = valid_ref[h, points:, :LANES].astype(jnp.float32)[:1, :]
            class_ids = lax.broadcasted_iota(jnp.int32, (LANES, LANES), 0).astype(jnp.float32)
            hots.append(jnp.where(class_ids == label_row, 1.0, 0.0).astype(jnp.bfloat16))
        hot = jnp.concatenate(hots, axis=1)
        block_wide = block.astype(jnp.float32)
        squares = block_wide * block_wide
        sq_high = squares.astype(jnp.bfloat16)
        sq_low = (squares - sq_high.astype(jnp.float32)).astype(jnp.bfloat16)
        block_sq = (dot(ones, sq_high, ((1,), (1,))) + dot(ones, sq_low, ((1,), (1,))))[:1, :]
        products = dot(left[:, :embed], block, ((1,), (1,)))
        label_part = dot(left[:, embed:], jnp.concatenate([hot] * 3, axis=0), ((1,), (0,)))
        cost = products + (train_sq + block_sq) * (1.0 / embed) + label_part
        cost_ref[:, pair * 2 * points : (pair + 1) * 2 * points] = cost * (1.0 / UNIT)
    col_out[...] = jnp.broadcast_to(col_partial(cost_ref, None)[None], col_out.shape)


def first_row_kernel(cost_ref, out_ref, row_a, row_b):
    out_ref[...] = jnp.broadcast_to(row_partial(cost_ref, None, row_a, row_b)[None], out_ref.shape)


def col_kernel(cost_ref, parts_ref, pot_ref, out_ref, new_ref, spread_ref, *, offset):
    pot = 0.5 * (pot_ref[...] + (offset - lse_lead(parts_ref[...])))
    new_ref[...] = pot
    spread_rows(pot, spread_ref)
    out_ref[...] = jnp.broadcast_to(col_partial(cost_ref, spread_ref)[None], out_ref.shape)


def row_kernel(cost_ref, parts_ref, pot_ref, out_ref, new_ref, row_a, row_b, *, offset):
    pot = 0.5 * (pot_ref[...] + (offset - lse_lead(parts_ref[...])))
    new_ref[...] = pot
    out_ref[...] = jnp.broadcast_to(row_partial(cost_ref, pot, row_a, row_b)[None], out_ref.shape)


def last_kernel(parts_ref, pot_ref, out_ref, *, offset):
    pot = 0.5 * (pot_ref[...] + (offset - lse_lead(parts_ref[...])))
    out_ref[...] = jnp.broadcast_to(pot[None], out_ref.shape)


def calibrate_kernel(parts_ref, pot_ref, out_ref, *, count):
    total = jnp.sum(jnp.sum(parts_ref[...], axis=0), keepdims=True)
    out_ref[...] = (pot_ref[...] * count - total) * (UNIT / (count - 1))


def exchange(copies, axis):
    return lax.all_to_all(copies, axis, 0, 0, tiled=True)


def call(kernel, out_shape, scratch, *args, smem=(), limit=8, **static):
    body = kernel if not static else (lambda *refs: kernel(*refs, **static))
    specs = [pl.BlockSpec(memory_space=pltpu.SMEM) if i in smem else VMEM for i in range(len(args))]
    return pl.pallas_call(
        body,
        out_shape=out_shape,
        in_specs=specs,
        out_specs=jax.tree.map(lambda _: VMEM, out_shape),
        scratch_shapes=scratch,
        compiler_params=pltpu.CompilerParams(vmem_limit_bytes=limit * 2**20),
        cost_estimate=pl.CostEstimate(flops=2**24, bytes_accessed=4 * 2**20, transcendentals=2**20),
    )(*args)


def shards(train_embed, valid_embed, train_labels, valid_labels, pair_level, level_cost):
    row_size, col_size = lax.axis_size(ROW), lax.axis_size("col")
    embed = train_embed.shape[1]
    train_pack = jnp.concatenate(
        [
            train_embed,
            jnp.broadcast_to(train_labels.astype(jnp.bfloat16)[:, None], (train_embed.shape[0], LANES)),
        ],
        axis=1,
    )
    label_row = jnp.tile(valid_labels.astype(jnp.bfloat16), embed // LANES)[None, :]
    valid_pack = jnp.concatenate([valid_embed, jnp.broadcast_to(label_row, (16, embed))], axis=0)
    train_all = exchange(jnp.broadcast_to(train_pack[None], (col_size,) + train_pack.shape), "col")
    valid_all = lax.all_gather(valid_pack[None], "zl", axis=0, tiled=True)
    for axis in ("zh", "core"):
        copies = jnp.broadcast_to(valid_all[None], (lax.axis_size(axis),) + valid_all.shape)
        valid_all = exchange(copies, axis).reshape((-1,) + valid_pack.shape)
    rows = train_embed.shape[0] * col_size
    cols = valid_embed.shape[0] * row_size
    row_chunks, col_chunks = rows // LANES, cols // LANES
    classes = pair_level.shape[0]
    levels = jnp.pad(pair_level, ((0, LANES - classes), (0, LANES - classes)), constant_values=-1)
    f32 = jnp.float32
    row_copies = jax.ShapeDtypeStruct((col_size, row_chunks, LANES), f32)
    col_copies = jax.ShapeDtypeStruct((row_size, col_chunks, LANES), f32)
    row_shape = jax.ShapeDtypeStruct((row_chunks, LANES), f32)
    col_shape = jax.ShapeDtypeStruct((col_chunks, LANES), f32)
    tall = pltpu.VMEM((rows, LANES), f32)
    cost, col_part = call(
        start_kernel,
        (jax.ShapeDtypeStruct((rows, cols), f32), col_copies),
        [],
        train_all,
        valid_all,
        levels,
        level_cost,
        smem=(3,),
        num_levels=level_cost.shape[0],
        limit=24,
    )
    row_part = call(first_row_kernel, row_copies, [tall, tall], cost)
    full_rows = rows * row_size
    full_cols = cols * col_size
    row_offset, col_offset = math.log2(full_cols), math.log2(full_rows)
    row_pot = jnp.zeros(row_shape.shape, f32)
    col_pot = jnp.zeros(col_shape.shape, f32)
    for iteration in range(ITERS - 1):
        row_got = exchange(row_part, "col")
        col_got = exchange(col_part, ROW)
        row_before, col_before = row_pot, col_pot
        if iteration < ITERS - 2:
            col_part, row_pot = call(
                col_kernel, (col_copies, row_shape), [tall], cost, row_got, row_before, offset=row_offset
            )
        row_part, col_pot = call(
            row_kernel, (row_copies, col_shape), [tall, tall], cost, col_got, col_before, offset=col_offset
        )
        if iteration == ITERS - 2:
            row_pot = call(
                last_kernel, jax.ShapeDtypeStruct((1,) + row_shape.shape, f32), [], row_got, row_before, offset=row_offset
            )[0]
    row_got = exchange(row_part, "col")
    final = call(
        last_kernel,
        jax.ShapeDtypeStruct((row_size,) + row_shape.shape, f32),
        [],
        row_got,
        row_pot,
        offset=row_offset,
    )
    finals = exchange(final, ROW)
    out = call(calibrate_kernel, row_shape, [], finals, final[0], count=full_rows)
    return out.reshape(rows)


def solution(mesh):
    row_size, col_size = mesh.shape["row"], mesh.shape["col"]
    finer = jax.sharding.Mesh(mesh.devices.reshape(row_size // 4, 2, 2, col_size), ROW + ("col",))
    both = ROW + ("col",)
    placed = (P(both, None), P(both, None), P(both), P(both), P(), P())
    return jax.shard_map(shards, mesh=finer, in_specs=placed, out_specs=P(ROW), check_vma=False)
```

```python
import math

import jax
import jax.numpy as jnp
from jax import lax
from jax.experimental import pallas as pl
from jax.experimental.pallas import tpu as pltpu
from jax.sharding import PartitionSpec as P

ITERS = 4
LANES = 128
SUB = 8
CHUNKS = 4

entropy_scale = 0.05
UNIT = entropy_scale * math.log(2.0)

ORDER = ("zh", "zl", "core", "yh", "yl", "x")
NEAR = ("zl", "core", "yl")
FAR = ("zh", "yh", "x")

VMEM = pl.BlockSpec(memory_space=pltpu.VMEM)


def lse_lead(parts):
    high = jnp.max(parts, axis=0)
    return high + jnp.log2(jnp.sum(jnp.exp2(parts - high[None]), axis=0))


def spread_rows(values, out_ref):
    for a in range(values.shape[0]):
        block = jnp.broadcast_to(values[a : a + 1, :], (LANES, LANES))
        out_ref[a * LANES : (a + 1) * LANES, :] = block.T


def lanes_of(ref, combine):
    rows = []
    for a in range(ref.shape[0] // LANES):
        block = ref[a * LANES : (a + 1) * LANES, :].T
        rows.append(combine(block, axis=0, keepdims=True))
    return jnp.concatenate(rows, axis=0)


def bring(cost_hbm, cost_ref, sems):
    rows = cost_ref.shape[0] // CHUNKS
    copies = [
        pltpu.make_async_copy(
            cost_hbm.at[q * rows : (q + 1) * rows, :], cost_ref.at[q * rows : (q + 1) * rows, :], sems.at[q]
        )
        for q in range(CHUNKS)
    ]
    for copy in copies:
        copy.start()
    return lambda q: copies[q].wait()


def no_wait(q):
    return None


def group_loops(rows, wait, step, carry):
    groups = rows // SUB // CHUNKS
    for q in range(CHUNKS):
        wait(q)
        carry = lax.fori_loop(q * groups, (q + 1) * groups, step, carry, unroll=4)
    return carry


def group(g):
    return pl.ds(pl.multiple_of(g * SUB, SUB), SUB)


def col_partial(cost_ref, row_ref, wait):
    rows, cols = cost_ref.shape
    chunks = range(cols // LANES)

    def tiles(g):
        cells = [cost_ref[group(g), k * LANES : (k + 1) * LANES] for k in chunks]
        if row_ref is None:
            return [-cell for cell in cells]
        base = row_ref[group(g), :]
        return [base - cell for cell in cells]

    def peaks(g, high):
        return tuple(jnp.maximum(h, t) for h, t in zip(high, tiles(g)))

    start = tuple(jnp.full((SUB, LANES), -jnp.inf, jnp.float32) for _ in chunks)
    high = group_loops(rows, wait, peaks, start)
    high = tuple(jnp.max(h, axis=0, keepdims=True) for h in high)

    def totals(g, total):
        return tuple(s + jnp.exp2(t - h) for s, t, h in zip(total, tiles(g), high))

    zero = tuple(jnp.zeros((SUB, LANES), jnp.float32) for _ in chunks)
    total = group_loops(rows, no_wait, totals, zero)
    return jnp.concatenate(
        [h + jnp.log2(jnp.sum(s, axis=0, keepdims=True)) for h, s in zip(high, total)], axis=0
    )


def row_partial(cost_ref, col, high_ref, total_ref, wait):
    rows, cols = cost_ref.shape
    chunks = range(cols // LANES)

    def tile(g, k):
        cell = cost_ref[group(g), k * LANES : (k + 1) * LANES]
        return -cell if col is None else col[k : k + 1, :] - cell

    def peaks(g, carry):
        high = tile(g, 0)
        for k in chunks[1:]:
            high = jnp.maximum(high, tile(g, k))
        high_ref[group(g), :] = jnp.broadcast_to(jnp.max(high, axis=1, keepdims=True), (SUB, LANES))
        return carry

    group_loops(rows, wait, peaks, 0)

    def totals(g, carry):
        high = high_ref[group(g), :]
        total = jnp.exp2(tile(g, 0) - high)
        for k in chunks[1:]:
            total = total + jnp.exp2(tile(g, k) - high)
        total_ref[group(g), :] = total
        return carry

    group_loops(rows, no_wait, totals, 0)
    return lanes_of(high_ref, jnp.max) + jnp.log2(lanes_of(total_ref, jnp.sum))


def split3(values):
    high = values.astype(jnp.bfloat16)
    rest = values - high.astype(jnp.float32)
    mid = rest.astype(jnp.bfloat16)
    low = (rest - mid.astype(jnp.float32)).astype(jnp.bfloat16)
    return high, mid, low


def dot(left, right, dims):
    return lax.dot_general(left, right, (dims, ((), ())), preferred_element_type=jnp.float32)


def start_kernel(
    train_ref, valid_ref, levels_ref, level_cost_ref, cost_hbm, row_out, cost_ref, row_a, row_b, sems, *, num_levels
):
    shards, shard_rows, width = train_ref.shape
    embed = width - LANES
    rows = shards * shard_rows
    packed = train_ref[...].reshape(rows, width)
    train = packed[:, :embed]
    wide = train.astype(jnp.float32)
    train_sq = jnp.sum(wide * wide, axis=1, keepdims=True)
    levels = levels_ref[...]
    table = jnp.zeros(levels.shape, jnp.float32)
    for level in range(num_levels):
        table = table + jnp.where(levels == level, level_cost_ref[level], 0.0)
    labels = packed[:, embed:].astype(jnp.float32)
    lane_ids = lax.broadcasted_iota(jnp.int32, labels.shape, 1).astype(jnp.float32)
    train_hot = jnp.where(labels == lane_ids, 1.0, 0.0).astype(jnp.bfloat16)
    parts = [dot(train_hot, part, ((1,), (0,))).astype(jnp.bfloat16) for part in split3(table)]
    left = jnp.concatenate([train * jnp.bfloat16(-2.0 / embed), *parts], axis=1)
    ones = jnp.ones((SUB, embed), jnp.bfloat16)
    blocks, block_rows, _ = valid_ref.shape
    points = LANES
    copies = []
    for pair in range(blocks // 2):
        halves = (2 * pair, 2 * pair + 1)
        block = jnp.concatenate([valid_ref[h, :points, :] for h in halves], axis=0)
        hots = []
        for h in halves:
            label_row = valid_ref[h, points:, :LANES].astype(jnp.float32)[:1, :]
            class_ids = lax.broadcasted_iota(jnp.int32, (LANES, LANES), 0).astype(jnp.float32)
            hots.append(jnp.where(class_ids == label_row, 1.0, 0.0).astype(jnp.bfloat16))
        hot = jnp.concatenate(hots, axis=1)
        block_wide = block.astype(jnp.float32)
        squares = block_wide * block_wide
        sq_high = squares.astype(jnp.bfloat16)
        sq_low = (squares - sq_high.astype(jnp.float32)).astype(jnp.bfloat16)
        block_sq = (dot(ones, sq_high, ((1,), (1,))) + dot(ones, sq_low, ((1,), (1,))))[:1, :]
        products = dot(left[:, :embed], block, ((1,), (1,)))
        label_part = dot(left[:, embed:], jnp.concatenate([hot] * 3, axis=0), ((1,), (0,)))
        cost = products + (train_sq + block_sq) * (1.0 / embed) + label_part
        here = slice(pair * 2 * points, (pair + 1) * 2 * points)
        cost_ref[:, here] = cost * (1.0 / UNIT)
        copies.append(pltpu.make_async_copy(cost_ref.at[:, here], cost_hbm.at[:, here], sems.at[pair]))
        copies[-1].start()
    row_out[...] = jnp.broadcast_to(row_partial(cost_ref, None, row_a, row_b, no_wait)[None], row_out.shape)
    for copy in copies:
        copy.wait()


def first_col_kernel(cost_hbm, out_ref, cost_ref, sems):
    wait = bring(cost_hbm, cost_ref, sems)
    out_ref[...] = col_partial(cost_ref, None, wait)


def col_kernel(cost_hbm, parts_ref, pot_ref, out_ref, new_ref, cost_ref, sems, spread_ref, *, offset):
    wait = bring(cost_hbm, cost_ref, sems)
    pot = 0.5 * (pot_ref[...] + (offset - lse_lead(parts_ref[...])))
    new_ref[...] = pot
    spread_rows(pot, spread_ref)
    out_ref[...] = col_partial(cost_ref, spread_ref, wait)


def row_kernel(cost_hbm, parts_ref, pot_ref, out_ref, new_ref, cost_ref, sems, row_a, row_b, *, offset):
    wait = bring(cost_hbm, cost_ref, sems)
    pot = 0.5 * (pot_ref[...] + (offset - lse_lead(parts_ref[...])))
    new_ref[...] = pot
    out_ref[...] = jnp.broadcast_to(row_partial(cost_ref, pot, row_a, row_b, wait)[None], out_ref.shape)


def last_kernel(parts_ref, pot_ref, out_ref, *, offset):
    pot = 0.5 * (pot_ref[...] + (offset - lse_lead(parts_ref[...])))
    out_ref[...] = jnp.broadcast_to(pot[None], out_ref.shape)


def calibrate_kernel(where_ref, parts_ref, out_ref, *, count):
    total = jnp.sum(jnp.sum(parts_ref[...], axis=0), keepdims=True)
    blocks = [parts_ref[where_ref[0] * 2 + side] for side in range(2)]
    row_ids = lax.broadcasted_iota(jnp.int32, blocks[0].shape, 0)
    low_half = lax.broadcasted_iota(jnp.int32, (1, LANES), 1) < LANES // 2
    rows = []
    for q in range(out_ref.shape[0] // 2):
        mine = row_ids == where_ref[1] * (out_ref.shape[0] // 2) + q
        first, second = [jnp.sum(jnp.where(mine, block, 0.0), axis=0, keepdims=True) for block in blocks]
        rows.append(jnp.where(low_half, first, pltpu.roll(second, LANES // 2, 1)))
        rows.append(jnp.where(low_half, pltpu.roll(first, LANES // 2, 1), second))
    picked = jnp.concatenate(rows, axis=0)
    out_ref[...] = (picked * count - total) * (UNIT / (count - 1))


def exchange(copies, axis):
    return lax.all_to_all(copies, axis, 0, 0, tiled=True)


def near_gather(block):
    return lax.all_gather(lax.all_gather(block[None], NEAR[:2], axis=0, tiled=True), NEAR[2], axis=0, tiled=True)


def call(kernel, out_shape, scratch, *args, smem=(), hbm=(), limit=16, **static):
    body = kernel if not static else (lambda *refs: kernel(*refs, **static))
    smem_spec, hbm_spec = pl.BlockSpec(memory_space=pltpu.SMEM), pl.BlockSpec(memory_space=pltpu.HBM)
    specs = [smem_spec if i in smem else hbm_spec if i in hbm else VMEM for i in range(len(args))]
    out_specs = [hbm_spec if len(o.shape) == 2 and o.shape[0] > 4 * LANES else VMEM for o in out_shape]
    return pl.pallas_call(
        body,
        out_shape=out_shape,
        in_specs=specs,
        out_specs=out_specs,
        scratch_shapes=scratch,
        compiler_params=pltpu.CompilerParams(vmem_limit_bytes=limit * 2**20),
        cost_estimate=pl.CostEstimate(flops=2**24, bytes_accessed=4 * 2**20, transcendentals=2**20),
    )(*args)


def shards(train_embed, valid_embed, train_labels, valid_labels, pair_level, level_cost):
    row_size, col_size = lax.axis_size(NEAR), lax.axis_size(FAR)
    embed = train_embed.shape[1]
    f32 = jnp.float32
    train_pack = jnp.concatenate(
        [
            train_embed,
            jnp.broadcast_to(train_labels.astype(jnp.bfloat16)[:, None], (train_embed.shape[0], LANES)),
        ],
        axis=1,
    )
    label_row = jnp.tile(valid_labels.astype(jnp.bfloat16), embed // LANES)[None, :]
    valid_pack = jnp.concatenate([valid_embed, jnp.broadcast_to(label_row, (16, embed))], axis=0)
    train_all = exchange(jnp.broadcast_to(train_pack[None], (col_size,) + train_pack.shape), FAR)
    valid_all = near_gather(valid_pack)
    rows = train_embed.shape[0] * col_size
    cols = valid_embed.shape[0] * row_size
    row_chunks, col_chunks = rows // LANES, cols // LANES
    classes = pair_level.shape[0]
    levels = jnp.pad(pair_level, ((0, LANES - classes), (0, LANES - classes)), constant_values=-1)
    tile = jax.ShapeDtypeStruct((rows, cols), f32)
    row_copies = jax.ShapeDtypeStruct((col_size, row_chunks, LANES), f32)
    row_shape = jax.ShapeDtypeStruct((row_chunks, LANES), f32)
    col_shape = jax.ShapeDtypeStruct((col_chunks, LANES), f32)
    tall = pltpu.VMEM((rows, LANES), f32)
    held = [pltpu.VMEM((rows, cols), f32), pltpu.SemaphoreType.DMA((CHUNKS,))]
    cost, row_part = call(
        start_kernel,
        (tile, row_copies),
        [held[0], tall, tall, pltpu.SemaphoreType.DMA((row_size // 2,))],
        train_all,
        valid_all,
        levels,
        level_cost,
        smem=(3,),
        num_levels=level_cost.shape[0],
        limit=40,
    )
    full_rows, full_cols = rows * row_size, cols * col_size
    row_offset, col_offset = math.log2(full_cols), math.log2(full_rows)
    row_pot = jnp.zeros(row_shape.shape, f32)
    col_pot = jnp.zeros(col_shape.shape, f32)
    row_got = None
    for iteration in range(ITERS - 1):
        sent = exchange(row_part, FAR)
        if iteration == 0:
            (col_part,) = call(first_col_kernel, (col_shape,), held, cost, hbm=(0,))
        else:
            col_part, row_pot = call(
                col_kernel, (col_shape, row_shape), held + [tall], cost, row_got, row_pot, hbm=(0,), offset=row_offset
            )
        row_part, col_pot = call(
            row_kernel,
            (row_copies, col_shape),
            held + [tall, tall],
            cost,
            near_gather(col_part),
            col_pot,
            hbm=(0,),
            offset=col_offset,
        )
        row_got = sent
    (row_pot,) = call(
        last_kernel, (jax.ShapeDtypeStruct((1,) + row_shape.shape, f32),), [], row_got, row_pot, offset=row_offset
    )
    row_got = exchange(row_part, FAR)
    (final,) = call(
        last_kernel,
        (jax.ShapeDtypeStruct((row_size,) + row_shape.shape, f32),),
        [],
        row_got,
        row_pot[0],
        offset=row_offset,
    )
    finals = exchange(final, NEAR)
    where = jnp.stack([lax.axis_index(NEAR[:2]), lax.axis_index("zh")]).astype(jnp.int32)
    out_rows = full_rows // lax.axis_size(("zh",) + NEAR[:2]) // LANES
    (out,) = call(
        calibrate_kernel, (jax.ShapeDtypeStruct((out_rows, LANES), f32),), [], where, finals, smem=(0,), count=full_rows
    )
    return out.reshape(out_rows * LANES)


def solution(mesh):
    row_size, col_size = mesh.shape["row"], mesh.shape["col"]
    sizes = (row_size // 4, 2, 2, 4, 2, col_size // 8)
    finer = jax.sharding.Mesh(mesh.devices.reshape(sizes), ORDER)
    placed = (P(ORDER, None), P(ORDER, None), P(ORDER), P(ORDER), P(), P())
    return jax.shard_map(shards, mesh=finer, in_specs=placed, out_specs=P(ORDER[:3]), check_vma=False)
```

```python
import math

import jax
import jax.numpy as jnp
from jax import lax
from jax.experimental import pallas as pl
from jax.experimental.pallas import tpu as pltpu
from jax.sharding import PartitionSpec as P

ITERS = 4
LANES = 128
SUB = 8

entropy_scale = 0.05
UNIT = entropy_scale * math.log(2.0)

VMEM = pl.BlockSpec(memory_space=pltpu.VMEM)


def lse_lead(parts):
    high = jnp.max(parts, axis=0)
    return high + jnp.log2(jnp.sum(jnp.exp2(parts - high[None]), axis=0))


def merge(high, total):
    top = jnp.max(high, axis=0, keepdims=True)
    return top + jnp.log2(jnp.sum(total * jnp.exp2(high - top), axis=0, keepdims=True))


def spread_rows(values, out_ref):
    for a in range(values.shape[0]):
        block = jnp.broadcast_to(values[a : a + 1, :], (LANES, LANES))
        out_ref[a * LANES : (a + 1) * LANES, :] = block.T


def peak_and_sum(tiles):
    high = tiles[0]
    for tile in tiles[1:]:
        high = jnp.maximum(high, tile)
    total = jnp.exp2(tiles[0] - high)
    for tile in tiles[1:]:
        total = total + jnp.exp2(tile - high)
    return high, total


def col_partial(cost_ref, row_ref, high_ref, total_ref):
    rows, cols = cost_ref.shape
    blocks, chunks = rows // LANES, cols // LANES
    groups = LANES // SUB

    def block_step(q, carry):
        start = pl.multiple_of(q * LANES, LANES)
        bases = None if row_ref is None else [row_ref[pl.ds(start + g * SUB, SUB), :] for g in range(groups)]
        for k in range(chunks):
            cells = [cost_ref[pl.ds(start + g * SUB, SUB), k * LANES : (k + 1) * LANES] for g in range(groups)]
            tiles = [-cell for cell in cells] if bases is None else [base - cell for base, cell in zip(bases, cells)]
            high, total = peak_and_sum(tiles)
            here = (pl.ds(pl.multiple_of(q * SUB, SUB), SUB), slice(k * LANES, (k + 1) * LANES))
            high_ref[here] = high
            total_ref[here] = total
        return carry

    lax.fori_loop(0, blocks, block_step, 0)
    out = [merge(high_ref[:, k * LANES : (k + 1) * LANES], total_ref[:, k * LANES : (k + 1) * LANES]) for k in range(chunks)]
    return jnp.concatenate(out, axis=0)


def row_partial(cost_ref, col, high_ref, total_ref):
    rows, cols = cost_ref.shape
    chunks = cols // LANES
    bases = None if col is None else [jnp.broadcast_to(col[k : k + 1, :], (SUB, LANES)) for k in range(chunks)]

    def group_step(g, carry):
        here = pl.ds(pl.multiple_of(g * SUB, SUB), SUB)
        cells = [cost_ref[here, k * LANES : (k + 1) * LANES] for k in range(chunks)]
        tiles = [-cell for cell in cells] if bases is None else [base - cell for base, cell in zip(bases, cells)]
        high_ref[here, :], total_ref[here, :] = peak_and_sum(tiles)
        return carry

    lax.fori_loop(0, rows // SUB, group_step, 0, unroll=4)
    out = []
    for a in range(rows // LANES):
        block = slice(a * LANES, (a + 1) * LANES)
        out.append(merge(high_ref[block, :].T, total_ref[block, :].T))
    return jnp.concatenate(out, axis=0)


def split3(values):
    high = values.astype(jnp.bfloat16)
    rest = values - high.astype(jnp.float32)
    mid = rest.astype(jnp.bfloat16)
    low = (rest - mid.astype(jnp.float32)).astype(jnp.bfloat16)
    return high, mid, low


def dot(left, right, dims):
    return lax.dot_general(left, right, (dims, ((), ())), preferred_element_type=jnp.float32)


def prepare_kernel(train_ref, label_ref, levels_ref, level_cost_ref, left_ref, sq_ref, hot_ref, *, num_levels):
    shards, shard_rows, width = train_ref.shape
    embed = width - LANES
    packed = train_ref[...].reshape(shards * shard_rows, width)
    train = packed[:, :embed]
    wide = train.astype(jnp.float32)
    train_sq = jnp.sum(wide * wide, axis=1, keepdims=True) * (1.0 / embed)
    sq_ref[...] = jnp.broadcast_to(train_sq, sq_ref.shape)
    left_ref[:, :embed] = train * jnp.bfloat16(-2.0 / embed)
    levels = levels_ref[...]
    table = jnp.zeros(levels.shape, jnp.float32)
    for level in range(num_levels):
        table = table + jnp.where(levels == level, level_cost_ref[level], 0.0)
    labels = packed[:, embed:].astype(jnp.float32)
    lane_ids = lax.broadcasted_iota(jnp.int32, labels.shape, 1).astype(jnp.float32)
    train_hot = jnp.where(labels == lane_ids, 1.0, 0.0).astype(jnp.bfloat16)
    parts = [dot(train_hot, part, ((1,), (0,))).astype(jnp.bfloat16) for part in split3(table)]
    left_ref[:, embed:] = jnp.concatenate(parts, axis=1)
    class_ids = lax.broadcasted_iota(jnp.int32, (LANES, LANES), 0).astype(jnp.float32)
    for k in range(label_ref.shape[0]):
        hot_ref[:, k * LANES : (k + 1) * LANES] = jnp.where(class_ids == label_ref[k], 1.0, 0.0).astype(jnp.bfloat16)


def start_kernel(left_ref, sq_ref, hot_ref, valid_ref, cost_ref, row_out, col_out, row_a, row_b, col_a, col_b):
    embed = valid_ref.shape[1]
    table_parts = (left_ref.shape[1] - embed) // LANES
    train_sq = jnp.concatenate([sq_ref[...]] * 2, axis=1)
    ones = jnp.ones((SUB, embed), jnp.bfloat16)
    step = 2 * LANES
    for pair in range(valid_ref.shape[0] // step):
        here = slice(pair * step, (pair + 1) * step)
        block = valid_ref[here, :]
        wide = block.astype(jnp.float32)
        squares = wide * wide
        sq_high = squares.astype(jnp.bfloat16)
        sq_low = (squares - sq_high.astype(jnp.float32)).astype(jnp.bfloat16)
        block_sq = (dot(ones, sq_high, ((1,), (1,))) + dot(ones, sq_low, ((1,), (1,))))[:1, :]
        cost = dot(left_ref[:, :embed], block, ((1,), (1,)))
        cost = cost + dot(left_ref[:, embed:], jnp.concatenate([hot_ref[:, here]] * table_parts, axis=0), ((1,), (0,)))
        cost_ref[:, here] = (cost + (train_sq + block_sq * (1.0 / embed))) * (1.0 / UNIT)
    row_out[...] = jnp.broadcast_to(row_partial(cost_ref, None, row_a, row_b)[None], row_out.shape)
    col_out[...] = jnp.broadcast_to(col_partial(cost_ref, None, col_a, col_b)[None], col_out.shape)


def updated(pot_ref, parts_ref, offset):
    return 0.5 * (pot_ref[...] + (offset - lse_lead(parts_ref[...])))


def both_kernel(
    cost_ref, row_parts, col_parts, row_pot, col_pot, row_out, col_out, row_new, col_new, row_a, row_b, col_a, col_b,
    spread_ref, *, row_offset, col_offset
):
    row, col = updated(row_pot, row_parts, row_offset), updated(col_pot, col_parts, col_offset)
    row_new[...] = row
    col_new[...] = col
    spread_rows(row, spread_ref)
    row_out[...] = jnp.broadcast_to(row_partial(cost_ref, col, row_a, row_b)[None], row_out.shape)
    col_out[...] = jnp.broadcast_to(col_partial(cost_ref, spread_ref, col_a, col_b)[None], col_out.shape)


def last_row_kernel(
    cost_ref, row_parts, col_parts, row_pot, col_pot, row_out, row_new, row_a, row_b, *, row_offset, col_offset
):
    row_new[...] = updated(row_pot, row_parts, row_offset)
    col = updated(col_pot, col_parts, col_offset)
    row_out[...] = jnp.broadcast_to(row_partial(cost_ref, col, row_a, row_b)[None], row_out.shape)


def last_kernel(parts_ref, pot_ref, out_ref, copies_ref, *, offset):
    pot = updated(pot_ref, parts_ref, offset)
    out_ref[...] = pot
    copies_ref[...] = jnp.broadcast_to(pot[None], copies_ref.shape)


def calibrate_kernel(parts_ref, pot_ref, out_ref, *, count):
    total = jnp.sum(jnp.sum(parts_ref[...], axis=0), keepdims=True)
    out_ref[...] = (pot_ref[...] * count - total) * (UNIT / (count - 1))


def exchange(block, axis):
    copies = block if block.ndim == 3 else jnp.broadcast_to(block[None], (lax.axis_size(axis),) + block.shape)
    return lax.all_to_all(copies, axis, 0, 0, tiled=True)


def call(kernel, out_shape, scratch, *args, smem=(), limit=8, **static):
    body = kernel if not static else (lambda *refs: kernel(*refs, **static))
    specs = [pl.BlockSpec(memory_space=pltpu.SMEM) if i in smem else VMEM for i in range(len(args))]
    return pl.pallas_call(
        body,
        out_shape=out_shape,
        in_specs=specs,
        out_specs=[VMEM] * len(out_shape),
        scratch_shapes=scratch,
        compiler_params=pltpu.CompilerParams(vmem_limit_bytes=limit * 2**20),
        cost_estimate=pl.CostEstimate(flops=2**24, bytes_accessed=4 * 2**20, transcendentals=2**20),
    )(*args)


def shards(train_embed, valid_embed, train_labels, valid_labels, pair_level, level_cost):
    row_size, col_size = lax.axis_size("row"), lax.axis_size("col")
    f32 = jnp.float32
    valid_all = lax.all_gather(valid_embed, "row", axis=0, tiled=True)
    shown = jnp.broadcast_to(train_labels.astype(jnp.bfloat16)[:, None], (train_embed.shape[0], LANES))
    train_all = exchange(jnp.concatenate([train_embed, shown], axis=1), "col")
    own_labels = valid_labels.astype(f32)[None, :]
    own_labels, train_all = lax.optimization_barrier((own_labels, train_all))
    label_all = exchange(own_labels, "row")
    rows, cols = train_embed.shape[0] * col_size, valid_all.shape[0]
    row_chunks, col_chunks = rows // LANES, cols // LANES
    classes = pair_level.shape[0]
    levels = jnp.pad(pair_level, ((0, LANES - classes), (0, LANES - classes)), constant_values=-1)
    tile = jax.ShapeDtypeStruct((rows, cols), f32)
    row_copies = jax.ShapeDtypeStruct((col_size, row_chunks, LANES), f32)
    col_copies = jax.ShapeDtypeStruct((row_size, col_chunks, LANES), f32)
    row_shape = jax.ShapeDtypeStruct((row_chunks, LANES), f32)
    col_shape = jax.ShapeDtypeStruct((col_chunks, LANES), f32)
    tall = [pltpu.VMEM((rows, LANES), f32)] * 2
    wide = [pltpu.VMEM((row_chunks * SUB, cols), f32)] * 2
    embed = train_embed.shape[1]
    prepared = call(
        prepare_kernel,
        (
            jax.ShapeDtypeStruct((rows, embed + 3 * LANES), jnp.bfloat16),
            jax.ShapeDtypeStruct((rows, LANES), f32),
            jax.ShapeDtypeStruct((LANES, cols), jnp.bfloat16),
        ),
        [],
        train_all,
        label_all,
        levels,
        level_cost,
        smem=(3,),
        num_levels=level_cost.shape[0],
        limit=16,
    )
    cost, row_part, col_part = call(
        start_kernel, (tile, row_copies, col_copies), tall + wide, *prepared, valid_all, limit=16
    )
    full_rows, full_cols = rows * row_size, cols * col_size
    offsets = {"row_offset": math.log2(full_cols), "col_offset": math.log2(full_rows)}
    row_pot = jnp.zeros(row_shape.shape, f32)
    col_pot = jnp.zeros(col_shape.shape, f32)
    for iteration in range(ITERS - 1):
        row_got = exchange(row_part, "col")
        col_got = exchange(col_part, "row")
        given = (cost, row_got, col_got, row_pot, col_pot)
        if iteration < ITERS - 2:
            row_part, col_part, row_pot, col_pot = call(
                both_kernel, (row_copies, col_copies, row_shape, col_shape), tall + wide + tall[:1], *given, **offsets
            )
        else:
            row_part, row_pot = call(last_row_kernel, (row_copies, row_shape), tall, *given, **offsets)
    row_got = exchange(row_part, "col")
    final_shape = jax.ShapeDtypeStruct((row_size, row_chunks, LANES), f32)
    final, copies = call(
        last_kernel, (row_shape, final_shape), [], row_got, row_pot, offset=offsets["row_offset"]
    )
    (out,) = call(calibrate_kernel, (row_shape,), [], exchange(copies, "row"), final, count=full_rows)
    return out.reshape(rows)


def solution(mesh):
    placed = (
        P(("row", "col"), None),
        P(("row", "col"), None),
        P(("row", "col")),
        P(("row", "col")),
        P(),
        P(),
    )
    return jax.shard_map(shards, mesh=mesh, in_specs=placed, out_specs=P("row"), check_vma=False)
```

```python
import math

import jax
import jax.numpy as jnp
from jax import lax
from jax.experimental import pallas as pl
from jax.experimental.pallas import tpu as pltpu
from jax.sharding import PartitionSpec as P

ITERS = 4
LANES = 128
SUB = 8

entropy_scale = 0.05
UNIT = entropy_scale * math.log(2.0)

ROW = ("zh", "zl", "core")

VMEM = pl.BlockSpec(memory_space=pltpu.VMEM)


def lse_lead(parts):
    high = jnp.max(parts, axis=0)
    return high + jnp.log2(jnp.sum(jnp.exp2(parts - high[None]), axis=0))


def merge(high, total):
    top = jnp.max(high, axis=0, keepdims=True)
    return top + jnp.log2(jnp.sum(total * jnp.exp2(high - top), axis=0, keepdims=True))


def spread_rows(values, out_ref):
    for a in range(values.shape[0]):
        block = jnp.broadcast_to(values[a : a + 1, :], (LANES, LANES))
        out_ref[a * LANES : (a + 1) * LANES, :] = block.T


def peak_and_sum(tiles):
    high = tiles[0]
    for tile in tiles[1:]:
        high = jnp.maximum(high, tile)
    total = jnp.exp2(tiles[0] - high)
    for tile in tiles[1:]:
        total = total + jnp.exp2(tile - high)
    return high, total


def col_partial(cost_ref, row_ref, high_ref, total_ref):
    rows, cols = cost_ref.shape
    blocks, chunks = rows // LANES, cols // LANES
    groups = LANES // SUB

    def block_step(q, carry):
        start = pl.multiple_of(q * LANES, LANES)
        bases = None if row_ref is None else [row_ref[pl.ds(start + g * SUB, SUB), :] for g in range(groups)]
        for k in range(chunks):
            cells = [cost_ref[pl.ds(start + g * SUB, SUB), k * LANES : (k + 1) * LANES] for g in range(groups)]
            tiles = [-cell for cell in cells] if bases is None else [base - cell for base, cell in zip(bases, cells)]
            high, total = peak_and_sum(tiles)
            here = (pl.ds(pl.multiple_of(q * SUB, SUB), SUB), slice(k * LANES, (k + 1) * LANES))
            high_ref[here] = high
            total_ref[here] = total
        return carry

    lax.fori_loop(0, blocks, block_step, 0)
    out = [merge(high_ref[:, k * LANES : (k + 1) * LANES], total_ref[:, k * LANES : (k + 1) * LANES]) for k in range(chunks)]
    return jnp.concatenate(out, axis=0)


def row_partial(cost_ref, col, high_ref, total_ref):
    rows, cols = cost_ref.shape
    chunks = cols // LANES
    bases = None if col is None else [jnp.broadcast_to(col[k : k + 1, :], (SUB, LANES)) for k in range(chunks)]

    def group_step(g, carry):
        here = pl.ds(pl.multiple_of(g * SUB, SUB), SUB)
        cells = [cost_ref[here, k * LANES : (k + 1) * LANES] for k in range(chunks)]
        tiles = [-cell for cell in cells] if bases is None else [base - cell for base, cell in zip(bases, cells)]
        high_ref[here, :], total_ref[here, :] = peak_and_sum(tiles)
        return carry

    lax.fori_loop(0, rows // SUB, group_step, 0, unroll=4)
    out = []
    for a in range(rows // LANES):
        block = slice(a * LANES, (a + 1) * LANES)
        out.append(merge(high_ref[block, :].T, total_ref[block, :].T))
    return jnp.concatenate(out, axis=0)


def split3(values):
    high = values.astype(jnp.bfloat16)
    rest = values - high.astype(jnp.float32)
    mid = rest.astype(jnp.bfloat16)
    low = (rest - mid.astype(jnp.float32)).astype(jnp.bfloat16)
    return high, mid, low


def dot(left, right, dims):
    return lax.dot_general(left, right, (dims, ((), ())), preferred_element_type=jnp.float32)


def prepare_kernel(train_ref, levels_ref, level_cost_ref, left_ref, sq_ref, *, num_levels):
    shards, shard_rows, width = train_ref.shape
    embed = width - LANES
    packed = train_ref[...].reshape(shards * shard_rows, width)
    train = packed[:, :embed]
    wide = train.astype(jnp.float32)
    train_sq = jnp.sum(wide * wide, axis=1, keepdims=True) * (1.0 / embed)
    sq_ref[...] = jnp.broadcast_to(train_sq, sq_ref.shape)
    left_ref[:, :embed] = train * jnp.bfloat16(-2.0 / embed)
    levels = levels_ref[...]
    table = jnp.zeros(levels.shape, jnp.float32)
    for level in range(num_levels):
        table = table + jnp.where(levels == level, level_cost_ref[level], 0.0)
    labels = packed[:, embed:].astype(jnp.float32)
    lane_ids = lax.broadcasted_iota(jnp.int32, labels.shape, 1).astype(jnp.float32)
    train_hot = jnp.where(labels == lane_ids, 1.0, 0.0).astype(jnp.bfloat16)
    parts = [dot(train_hot, part, ((1,), (0,))).astype(jnp.bfloat16) for part in split3(table)]
    left_ref[:, embed:] = jnp.concatenate(parts, axis=1)


def start_kernel(
    where_ref, left_ref, sq_ref, mine_ref, other_ref, cost_ref, row_out, col_out, row_a, row_b, col_a, col_b
):
    steps, sides, block_rows, embed = mine_ref.shape
    table_parts = (left_ref.shape[1] - embed) // LANES
    train_sq = jnp.concatenate([sq_ref[...]] * sides, axis=1)
    ones = jnp.ones((SUB, embed), jnp.bfloat16)
    class_ids = lax.broadcasted_iota(jnp.int32, (LANES, LANES), 0).astype(jnp.float32)
    step = sides * LANES
    for pair in range(2 * steps):
        core, z_pair = divmod(pair, steps)
        back = lax.rem(where_ref[0] - z_pair + steps, steps)
        own = where_ref[1] == core
        blocks = [jnp.where(own, mine_ref[back, side], other_ref[back, side]) for side in range(sides)]
        block = jnp.concatenate([b[:LANES, :] for b in blocks], axis=0)
        label_rows = [b[LANES:, :LANES].astype(jnp.float32)[:1, :] for b in blocks]
        hots = [jnp.where(class_ids == label_row, 1.0, 0.0).astype(jnp.bfloat16) for label_row in label_rows]
        hot = jnp.concatenate(hots, axis=1)
        wide = block.astype(jnp.float32)
        squares = wide * wide
        sq_high = squares.astype(jnp.bfloat16)
        sq_low = (squares - sq_high.astype(jnp.float32)).astype(jnp.bfloat16)
        block_sq = (dot(ones, sq_high, ((1,), (1,))) + dot(ones, sq_low, ((1,), (1,))))[:1, :]
        cost = dot(left_ref[:, :embed], block, ((1,), (1,)))
        cost = cost + dot(left_ref[:, embed:], jnp.concatenate([hot] * table_parts, axis=0), ((1,), (0,)))
        here = slice(pair * step, (pair + 1) * step)
        cost_ref[:, here] = (cost + (train_sq + block_sq * (1.0 / embed))) * (1.0 / UNIT)
    row_out[...] = jnp.broadcast_to(row_partial(cost_ref, None, row_a, row_b)[None], row_out.shape)
    col_out[...] = jnp.broadcast_to(col_partial(cost_ref, None, col_a, col_b)[None], col_out.shape)


def updated(pot_ref, parts_ref, offset):
    return 0.5 * (pot_ref[...] + (offset - lse_lead(parts_ref[...])))


def both_kernel(
    cost_ref, row_parts, col_parts, row_pot, col_pot, row_out, col_out, row_new, col_new, row_a, row_b, col_a, col_b,
    spread_ref, *, row_offset, col_offset
):
    row, col = updated(row_pot, row_parts, row_offset), updated(col_pot, col_parts, col_offset)
    row_new[...] = row
    col_new[...] = col
    spread_rows(row, spread_ref)
    row_out[...] = jnp.broadcast_to(row_partial(cost_ref, col, row_a, row_b)[None], row_out.shape)
    col_out[...] = jnp.broadcast_to(col_partial(cost_ref, spread_ref, col_a, col_b)[None], col_out.shape)


def last_row_kernel(
    cost_ref, row_parts, col_parts, row_pot, col_pot, row_out, row_new, row_a, row_b, *, row_offset, col_offset
):
    row_new[...] = updated(row_pot, row_parts, row_offset)
    col = updated(col_pot, col_parts, col_offset)
    row_out[...] = jnp.broadcast_to(row_partial(cost_ref, col, row_a, row_b)[None], row_out.shape)


def last_kernel(parts_ref, pot_ref, out_ref, copies_ref, *, offset):
    pot = updated(pot_ref, parts_ref, offset)
    out_ref[...] = pot
    copies_ref[...] = jnp.broadcast_to(pot[None], copies_ref.shape)


def calibrate_kernel(parts_ref, pot_ref, out_ref, *, count):
    total = jnp.sum(jnp.sum(parts_ref[...], axis=0), keepdims=True)
    out_ref[...] = (pot_ref[...] * count - total) * (UNIT / (count - 1))


def exchange(block, axis):
    copies = block if block.ndim == 3 else jnp.broadcast_to(block[None], (lax.axis_size(axis),) + block.shape)
    return lax.all_to_all(copies, axis, 0, 0, tiled=True)


def call(kernel, out_shape, scratch, *args, smem=(), limit=8, **static):
    body = kernel if not static else (lambda *refs: kernel(*refs, **static))
    specs = [pl.BlockSpec(memory_space=pltpu.SMEM) if i in smem else VMEM for i in range(len(args))]
    return pl.pallas_call(
        body,
        out_shape=out_shape,
        in_specs=specs,
        out_specs=[VMEM] * len(out_shape),
        scratch_shapes=scratch,
        compiler_params=pltpu.CompilerParams(vmem_limit_bytes=limit * 2**20),
        cost_estimate=pl.CostEstimate(flops=2**24, bytes_accessed=4 * 2**20, transcendentals=2**20),
    )(*args)


def shards(train_embed, valid_embed, train_labels, valid_labels, pair_level, level_cost):
    row_size, col_size = lax.axis_size(ROW), lax.axis_size("col")
    f32 = jnp.float32
    embed = train_embed.shape[1]
    shown = jnp.broadcast_to(train_labels.astype(jnp.bfloat16)[:, None], (train_embed.shape[0], LANES))
    train_all = exchange(jnp.concatenate([train_embed, shown], axis=1), "col")
    label_row = jnp.tile(valid_labels.astype(jnp.bfloat16), embed // LANES)[None, :]
    valid_pack = jnp.concatenate([valid_embed, jnp.broadcast_to(label_row, (16, embed))], axis=0)
    pair = lax.all_gather(valid_pack, "zl", axis=0)
    steps = lax.axis_size("zh")
    turn = [[(i, (i + k) % steps) for i in range(steps)] for k in range(steps)]
    mine = jnp.stack([pair] + [lax.ppermute(pair, "zh", turn[k]) for k in range(1, steps)])
    other = lax.ppermute(mine, "core", [(0, 1), (1, 0)])
    where = jnp.stack([lax.axis_index("zh"), lax.axis_index("core")]).astype(jnp.int32)
    rows, cols = train_embed.shape[0] * col_size, valid_embed.shape[0] * row_size
    row_chunks, col_chunks = rows // LANES, cols // LANES
    classes = pair_level.shape[0]
    levels = jnp.pad(pair_level, ((0, LANES - classes), (0, LANES - classes)), constant_values=-1)
    tile = jax.ShapeDtypeStruct((rows, cols), f32)
    row_copies = jax.ShapeDtypeStruct((col_size, row_chunks, LANES), f32)
    col_copies = jax.ShapeDtypeStruct((row_size, col_chunks, LANES), f32)
    row_shape = jax.ShapeDtypeStruct((row_chunks, LANES), f32)
    col_shape = jax.ShapeDtypeStruct((col_chunks, LANES), f32)
    tall = [pltpu.VMEM((rows, LANES), f32)] * 2
    wide = [pltpu.VMEM((row_chunks * SUB, cols), f32)] * 2
    prepared = call(
        prepare_kernel,
        (jax.ShapeDtypeStruct((rows, embed + 3 * LANES), jnp.bfloat16), jax.ShapeDtypeStruct((rows, LANES), f32)),
        [],
        train_all,
        levels,
        level_cost,
        smem=(2,),
        num_levels=level_cost.shape[0],
        limit=16,
    )
    cost, row_part, col_part = call(
        start_kernel,
        (tile, row_copies, col_copies),
        tall + wide,
        where,
        *prepared,
        mine,
        other,
        smem=(0,),
        limit=16,
    )
    full_rows, full_cols = rows * row_size, cols * col_size
    offsets = {"row_offset": math.log2(full_cols), "col_offset": math.log2(full_rows)}
    row_pot = jnp.zeros(row_shape.shape, f32)
    col_pot = jnp.zeros(col_shape.shape, f32)
    for iteration in range(ITERS - 1):
        row_got = exchange(row_part, "col")
        col_got = exchange(col_part, ROW)
        given = (cost, row_got, col_got, row_pot, col_pot)
        if iteration < ITERS - 2:
            row_part, col_part, row_pot, col_pot = call(
                both_kernel, (row_copies, col_copies, row_shape, col_shape), tall + wide + tall[:1], *given, **offsets
            )
        else:
            row_part, row_pot = call(last_row_kernel, (row_copies, row_shape), tall, *given, **offsets)
    row_got = exchange(row_part, "col")
    final_shape = jax.ShapeDtypeStruct((row_size, row_chunks, LANES), f32)
    final, copies = call(
        last_kernel, (row_shape, final_shape), [], row_got, row_pot, offset=offsets["row_offset"]
    )
    (out,) = call(calibrate_kernel, (row_shape,), [], exchange(copies, ROW), final, count=full_rows)
    return out.reshape(rows)


def solution(mesh):
    row_size, col_size = mesh.shape["row"], mesh.shape["col"]
    finer = jax.sharding.Mesh(mesh.devices.reshape(row_size // 4, 2, 2, col_size), ROW + ("col",))
    both = ROW + ("col",)
    placed = (P(both, None), P(both, None), P(both), P(both), P(), P())
    return jax.shard_map(shards, mesh=finer, in_specs=placed, out_specs=P(ROW), check_vma=False)
```

```python
import math

import jax
import jax.numpy as jnp
from jax import lax
from jax.experimental import pallas as pl
from jax.experimental.pallas import tpu as pltpu
from jax.sharding import PartitionSpec as P

ITERS = 4
LANES = 128
SUB = 8

entropy_scale = 0.05
UNIT = entropy_scale * math.log(2.0)

ROW = ("zh", "zl", "core")

VMEM = pl.BlockSpec(memory_space=pltpu.VMEM)


def lse_lead(parts):
    high = jnp.max(parts, axis=0)
    return high + jnp.log2(jnp.sum(jnp.exp2(parts - high[None]), axis=0))


def merge(high, total):
    top = jnp.max(high, axis=0, keepdims=True)
    return top + jnp.log2(jnp.sum(total * jnp.exp2(high - top), axis=0, keepdims=True))


def spread_rows(values, out_ref):
    for a in range(values.shape[0]):
        block = jnp.broadcast_to(values[a : a + 1, :], (LANES, LANES))
        out_ref[a * LANES : (a + 1) * LANES, :] = block.T


def peak_and_sum(tiles):
    high = tiles[0]
    for tile in tiles[1:]:
        high = jnp.maximum(high, tile)
    total = jnp.exp2(tiles[0] - high)
    for tile in tiles[1:]:
        total = total + jnp.exp2(tile - high)
    return high, total


def col_partial(cost_ref, row_ref, high_ref, total_ref):
    rows, cols = cost_ref.shape
    blocks, chunks = rows // LANES, cols // LANES
    groups = LANES // SUB

    def block_step(q, carry):
        start = pl.multiple_of(q * LANES, LANES)
        bases = None if row_ref is None else [row_ref[pl.ds(start + g * SUB, SUB), :] for g in range(groups)]
        for k in range(chunks):
            cells = [cost_ref[pl.ds(start + g * SUB, SUB), k * LANES : (k + 1) * LANES] for g in range(groups)]
            tiles = [-cell for cell in cells] if bases is None else [base - cell for base, cell in zip(bases, cells)]
            high, total = peak_and_sum(tiles)
            here = (pl.ds(pl.multiple_of(q * SUB, SUB), SUB), slice(k * LANES, (k + 1) * LANES))
            high_ref[here] = high
            total_ref[here] = total
        return carry

    lax.fori_loop(0, blocks, block_step, 0)
    out = [merge(high_ref[:, k * LANES : (k + 1) * LANES], total_ref[:, k * LANES : (k + 1) * LANES]) for k in range(chunks)]
    return jnp.concatenate(out, axis=0)


def row_partial(cost_ref, col, high_ref, total_ref):
    rows, cols = cost_ref.shape
    chunks = cols // LANES
    bases = None if col is None else [jnp.broadcast_to(col[k : k + 1, :], (SUB, LANES)) for k in range(chunks)]

    def group_step(g, carry):
        here = pl.ds(pl.multiple_of(g * SUB, SUB), SUB)
        cells = [cost_ref[here, k * LANES : (k + 1) * LANES] for k in range(chunks)]
        tiles = [-cell for cell in cells] if bases is None else [base - cell for base, cell in zip(bases, cells)]
        high_ref[here, :], total_ref[here, :] = peak_and_sum(tiles)
        return carry

    lax.fori_loop(0, rows // SUB, group_step, 0, unroll=4)
    out = []
    for a in range(rows // LANES):
        block = slice(a * LANES, (a + 1) * LANES)
        out.append(merge(high_ref[block, :].T, total_ref[block, :].T))
    return jnp.concatenate(out, axis=0)


def split3(values):
    high = values.astype(jnp.bfloat16)
    rest = values - high.astype(jnp.float32)
    mid = rest.astype(jnp.bfloat16)
    low = (rest - mid.astype(jnp.float32)).astype(jnp.bfloat16)
    return high, mid, low


def dot(left, right, dims):
    return lax.dot_general(left, right, (dims, ((), ())), preferred_element_type=jnp.float32)


def prepare_kernel(train_ref, levels_ref, level_cost_ref, left_ref, sq_ref, *, num_levels):
    shards, shard_rows, width = train_ref.shape
    embed = width - LANES
    packed = train_ref[...].reshape(shards * shard_rows, width)
    train = packed[:, :embed]
    wide = train.astype(jnp.float32)
    train_sq = jnp.sum(wide * wide, axis=1, keepdims=True) * (1.0 / embed)
    sq_ref[...] = jnp.broadcast_to(train_sq, sq_ref.shape)
    left_ref[:, :embed] = train * jnp.bfloat16(-2.0 / embed)
    levels = levels_ref[...]
    table = jnp.zeros(levels.shape, jnp.float32)
    for level in range(num_levels):
        table = table + jnp.where(levels == level, level_cost_ref[level], 0.0)
    labels = packed[:, embed:].astype(jnp.float32)
    lane_ids = lax.broadcasted_iota(jnp.int32, labels.shape, 1).astype(jnp.float32)
    train_hot = jnp.where(labels == lane_ids, 1.0, 0.0).astype(jnp.bfloat16)
    parts = [dot(train_hot, part, ((1,), (0,))).astype(jnp.bfloat16) for part in split3(table)]
    left_ref[:, embed:] = jnp.concatenate(parts, axis=1)


def start_kernel(
    where_ref, left_ref, sq_ref, mine_ref, other_ref, cost_ref, row_out, col_out, row_a, row_b, col_a, col_b
):
    steps, sides, block_rows, embed = mine_ref.shape
    table_parts = (left_ref.shape[1] - embed) // LANES
    train_sq = jnp.concatenate([sq_ref[...]] * sides, axis=1)
    ones = jnp.ones((SUB, embed), jnp.bfloat16)
    class_ids = lax.broadcasted_iota(jnp.int32, (LANES, LANES), 0).astype(jnp.float32)
    step = sides * LANES
    for pair in range(2 * steps):
        core, z_pair = divmod(pair, steps)
        back = lax.rem(where_ref[0] - z_pair + steps, steps)
        own = where_ref[1] == core
        blocks = [jnp.where(own, mine_ref[back, side], other_ref[back, side]) for side in range(sides)]
        block = jnp.concatenate([b[:LANES, :] for b in blocks], axis=0)
        label_rows = [b[LANES:, :LANES].astype(jnp.float32)[:1, :] for b in blocks]
        hots = [jnp.where(class_ids == label_row, 1.0, 0.0).astype(jnp.bfloat16) for label_row in label_rows]
        hot = jnp.concatenate(hots, axis=1)
        wide = block.astype(jnp.float32)
        squares = wide * wide
        sq_high = squares.astype(jnp.bfloat16)
        sq_low = (squares - sq_high.astype(jnp.float32)).astype(jnp.bfloat16)
        block_sq = (dot(ones, sq_high, ((1,), (1,))) + dot(ones, sq_low, ((1,), (1,))))[:1, :]
        cost = dot(left_ref[:, :embed], block, ((1,), (1,)))
        cost = cost + dot(left_ref[:, embed:], jnp.concatenate([hot] * table_parts, axis=0), ((1,), (0,)))
        here = slice(pair * step, (pair + 1) * step)
        cost_ref[:, here] = (cost + (train_sq + block_sq * (1.0 / embed))) * (1.0 / UNIT)
    row_out[...] = jnp.broadcast_to(row_partial(cost_ref, None, row_a, row_b)[None], row_out.shape)
    col_out[...] = jnp.broadcast_to(col_partial(cost_ref, None, col_a, col_b)[None], col_out.shape)


def updated(pot_ref, parts_ref, offset):
    return 0.5 * (pot_ref[...] + (offset - lse_lead(parts_ref[...])))


def both_kernel(
    cost_ref, row_parts, col_parts, row_pot, col_pot, row_out, col_out, row_new, col_new, row_a, row_b, col_a, col_b,
    spread_ref, *, row_offset, col_offset
):
    row, col = updated(row_pot, row_parts, row_offset), updated(col_pot, col_parts, col_offset)
    row_new[...] = row
    col_new[...] = col
    spread_rows(row, spread_ref)
    row_out[...] = jnp.broadcast_to(row_partial(cost_ref, col, row_a, row_b)[None], row_out.shape)
    col_out[...] = jnp.broadcast_to(col_partial(cost_ref, spread_ref, col_a, col_b)[None], col_out.shape)


def last_row_kernel(
    cost_ref, row_parts, col_parts, row_pot, col_pot, row_out, row_new, row_a, row_b, *, row_offset, col_offset
):
    row_new[...] = updated(row_pot, row_parts, row_offset)
    col = updated(col_pot, col_parts, col_offset)
    row_out[...] = jnp.broadcast_to(row_partial(cost_ref, col, row_a, row_b)[None], row_out.shape)


def last_kernel(parts_ref, pot_ref, out_ref, copies_ref, *, offset):
    pot = updated(pot_ref, parts_ref, offset)
    out_ref[...] = pot
    copies_ref[...] = jnp.broadcast_to(pot[None], copies_ref.shape)


def calibrate_kernel(parts_ref, pot_ref, out_ref, *, count):
    total = jnp.sum(jnp.sum(parts_ref[...], axis=0), keepdims=True)
    out_ref[...] = (pot_ref[...] * count - total) * (UNIT / (count - 1))


def exchange(block, axis):
    copies = block if block.ndim == 3 else jnp.broadcast_to(block[None], (lax.axis_size(axis),) + block.shape)
    return lax.all_to_all(copies, axis, 0, 0, tiled=True)


def call(kernel, out_shape, scratch, *args, smem=(), limit=8, **static):
    body = kernel if not static else (lambda *refs: kernel(*refs, **static))
    specs = [pl.BlockSpec(memory_space=pltpu.SMEM) if i in smem else VMEM for i in range(len(args))]
    return pl.pallas_call(
        body,
        out_shape=out_shape,
        in_specs=specs,
        out_specs=[VMEM] * len(out_shape),
        scratch_shapes=scratch,
        compiler_params=pltpu.CompilerParams(vmem_limit_bytes=limit * 2**20),
        cost_estimate=pl.CostEstimate(flops=2**24, bytes_accessed=4 * 2**20, transcendentals=2**20),
    )(*args)


def shards(train_embed, valid_embed, train_labels, valid_labels, pair_level, level_cost):
    row_size, col_size = lax.axis_size(ROW), lax.axis_size("col")
    f32 = jnp.float32
    embed = train_embed.shape[1]
    shown = jnp.broadcast_to(train_labels.astype(jnp.bfloat16)[:, None], (train_embed.shape[0], LANES))
    train_all = exchange(jnp.concatenate([train_embed, shown], axis=1), "col")
    label_row = jnp.tile(valid_labels.astype(jnp.bfloat16), embed // LANES)[None, :]
    valid_pack = jnp.concatenate([valid_embed, jnp.broadcast_to(label_row, (16, embed))], axis=0)
    pair = lax.all_gather(valid_pack, "zl", axis=0)
    steps = lax.axis_size("zh")
    turn = [[(i, (i + k) % steps) for i in range(steps)] for k in range(steps)]
    mine = jnp.stack([pair] + [lax.ppermute(pair, "zh", turn[k]) for k in range(1, steps)])
    mine, train_all = lax.optimization_barrier((mine, train_all))
    other = lax.ppermute(mine, "core", [(0, 1), (1, 0)])
    where = jnp.stack([lax.axis_index("zh"), lax.axis_index("core")]).astype(jnp.int32)
    rows, cols = train_embed.shape[0] * col_size, valid_embed.shape[0] * row_size
    row_chunks, col_chunks = rows // LANES, cols // LANES
    classes = pair_level.shape[0]
    levels = jnp.pad(pair_level, ((0, LANES - classes), (0, LANES - classes)), constant_values=-1)
    tile = jax.ShapeDtypeStruct((rows, cols), f32)
    row_copies = jax.ShapeDtypeStruct((col_size, row_chunks, LANES), f32)
    col_copies = jax.ShapeDtypeStruct((row_size, col_chunks, LANES), f32)
    row_shape = jax.ShapeDtypeStruct((row_chunks, LANES), f32)
    col_shape = jax.ShapeDtypeStruct((col_chunks, LANES), f32)
    tall = [pltpu.VMEM((rows, LANES), f32)] * 2
    wide = [pltpu.VMEM((row_chunks * SUB, cols), f32)] * 2
    prepared = call(
        prepare_kernel,
        (jax.ShapeDtypeStruct((rows, embed + 3 * LANES), jnp.bfloat16), jax.ShapeDtypeStruct((rows, LANES), f32)),
        [],
        train_all,
        levels,
        level_cost,
        smem=(2,),
        num_levels=level_cost.shape[0],
        limit=16,
    )
    cost, row_part, col_part = call(
        start_kernel,
        (tile, row_copies, col_copies),
        tall + wide,
        where,
        *prepared,
        mine,
        other,
        smem=(0,),
        limit=16,
    )
    full_rows, full_cols = rows * row_size, cols * col_size
    offsets = {"row_offset": math.log2(full_cols), "col_offset": math.log2(full_rows)}
    row_pot = jnp.zeros(row_shape.shape, f32)
    col_pot = jnp.zeros(col_shape.shape, f32)
    for iteration in range(ITERS - 1):
        row_got = exchange(row_part, "col")
        col_got = exchange(col_part, ROW)
        given = (cost, row_got, col_got, row_pot, col_pot)
        if iteration < ITERS - 2:
            row_part, col_part, row_pot, col_pot = call(
                both_kernel, (row_copies, col_copies, row_shape, col_shape), tall + wide + tall[:1], *given, **offsets
            )
        else:
            row_part, row_pot = call(last_row_kernel, (row_copies, row_shape), tall, *given, **offsets)
    row_got = exchange(row_part, "col")
    final_shape = jax.ShapeDtypeStruct((row_size, row_chunks, LANES), f32)
    final, copies = call(
        last_kernel, (row_shape, final_shape), [], row_got, row_pot, offset=offsets["row_offset"]
    )
    (out,) = call(calibrate_kernel, (row_shape,), [], exchange(copies, ROW), final, count=full_rows)
    return out.reshape(rows)


def solution(mesh):
    row_size, col_size = mesh.shape["row"], mesh.shape["col"]
    finer = jax.sharding.Mesh(mesh.devices.reshape(row_size // 4, 2, 2, col_size), ROW + ("col",))
    both = ROW + ("col",)
    placed = (P(both, None), P(both, None), P(both), P(both), P(), P())
    return jax.shard_map(shards, mesh=finer, in_specs=placed, out_specs=P(ROW), check_vma=False)
```

```python
import math

import jax
import jax.numpy as jnp
from jax import lax
from jax.experimental import pallas as pl
from jax.experimental.pallas import tpu as pltpu
from jax.sharding import PartitionSpec as P

ITERS = 4
LANES = 128
SUB = 8

entropy_scale = 0.05
UNIT = entropy_scale * math.log(2.0)

ROW = ("zh", "zl", "core")

VMEM = pl.BlockSpec(memory_space=pltpu.VMEM)


def lse_lead(parts):
    high = jnp.max(parts, axis=0)
    return high + jnp.log2(jnp.sum(jnp.exp2(parts - high[None]), axis=0))


def merge(high, total):
    top = jnp.max(high, axis=0, keepdims=True)
    return top + jnp.log2(jnp.sum(total * jnp.exp2(high - top), axis=0, keepdims=True))


def spread_rows(values, out_ref):
    for a in range(values.shape[0]):
        block = jnp.broadcast_to(values[a : a + 1, :], (LANES, LANES))
        out_ref[a * LANES : (a + 1) * LANES, :] = block.T


def peak_and_sum(tiles):
    high = tiles[0]
    for tile in tiles[1:]:
        high = jnp.maximum(high, tile)
    total = jnp.exp2(tiles[0] - high)
    for tile in tiles[1:]:
        total = total + jnp.exp2(tile - high)
    return high, total


def col_partial(cost_ref, row_ref, high_ref, total_ref):
    rows, cols = cost_ref.shape
    blocks, chunks = rows // LANES, cols // LANES
    groups = LANES // SUB

    def block_step(q, carry):
        start = pl.multiple_of(q * LANES, LANES)
        bases = None if row_ref is None else [row_ref[pl.ds(start + g * SUB, SUB), :] for g in range(groups)]
        for k in range(chunks):
            cells = [cost_ref[pl.ds(start + g * SUB, SUB), k * LANES : (k + 1) * LANES] for g in range(groups)]
            tiles = [-cell for cell in cells] if bases is None else [base - cell for base, cell in zip(bases, cells)]
            high, total = peak_and_sum(tiles)
            here = (pl.ds(pl.multiple_of(q * SUB, SUB), SUB), slice(k * LANES, (k + 1) * LANES))
            high_ref[here] = high
            total_ref[here] = total
        return carry

    lax.fori_loop(0, blocks, block_step, 0)
    out = [merge(high_ref[:, k * LANES : (k + 1) * LANES], total_ref[:, k * LANES : (k + 1) * LANES]) for k in range(chunks)]
    return jnp.concatenate(out, axis=0)


def row_partial(cost_ref, col, high_ref, total_ref):
    rows, cols = cost_ref.shape
    chunks = cols // LANES
    bases = None if col is None else [jnp.broadcast_to(col[k : k + 1, :], (SUB, LANES)) for k in range(chunks)]

    def group_step(g, carry):
        here = pl.ds(pl.multiple_of(g * SUB, SUB), SUB)
        cells = [cost_ref[here, k * LANES : (k + 1) * LANES] for k in range(chunks)]
        tiles = [-cell for cell in cells] if bases is None else [base - cell for base, cell in zip(bases, cells)]
        high_ref[here, :], total_ref[here, :] = peak_and_sum(tiles)
        return carry

    lax.fori_loop(0, rows // SUB, group_step, 0, unroll=4)
    out = []
    for a in range(rows // LANES):
        block = slice(a * LANES, (a + 1) * LANES)
        out.append(merge(high_ref[block, :].T, total_ref[block, :].T))
    return jnp.concatenate(out, axis=0)


def split3(values):
    high = values.astype(jnp.bfloat16)
    rest = values - high.astype(jnp.float32)
    mid = rest.astype(jnp.bfloat16)
    low = (rest - mid.astype(jnp.float32)).astype(jnp.bfloat16)
    return high, mid, low


def dot(left, right, dims):
    return lax.dot_general(left, right, (dims, ((), ())), preferred_element_type=jnp.float32)


def prepare_kernel(train_ref, levels_ref, level_cost_ref, left_ref, sq_ref, *, num_levels):
    shards, shard_rows, width = train_ref.shape
    embed = width - LANES
    packed = train_ref[...].reshape(shards * shard_rows, width)
    train = packed[:, :embed]
    wide = train.astype(jnp.float32)
    train_sq = jnp.sum(wide * wide, axis=1, keepdims=True) * (1.0 / embed)
    sq_ref[...] = jnp.broadcast_to(train_sq, sq_ref.shape)
    left_ref[:, :embed] = train * jnp.bfloat16(-2.0 / embed)
    levels = levels_ref[...]
    table = jnp.zeros(levels.shape, jnp.float32)
    for level in range(num_levels):
        table = table + jnp.where(levels == level, level_cost_ref[level], 0.0)
    labels = packed[:, embed:].astype(jnp.float32)
    lane_ids = lax.broadcasted_iota(jnp.int32, labels.shape, 1).astype(jnp.float32)
    train_hot = jnp.where(labels == lane_ids, 1.0, 0.0).astype(jnp.bfloat16)
    parts = [dot(train_hot, part, ((1,), (0,))).astype(jnp.bfloat16) for part in split3(table)]
    left_ref[:, embed:] = jnp.concatenate(parts, axis=1)


def start_kernel(
    where_ref, left_ref, sq_ref, mine_ref, other_ref, cost_ref, row_out, col_out, row_a, row_b, col_a, col_b
):
    steps, sides, block_rows, embed = mine_ref.shape
    table_parts = (left_ref.shape[1] - embed) // LANES
    train_sq = jnp.concatenate([sq_ref[...]] * sides, axis=1)
    ones = jnp.ones((SUB, embed), jnp.bfloat16)
    class_ids = lax.broadcasted_iota(jnp.int32, (LANES, LANES), 0).astype(jnp.float32)
    step = sides * LANES
    for pair in range(2 * steps):
        core, z_pair = divmod(pair, steps)
        back = lax.rem(where_ref[0] - z_pair + steps, steps)
        own = where_ref[1] == core
        blocks = [jnp.where(own, mine_ref[back, side], other_ref[back, side]) for side in range(sides)]
        block = jnp.concatenate([b[:LANES, :] for b in blocks], axis=0)
        label_rows = [b[LANES:, :LANES].astype(jnp.float32)[:1, :] for b in blocks]
        hots = [jnp.where(class_ids == label_row, 1.0, 0.0).astype(jnp.bfloat16) for label_row in label_rows]
        hot = jnp.concatenate(hots, axis=1)
        wide = block.astype(jnp.float32)
        squares = wide * wide
        sq_high = squares.astype(jnp.bfloat16)
        sq_low = (squares - sq_high.astype(jnp.float32)).astype(jnp.bfloat16)
        block_sq = (dot(ones, sq_high, ((1,), (1,))) + dot(ones, sq_low, ((1,), (1,))))[:1, :]
        cost = dot(left_ref[:, :embed], block, ((1,), (1,)))
        cost = cost + dot(left_ref[:, embed:], jnp.concatenate([hot] * table_parts, axis=0), ((1,), (0,)))
        here = slice(pair * step, (pair + 1) * step)
        cost_ref[:, here] = (cost + (train_sq + block_sq * (1.0 / embed))) * (1.0 / UNIT)
    row_out[...] = jnp.broadcast_to(row_partial(cost_ref, None, row_a, row_b)[None], row_out.shape)
    col_out[...] = jnp.broadcast_to(col_partial(cost_ref, None, col_a, col_b)[None], col_out.shape)


def updated(pot_ref, parts_ref, offset):
    return 0.5 * (pot_ref[...] + (offset - lse_lead(parts_ref[...])))


def both_kernel(
    cost_ref, row_parts, col_parts, row_pot, col_pot, row_out, col_out, row_new, col_new, row_a, row_b, col_a, col_b,
    spread_ref, *, row_offset, col_offset
):
    row, col = updated(row_pot, row_parts, row_offset), updated(col_pot, col_parts, col_offset)
    row_new[...] = row
    col_new[...] = col
    spread_rows(row, spread_ref)
    row_out[...] = jnp.broadcast_to(row_partial(cost_ref, col, row_a, row_b)[None], row_out.shape)
    col_out[...] = jnp.broadcast_to(col_partial(cost_ref, spread_ref, col_a, col_b)[None], col_out.shape)


def last_row_kernel(
    cost_ref, row_parts, col_parts, row_pot, col_pot, row_out, row_new, row_a, row_b, *, row_offset, col_offset
):
    row_new[...] = updated(row_pot, row_parts, row_offset)
    col = updated(col_pot, col_parts, col_offset)
    row_out[...] = jnp.broadcast_to(row_partial(cost_ref, col, row_a, row_b)[None], row_out.shape)


def last_kernel(parts_ref, pot_ref, out_ref, copies_ref, *, offset):
    pot = updated(pot_ref, parts_ref, offset)
    out_ref[...] = pot
    copies_ref[...] = jnp.broadcast_to(pot[None], copies_ref.shape)


def calibrate_kernel(parts_ref, pot_ref, out_ref, *, count):
    total = jnp.sum(jnp.sum(parts_ref[...], axis=0), keepdims=True)
    out_ref[...] = (pot_ref[...] * count - total) * (UNIT / (count - 1))


def exchange(block, axis):
    copies = block if block.ndim == 3 else jnp.broadcast_to(block[None], (lax.axis_size(axis),) + block.shape)
    return lax.all_to_all(copies, axis, 0, 0, tiled=True)


def call(kernel, out_shape, scratch, *args, smem=(), limit=8, **static):
    body = kernel if not static else (lambda *refs: kernel(*refs, **static))
    specs = [pl.BlockSpec(memory_space=pltpu.SMEM) if i in smem else VMEM for i in range(len(args))]
    return pl.pallas_call(
        body,
        out_shape=out_shape,
        in_specs=specs,
        out_specs=[VMEM] * len(out_shape),
        scratch_shapes=scratch,
        compiler_params=pltpu.CompilerParams(vmem_limit_bytes=limit * 2**20),
        cost_estimate=pl.CostEstimate(flops=2**24, bytes_accessed=4 * 2**20, transcendentals=2**20),
    )(*args)


def shards(train_embed, valid_embed, train_labels, valid_labels, pair_level, level_cost):
    row_size, col_size = lax.axis_size(ROW), lax.axis_size("col")
    f32 = jnp.float32
    embed = train_embed.shape[1]
    shown = jnp.broadcast_to(train_labels.astype(jnp.bfloat16)[:, None], (train_embed.shape[0], LANES))
    train_all = exchange(jnp.concatenate([train_embed, shown], axis=1), "col")
    label_row = jnp.tile(valid_labels.astype(jnp.bfloat16), embed // LANES)[None, :]
    valid_pack = jnp.concatenate([valid_embed, jnp.broadcast_to(label_row, (16, embed))], axis=0)
    pair = lax.all_gather(valid_pack, "zl", axis=0)
    steps = lax.axis_size("zh")
    ahead, behind = [[(i, (i + k) % steps) for i in range(steps)] for k in (1, -1)]
    from_low, from_high = lax.ppermute(pair, "zh", ahead), lax.ppermute(pair, "zh", behind)
    opposite = [lax.ppermute(from_high[:1], "zh", behind), lax.ppermute(from_low[1:], "zh", ahead)]
    mine = jnp.stack([pair, from_low, jnp.concatenate(opposite), from_high])
    mine, train_all = lax.optimization_barrier((mine, train_all))
    other = lax.ppermute(mine, "core", [(0, 1), (1, 0)])
    where = jnp.stack([lax.axis_index("zh"), lax.axis_index("core")]).astype(jnp.int32)
    rows, cols = train_embed.shape[0] * col_size, valid_embed.shape[0] * row_size
    row_chunks, col_chunks = rows // LANES, cols // LANES
    classes = pair_level.shape[0]
    levels = jnp.pad(pair_level, ((0, LANES - classes), (0, LANES - classes)), constant_values=-1)
    tile = jax.ShapeDtypeStruct((rows, cols), f32)
    row_copies = jax.ShapeDtypeStruct((col_size, row_chunks, LANES), f32)
    col_copies = jax.ShapeDtypeStruct((row_size, col_chunks, LANES), f32)
    row_shape = jax.ShapeDtypeStruct((row_chunks, LANES), f32)
    col_shape = jax.ShapeDtypeStruct((col_chunks, LANES), f32)
    tall = [pltpu.VMEM((rows, LANES), f32)] * 2
    wide = [pltpu.VMEM((row_chunks * SUB, cols), f32)] * 2
    prepared = call(
        prepare_kernel,
        (jax.ShapeDtypeStruct((rows, embed + 3 * LANES), jnp.bfloat16), jax.ShapeDtypeStruct((rows, LANES), f32)),
        [],
        train_all,
        levels,
        level_cost,
        smem=(2,),
        num_levels=level_cost.shape[0],
        limit=16,
    )
    cost, row_part, col_part = call(
        start_kernel,
        (tile, row_copies, col_copies),
        tall + wide,
        where,
        *prepared,
        mine,
        other,
        smem=(0,),
        limit=16,
    )
    full_rows, full_cols = rows * row_size, cols * col_size
    offsets = {"row_offset": math.log2(full_cols), "col_offset": math.log2(full_rows)}
    row_pot = jnp.zeros(row_shape.shape, f32)
    col_pot = jnp.zeros(col_shape.shape, f32)
    for iteration in range(ITERS - 1):
        row_got = exchange(row_part, "col")
        col_got = exchange(col_part, ROW)
        given = (cost, row_got, col_got, row_pot, col_pot)
        if iteration < ITERS - 2:
            row_part, col_part, row_pot, col_pot = call(
                both_kernel, (row_copies, col_copies, row_shape, col_shape), tall + wide + tall[:1], *given, **offsets
            )
        else:
            row_part, row_pot = call(last_row_kernel, (row_copies, row_shape), tall, *given, **offsets)
    row_got = exchange(row_part, "col")
    final_shape = jax.ShapeDtypeStruct((row_size, row_chunks, LANES), f32)
    final, copies = call(
        last_kernel, (row_shape, final_shape), [], row_got, row_pot, offset=offsets["row_offset"]
    )
    (out,) = call(calibrate_kernel, (row_shape,), [], exchange(copies, ROW), final, count=full_rows)
    return out.reshape(rows)


def solution(mesh):
    row_size, col_size = mesh.shape["row"], mesh.shape["col"]
    finer = jax.sharding.Mesh(mesh.devices.reshape(row_size // 4, 2, 2, col_size), ROW + ("col",))
    both = ROW + ("col",)
    placed = (P(both, None), P(both, None), P(both), P(both), P(), P())
    return jax.shard_map(shards, mesh=finer, in_specs=placed, out_specs=P(ROW), check_vma=False)
```

```python
import math

import jax
import jax.numpy as jnp
from jax import lax
from jax.experimental import pallas as pl
from jax.experimental.pallas import tpu as pltpu
from jax.sharding import PartitionSpec as P

ITERS = 4
LANES = 128
SUB = 8

entropy_scale = 0.05
UNIT = entropy_scale * math.log(2.0)

ROW = ("zh", "zl", "core")

VMEM = pl.BlockSpec(memory_space=pltpu.VMEM)


def lse_lead(parts):
    high = jnp.max(parts, axis=0)
    return high + jnp.log2(jnp.sum(jnp.exp2(parts - high[None]), axis=0))


def merge(high, total):
    top = jnp.max(high, axis=0, keepdims=True)
    return top + jnp.log2(jnp.sum(total * jnp.exp2(high - top), axis=0, keepdims=True))


def spread_rows(values, out_ref):
    for a in range(values.shape[0]):
        block = jnp.broadcast_to(values[a : a + 1, :], (LANES, LANES))
        out_ref[a * LANES : (a + 1) * LANES, :] = block.T


def peak_and_sum(tiles):
    high = tiles[0]
    for tile in tiles[1:]:
        high = jnp.maximum(high, tile)
    total = jnp.exp2(tiles[0] - high)
    for tile in tiles[1:]:
        total = total + jnp.exp2(tile - high)
    return high, total


def col_partial(cost_ref, row_ref, high_ref, total_ref):
    rows, cols = cost_ref.shape
    blocks, chunks = rows // LANES, cols // LANES
    groups = LANES // SUB

    def block_step(q, carry):
        start = pl.multiple_of(q * LANES, LANES)
        bases = None if row_ref is None else [row_ref[pl.ds(start + g * SUB, SUB), :] for g in range(groups)]
        for k in range(chunks):
            cells = [cost_ref[pl.ds(start + g * SUB, SUB), k * LANES : (k + 1) * LANES] for g in range(groups)]
            tiles = [-cell for cell in cells] if bases is None else [base - cell for base, cell in zip(bases, cells)]
            high, total = peak_and_sum(tiles)
            here = (pl.ds(pl.multiple_of(q * SUB, SUB), SUB), slice(k * LANES, (k + 1) * LANES))
            high_ref[here] = high
            total_ref[here] = total
        return carry

    lax.fori_loop(0, blocks, block_step, 0)
    out = [merge(high_ref[:, k * LANES : (k + 1) * LANES], total_ref[:, k * LANES : (k + 1) * LANES]) for k in range(chunks)]
    return jnp.concatenate(out, axis=0)


def row_partial(cost_ref, col, high_ref, total_ref):
    rows, cols = cost_ref.shape
    chunks = cols // LANES
    bases = None if col is None else [jnp.broadcast_to(col[k : k + 1, :], (SUB, LANES)) for k in range(chunks)]

    def group_step(g, carry):
        here = pl.ds(pl.multiple_of(g * SUB, SUB), SUB)
        cells = [cost_ref[here, k * LANES : (k + 1) * LANES] for k in range(chunks)]
        tiles = [-cell for cell in cells] if bases is None else [base - cell for base, cell in zip(bases, cells)]
        high_ref[here, :], total_ref[here, :] = peak_and_sum(tiles)
        return carry

    lax.fori_loop(0, rows // SUB, group_step, 0, unroll=4)
    out = []
    for a in range(rows // LANES):
        block = slice(a * LANES, (a + 1) * LANES)
        out.append(merge(high_ref[block, :].T, total_ref[block, :].T))
    return jnp.concatenate(out, axis=0)


def split3(values):
    high = values.astype(jnp.bfloat16)
    rest = values - high.astype(jnp.float32)
    mid = rest.astype(jnp.bfloat16)
    low = (rest - mid.astype(jnp.float32)).astype(jnp.bfloat16)
    return high, mid, low


def dot(left, right, dims):
    return lax.dot_general(left, right, (dims, ((), ())), preferred_element_type=jnp.float32)


def pack_kernel(
    train_label_hbm, train_hbm, valid_hbm, valid_label_hbm, train_out, valid_out,
    train_label_ref, train_ref, valid_label_ref, sems
):
    count, embed = train_hbm.shape
    points = valid_hbm.shape[0]
    pairs = (
        (train_label_hbm, train_label_ref),
        (train_hbm, train_ref),
        (valid_label_hbm, valid_label_ref),
        (valid_hbm, valid_out.at[:points, :]),
    )
    copies = [pltpu.make_async_copy(source, target, sems.at[i]) for i, (source, target) in enumerate(pairs)]
    for copy in copies:
        copy.start()
    for copy in copies:
        copy.wait()
    row_ids = lax.broadcasted_iota(jnp.int32, (count, LANES), 0)
    shown = jnp.zeros((count, LANES), jnp.int32)
    for i in range(count):
        shown = jnp.where(row_ids == i, train_label_ref[i], shown)
    packed = jnp.concatenate([train_ref[...], shown.astype(jnp.float32).astype(jnp.bfloat16)], axis=1)
    train_out[...] = jnp.broadcast_to(packed[None], train_out.shape)
    row = jnp.broadcast_to(valid_label_ref[...].astype(jnp.float32), (valid_out.shape[0] - points, LANES))
    valid_out[points:, :] = jnp.concatenate([row] * (embed // LANES), axis=1).astype(jnp.bfloat16)


def start_kernel(
    where_ref, train_ref, table_ref, mine_ref, other_ref, cost_ref, row_out, col_out, left_ref, row_a, row_b, col_a, col_b
):
    steps, sides, block_rows, embed = mine_ref.shape
    packed = train_ref[...].reshape(cost_ref.shape[0], embed + LANES)
    train = packed[:, :embed]
    wide = train.astype(jnp.float32)
    train_sq = jnp.sum(wide * wide, axis=1, keepdims=True) * (1.0 / embed)
    labels = packed[:, embed:].astype(jnp.float32)
    lane_ids = lax.broadcasted_iota(jnp.int32, labels.shape, 1).astype(jnp.float32)
    train_hot = jnp.where(labels == lane_ids, 1.0, 0.0).astype(jnp.bfloat16)
    parts = [dot(train_hot, part, ((1,), (0,))).astype(jnp.bfloat16) for part in split3(table_ref[...])]
    table_parts = len(parts)
    left_ref[...] = jnp.concatenate([train * jnp.bfloat16(-2.0 / embed), *parts], axis=1)
    ones = jnp.ones((SUB, embed), jnp.bfloat16)
    class_ids = lax.broadcasted_iota(jnp.int32, (LANES, LANES), 0).astype(jnp.float32)
    step = sides * LANES
    for pair in range(2 * steps):
        core, z_pair = divmod(pair, steps)
        back = lax.rem(where_ref[0] - z_pair + steps, steps)
        own = where_ref[1] == core
        blocks = [jnp.where(own, mine_ref[back, side], other_ref[back, side]) for side in range(sides)]
        block = jnp.concatenate([b[:LANES, :] for b in blocks], axis=0)
        label_rows = [b[LANES:, :LANES].astype(jnp.float32)[:1, :] for b in blocks]
        hots = [jnp.where(class_ids == label_row, 1.0, 0.0).astype(jnp.bfloat16) for label_row in label_rows]
        hot = jnp.concatenate(hots, axis=1)
        wide = block.astype(jnp.float32)
        squares = wide * wide
        sq_high = squares.astype(jnp.bfloat16)
        sq_low = (squares - sq_high.astype(jnp.float32)).astype(jnp.bfloat16)
        block_sq = (dot(ones, sq_high, ((1,), (1,))) + dot(ones, sq_low, ((1,), (1,))))[:1, :]
        cost = dot(left_ref[:, :embed], block, ((1,), (1,)))
        cost = cost + dot(left_ref[:, embed:], jnp.concatenate([hot] * table_parts, axis=0), ((1,), (0,)))
        here = slice(pair * step, (pair + 1) * step)
        cost_ref[:, here] = (cost + (train_sq + block_sq * (1.0 / embed))) * (1.0 / UNIT)
    row_out[...] = jnp.broadcast_to(row_partial(cost_ref, None, row_a, row_b)[None], row_out.shape)
    col_out[...] = jnp.broadcast_to(col_partial(cost_ref, None, col_a, col_b)[None], col_out.shape)


def updated(pot_ref, parts_ref, offset):
    return 0.5 * (pot_ref[...] + (offset - lse_lead(parts_ref[...])))


def both_kernel(
    cost_ref, row_parts, col_parts, row_pot, col_pot, row_out, col_out, row_new, col_new, row_a, row_b, col_a, col_b,
    spread_ref, *, row_offset, col_offset
):
    row, col = updated(row_pot, row_parts, row_offset), updated(col_pot, col_parts, col_offset)
    row_new[...] = row
    col_new[...] = col
    spread_rows(row, spread_ref)
    row_out[...] = jnp.broadcast_to(row_partial(cost_ref, col, row_a, row_b)[None], row_out.shape)
    col_out[...] = jnp.broadcast_to(col_partial(cost_ref, spread_ref, col_a, col_b)[None], col_out.shape)


def last_row_kernel(
    cost_ref, row_parts, col_parts, row_pot, col_pot, row_out, row_new, row_a, row_b, *, row_offset, col_offset
):
    row_new[...] = updated(row_pot, row_parts, row_offset)
    col = updated(col_pot, col_parts, col_offset)
    row_out[...] = jnp.broadcast_to(row_partial(cost_ref, col, row_a, row_b)[None], row_out.shape)


def last_kernel(parts_ref, pot_ref, out_ref, copies_ref, *, offset):
    pot = updated(pot_ref, parts_ref, offset)
    out_ref[...] = pot
    copies_ref[...] = jnp.broadcast_to(pot[None], copies_ref.shape)


def calibrate_kernel(parts_ref, pot_ref, out_ref, *, count):
    total = jnp.sum(jnp.sum(parts_ref[...], axis=0), keepdims=True)
    out_ref[...] = (pot_ref[...] * count - total) * (UNIT / (count - 1))


def exchange(block, axis):
    copies = block if block.ndim == 3 else jnp.broadcast_to(block[None], (lax.axis_size(axis),) + block.shape)
    return lax.all_to_all(copies, axis, 0, 0, tiled=True)


def call(kernel, out_shape, scratch, *args, smem=(), hbm=(), limit=8, **static):
    body = kernel if not static else (lambda *refs: kernel(*refs, **static))
    smem_spec, hbm_spec = pl.BlockSpec(memory_space=pltpu.SMEM), pl.BlockSpec(memory_space=pl.ANY)
    specs = [smem_spec if i in smem else hbm_spec if i in hbm else VMEM for i in range(len(args))]
    return pl.pallas_call(
        body,
        out_shape=out_shape,
        in_specs=specs,
        out_specs=[VMEM] * len(out_shape),
        scratch_shapes=scratch,
        compiler_params=pltpu.CompilerParams(vmem_limit_bytes=limit * 2**20),
        cost_estimate=pl.CostEstimate(flops=2**24, bytes_accessed=4 * 2**20, transcendentals=2**20),
    )(*args)


def shards(train_embed, valid_embed, train_labels, valid_labels, pair_level, level_cost):
    row_size, col_size = lax.axis_size(ROW), lax.axis_size("col")
    f32 = jnp.float32
    embed = train_embed.shape[1]
    train_copies, valid_pack = call(
        pack_kernel,
        (
            jax.ShapeDtypeStruct((col_size, train_embed.shape[0], embed + LANES), jnp.bfloat16),
            jax.ShapeDtypeStruct((valid_embed.shape[0] + 16, embed), jnp.bfloat16),
        ),
        [
            pltpu.SMEM(train_labels.shape, jnp.int32),
            pltpu.VMEM(train_embed.shape, train_embed.dtype),
            pltpu.VMEM((1,) + valid_labels.shape, jnp.int32),
            pltpu.SemaphoreType.DMA((4,)),
        ],
        train_labels,
        train_embed,
        valid_embed,
        valid_labels[None, :],
        hbm=(0, 1, 2, 3),
        limit=60,
    )
    train_all = exchange(train_copies, "col")
    pair = lax.all_gather(valid_pack, "zl", axis=0)
    steps = lax.axis_size("zh")
    turn = [[(i, (i + k) % steps) for i in range(steps)] for k in range(steps)]
    mine = jnp.stack([pair] + [lax.ppermute(pair, "zh", turn[k]) for k in range(1, steps)])
    other = lax.ppermute(mine, "core", [(0, 1), (1, 0)])
    where = jnp.stack([lax.axis_index("zh"), lax.axis_index("core")]).astype(jnp.int32)
    rows, cols = train_embed.shape[0] * col_size, valid_embed.shape[0] * row_size
    row_chunks, col_chunks = rows // LANES, cols // LANES
    classes = pair_level.shape[0]
    level_ids = jnp.arange(level_cost.shape[0], dtype=jnp.int32)
    chosen = (pair_level[:, :, None] == level_ids).astype(f32)
    table = jnp.pad(jnp.sum(chosen * level_cost, axis=2), ((0, LANES - classes), (0, LANES - classes)))
    tile = jax.ShapeDtypeStruct((rows, cols), f32)
    row_copies = jax.ShapeDtypeStruct((col_size, row_chunks, LANES), f32)
    col_copies = jax.ShapeDtypeStruct((row_size, col_chunks, LANES), f32)
    row_shape = jax.ShapeDtypeStruct((row_chunks, LANES), f32)
    col_shape = jax.ShapeDtypeStruct((col_chunks, LANES), f32)
    tall = [pltpu.VMEM((rows, LANES), f32)] * 2
    wide = [pltpu.VMEM((row_chunks * SUB, cols), f32)] * 2
    cost, row_part, col_part = call(
        start_kernel,
        (tile, row_copies, col_copies),
        [pltpu.VMEM((rows, embed + 3 * LANES), jnp.bfloat16)] + tall + wide,
        where,
        train_all,
        table,
        mine,
        other,
        smem=(0,),
        limit=16,
    )
    full_rows, full_cols = rows * row_size, cols * col_size
    offsets = {"row_offset": math.log2(full_cols), "col_offset": math.log2(full_rows)}
    row_pot = jnp.zeros(row_shape.shape, f32)
    col_pot = jnp.zeros(col_shape.shape, f32)
    for iteration in range(ITERS - 1):
        row_got = exchange(row_part, "col")
        col_got = exchange(col_part, ROW)
        given = (cost, row_got, col_got, row_pot, col_pot)
        if iteration < ITERS - 2:
            row_part, col_part, row_pot, col_pot = call(
                both_kernel, (row_copies, col_copies, row_shape, col_shape), tall + wide + tall[:1], *given, **offsets
            )
        else:
            row_part, row_pot = call(last_row_kernel, (row_copies, row_shape), tall, *given, **offsets)
    row_got = exchange(row_part, "col")
    final_shape = jax.ShapeDtypeStruct((row_size, row_chunks, LANES), f32)
    final, copies = call(
        last_kernel, (row_shape, final_shape), [], row_got, row_pot, offset=offsets["row_offset"]
    )
    (out,) = call(calibrate_kernel, (row_shape,), [], exchange(copies, ROW), final, count=full_rows)
    return out.reshape(rows)


def solution(mesh):
    row_size, col_size = mesh.shape["row"], mesh.shape["col"]
    finer = jax.sharding.Mesh(mesh.devices.reshape(row_size // 4, 2, 2, col_size), ROW + ("col",))
    both = ROW + ("col",)
    placed = (P(both, None), P(both, None), P(both), P(both), P(), P())
    return jax.shard_map(shards, mesh=finer, in_specs=placed, out_specs=P(ROW), check_vma=False)
```

```python
import math

import jax
import jax.numpy as jnp
from jax import lax
from jax.experimental import pallas as pl
from jax.experimental.pallas import tpu as pltpu
from jax.sharding import PartitionSpec as P

ITERS = 4
LANES = 128
SUB = 8

entropy_scale = 0.05
UNIT = entropy_scale * math.log(2.0)

ROW = ("zh", "zl", "core")

VMEM = pl.BlockSpec(memory_space=pltpu.VMEM)


def lse_lead(parts):
    high = jnp.max(parts, axis=0)
    return high + jnp.log2(jnp.sum(jnp.exp2(parts - high[None]), axis=0))


def merge(high, total):
    top = jnp.max(high, axis=0, keepdims=True)
    return top + jnp.log2(jnp.sum(total * jnp.exp2(high - top), axis=0, keepdims=True))


def spread_rows(values, out_ref):
    for a in range(values.shape[0]):
        block = jnp.broadcast_to(values[a : a + 1, :], (LANES, LANES))
        out_ref[a * LANES : (a + 1) * LANES, :] = block.T


def peak_and_sum(tiles):
    high = tiles[0]
    for tile in tiles[1:]:
        high = jnp.maximum(high, tile)
    total = jnp.exp2(tiles[0] - high)
    for tile in tiles[1:]:
        total = total + jnp.exp2(tile - high)
    return high, total


def col_partial(cost_ref, row_ref, high_ref, total_ref):
    rows, cols = cost_ref.shape
    blocks, chunks = rows // LANES, cols // LANES
    groups = LANES // SUB

    def block_step(q, carry):
        start = pl.multiple_of(q * LANES, LANES)
        bases = None if row_ref is None else [row_ref[pl.ds(start + g * SUB, SUB), :] for g in range(groups)]
        for k in range(chunks):
            cells = [cost_ref[pl.ds(start + g * SUB, SUB), k * LANES : (k + 1) * LANES] for g in range(groups)]
            tiles = [-cell for cell in cells] if bases is None else [base - cell for base, cell in zip(bases, cells)]
            high, total = peak_and_sum(tiles)
            here = (pl.ds(pl.multiple_of(q * SUB, SUB), SUB), slice(k * LANES, (k + 1) * LANES))
            high_ref[here] = high
            total_ref[here] = total
        return carry

    lax.fori_loop(0, blocks, block_step, 0)
    out = [merge(high_ref[:, k * LANES : (k + 1) * LANES], total_ref[:, k * LANES : (k + 1) * LANES]) for k in range(chunks)]
    return jnp.concatenate(out, axis=0)


def row_partial(cost_ref, col, high_ref, total_ref):
    rows, cols = cost_ref.shape
    chunks = cols // LANES
    bases = None if col is None else [jnp.broadcast_to(col[k : k + 1, :], (SUB, LANES)) for k in range(chunks)]

    def group_step(g, carry):
        here = pl.ds(pl.multiple_of(g * SUB, SUB), SUB)
        cells = [cost_ref[here, k * LANES : (k + 1) * LANES] for k in range(chunks)]
        tiles = [-cell for cell in cells] if bases is None else [base - cell for base, cell in zip(bases, cells)]
        high_ref[here, :], total_ref[here, :] = peak_and_sum(tiles)
        return carry

    lax.fori_loop(0, rows // SUB, group_step, 0, unroll=4)
    out = []
    for a in range(rows // LANES):
        block = slice(a * LANES, (a + 1) * LANES)
        out.append(merge(high_ref[block, :].T, total_ref[block, :].T))
    return jnp.concatenate(out, axis=0)


def split3(values):
    high = values.astype(jnp.bfloat16)
    rest = values - high.astype(jnp.float32)
    mid = rest.astype(jnp.bfloat16)
    low = (rest - mid.astype(jnp.float32)).astype(jnp.bfloat16)
    return high, mid, low


def dot(left, right, dims):
    return lax.dot_general(left, right, (dims, ((), ())), preferred_element_type=jnp.float32)


def pack_kernel(
    train_label_hbm, train_hbm, valid_hbm, valid_label_hbm, train_out, valid_out,
    train_label_ref, train_ref, valid_label_ref, sems
):
    count, embed = train_hbm.shape
    points = valid_hbm.shape[0]
    pairs = (
        (train_label_hbm, train_label_ref),
        (train_hbm, train_ref),
        (valid_label_hbm, valid_label_ref),
        (valid_hbm, valid_out.at[:points, :]),
    )
    copies = [pltpu.make_async_copy(source, target, sems.at[i]) for i, (source, target) in enumerate(pairs)]
    for copy in copies:
        copy.start()
    for copy in copies:
        copy.wait()
    row_ids = lax.broadcasted_iota(jnp.int32, (count, LANES), 0)
    shown = jnp.zeros((count, LANES), jnp.int32)
    for i in range(count):
        shown = jnp.where(row_ids == i, train_label_ref[i], shown)
    packed = jnp.concatenate([train_ref[...], shown.astype(jnp.float32).astype(jnp.bfloat16)], axis=1)
    train_out[...] = jnp.broadcast_to(packed[None], train_out.shape)
    row = jnp.broadcast_to(valid_label_ref[...].astype(jnp.float32), (valid_out.shape[0] - points, LANES))
    valid_out[points:, :] = jnp.concatenate([row] * (embed // LANES), axis=1).astype(jnp.bfloat16)


def start_kernel(
    where_ref, train_ref, table_ref, own_ref, core_ref, beside_ref, both_ref, cost_ref, row_out, col_out, left_ref, row_a, row_b, col_a, col_b
):
    steps, _, embed = own_ref.shape
    sides = 2
    packed = train_ref[...].reshape(cost_ref.shape[0], embed + LANES)
    train = packed[:, :embed]
    wide = train.astype(jnp.float32)
    train_sq = jnp.sum(wide * wide, axis=1, keepdims=True) * (1.0 / embed)
    labels = packed[:, embed:].astype(jnp.float32)
    lane_ids = lax.broadcasted_iota(jnp.int32, labels.shape, 1).astype(jnp.float32)
    train_hot = jnp.where(labels == lane_ids, 1.0, 0.0).astype(jnp.bfloat16)
    parts = [dot(train_hot, part, ((1,), (0,))).astype(jnp.bfloat16) for part in split3(table_ref[...])]
    table_parts = len(parts)
    left_ref[...] = jnp.concatenate([train * jnp.bfloat16(-2.0 / embed), *parts], axis=1)
    ones = jnp.ones((SUB, embed), jnp.bfloat16)
    class_ids = lax.broadcasted_iota(jnp.int32, (LANES, LANES), 0).astype(jnp.float32)
    step = sides * LANES
    for pair in range(2 * steps):
        core, z_pair = divmod(pair, steps)
        back = lax.rem(where_ref[0] - z_pair + steps, steps)
        same_core = where_ref[2] == core
        near = jnp.where(same_core, own_ref[back], core_ref[back])
        far = jnp.where(same_core, beside_ref[back], both_ref[back])
        even = where_ref[1] == 0
        blocks = [jnp.where(even, near, far), jnp.where(even, far, near)]
        block = jnp.concatenate([b[:LANES, :] for b in blocks], axis=0)
        label_rows = [b[LANES:, :LANES].astype(jnp.float32)[:1, :] for b in blocks]
        hots = [jnp.where(class_ids == label_row, 1.0, 0.0).astype(jnp.bfloat16) for label_row in label_rows]
        hot = jnp.concatenate(hots, axis=1)
        wide = block.astype(jnp.float32)
        squares = wide * wide
        sq_high = squares.astype(jnp.bfloat16)
        sq_low = (squares - sq_high.astype(jnp.float32)).astype(jnp.bfloat16)
        block_sq = (dot(ones, sq_high, ((1,), (1,))) + dot(ones, sq_low, ((1,), (1,))))[:1, :]
        cost = dot(left_ref[:, :embed], block, ((1,), (1,)))
        cost = cost + dot(left_ref[:, embed:], jnp.concatenate([hot] * table_parts, axis=0), ((1,), (0,)))
        here = slice(pair * step, (pair + 1) * step)
        cost_ref[:, here] = (cost + (train_sq + block_sq * (1.0 / embed))) * (1.0 / UNIT)
    row_out[...] = jnp.broadcast_to(row_partial(cost_ref, None, row_a, row_b)[None], row_out.shape)
    col_out[...] = jnp.broadcast_to(col_partial(cost_ref, None, col_a, col_b)[None], col_out.shape)


def updated(pot_ref, parts_ref, offset):
    return 0.5 * (pot_ref[...] + (offset - lse_lead(parts_ref[...])))


def both_kernel(
    cost_ref, row_parts, col_parts, row_pot, col_pot, row_out, col_out, row_new, col_new, row_a, row_b, col_a, col_b,
    spread_ref, *, row_offset, col_offset
):
    row, col = updated(row_pot, row_parts, row_offset), updated(col_pot, col_parts, col_offset)
    row_new[...] = row
    col_new[...] = col
    spread_rows(row, spread_ref)
    row_out[...] = jnp.broadcast_to(row_partial(cost_ref, col, row_a, row_b)[None], row_out.shape)
    col_out[...] = jnp.broadcast_to(col_partial(cost_ref, spread_ref, col_a, col_b)[None], col_out.shape)


def last_row_kernel(
    cost_ref, row_parts, col_parts, row_pot, col_pot, row_out, row_new, row_a, row_b, *, row_offset, col_offset
):
    row_new[...] = updated(row_pot, row_parts, row_offset)
    col = updated(col_pot, col_parts, col_offset)
    row_out[...] = jnp.broadcast_to(row_partial(cost_ref, col, row_a, row_b)[None], row_out.shape)


def last_kernel(parts_ref, pot_ref, out_ref, copies_ref, *, offset):
    pot = updated(pot_ref, parts_ref, offset)
    out_ref[...] = pot
    copies_ref[...] = jnp.broadcast_to(pot[None], copies_ref.shape)


def calibrate_kernel(parts_ref, pot_ref, out_ref, *, count):
    total = jnp.sum(jnp.sum(parts_ref[...], axis=0), keepdims=True)
    out_ref[...] = (pot_ref[...] * count - total) * (UNIT / (count - 1))


def exchange(block, axis):
    copies = block if block.ndim == 3 else jnp.broadcast_to(block[None], (lax.axis_size(axis),) + block.shape)
    return lax.all_to_all(copies, axis, 0, 0, tiled=True)


def call(kernel, out_shape, scratch, *args, smem=(), hbm=(), limit=8, **static):
    body = kernel if not static else (lambda *refs: kernel(*refs, **static))
    smem_spec, hbm_spec = pl.BlockSpec(memory_space=pltpu.SMEM), pl.BlockSpec(memory_space=pl.ANY)
    specs = [smem_spec if i in smem else hbm_spec if i in hbm else VMEM for i in range(len(args))]
    return pl.pallas_call(
        body,
        out_shape=out_shape,
        in_specs=specs,
        out_specs=[VMEM] * len(out_shape),
        scratch_shapes=scratch,
        compiler_params=pltpu.CompilerParams(vmem_limit_bytes=limit * 2**20),
        cost_estimate=pl.CostEstimate(flops=2**24, bytes_accessed=4 * 2**20, transcendentals=2**20),
    )(*args)


def shards(train_embed, valid_embed, train_labels, valid_labels, pair_level, level_cost):
    row_size, col_size = lax.axis_size(ROW), lax.axis_size("col")
    f32 = jnp.float32
    embed = train_embed.shape[1]
    train_copies, valid_pack = call(
        pack_kernel,
        (
            jax.ShapeDtypeStruct((col_size, train_embed.shape[0], embed + LANES), jnp.bfloat16),
            jax.ShapeDtypeStruct((valid_embed.shape[0] + 16, embed), jnp.bfloat16),
        ),
        [
            pltpu.SMEM(train_labels.shape, jnp.int32),
            pltpu.VMEM(train_embed.shape, train_embed.dtype),
            pltpu.VMEM((1,) + valid_labels.shape, jnp.int32),
            pltpu.SemaphoreType.DMA((4,)),
        ],
        train_labels,
        train_embed,
        valid_embed,
        valid_labels[None, :],
        hbm=(0, 1, 2, 3),
        limit=60,
    )
    train_all = exchange(train_copies, "col")
    steps = lax.axis_size("zh")
    turn = [[(i, (i + k) % steps) for i in range(steps)] for k in range(steps)]
    swap = [(0, 1), (1, 0)]
    own = jnp.stack([valid_pack] + [lax.ppermute(valid_pack, "zh", turn[k]) for k in range(1, steps)])
    beside = lax.ppermute(own, "zl", swap)
    valid_all = (own, lax.ppermute(own, "core", swap), beside, lax.ppermute(beside, "core", swap))
    where = jnp.stack([lax.axis_index(axis) for axis in ROW]).astype(jnp.int32)
    rows, cols = train_embed.shape[0] * col_size, valid_embed.shape[0] * row_size
    row_chunks, col_chunks = rows // LANES, cols // LANES
    classes = pair_level.shape[0]
    level_ids = jnp.arange(level_cost.shape[0], dtype=jnp.int32)
    chosen = (pair_level[:, :, None] == level_ids).astype(f32)
    table = jnp.pad(jnp.sum(chosen * level_cost, axis=2), ((0, LANES - classes), (0, LANES - classes)))
    tile = jax.ShapeDtypeStruct((rows, cols), f32)
    row_copies = jax.ShapeDtypeStruct((col_size, row_chunks, LANES), f32)
    col_copies = jax.ShapeDtypeStruct((row_size, col_chunks, LANES), f32)
    row_shape = jax.ShapeDtypeStruct((row_chunks, LANES), f32)
    col_shape = jax.ShapeDtypeStruct((col_chunks, LANES), f32)
    tall = [pltpu.VMEM((rows, LANES), f32)] * 2
    wide = [pltpu.VMEM((row_chunks * SUB, cols), f32)] * 2
    cost, row_part, col_part = call(
        start_kernel,
        (tile, row_copies, col_copies),
        [pltpu.VMEM((rows, embed + 3 * LANES), jnp.bfloat16)] + tall + wide,
        where,
        train_all,
        table,
        *valid_all,
        smem=(0,),
        limit=16,
    )
    full_rows, full_cols = rows * row_size, cols * col_size
    offsets = {"row_offset": math.log2(full_cols), "col_offset": math.log2(full_rows)}
    row_pot = jnp.zeros(row_shape.shape, f32)
    col_pot = jnp.zeros(col_shape.shape, f32)
    for iteration in range(ITERS - 1):
        row_got = exchange(row_part, "col")
        col_got = exchange(col_part, ROW)
        given = (cost, row_got, col_got, row_pot, col_pot)
        if iteration < ITERS - 2:
            row_part, col_part, row_pot, col_pot = call(
                both_kernel, (row_copies, col_copies, row_shape, col_shape), tall + wide + tall[:1], *given, **offsets
            )
        else:
            row_part, row_pot = call(last_row_kernel, (row_copies, row_shape), tall, *given, **offsets)
    row_got = exchange(row_part, "col")
    final_shape = jax.ShapeDtypeStruct((row_size, row_chunks, LANES), f32)
    final, copies = call(
        last_kernel, (row_shape, final_shape), [], row_got, row_pot, offset=offsets["row_offset"]
    )
    (out,) = call(calibrate_kernel, (row_shape,), [], exchange(copies, ROW), final, count=full_rows)
    return out.reshape(rows)


def solution(mesh):
    row_size, col_size = mesh.shape["row"], mesh.shape["col"]
    finer = jax.sharding.Mesh(mesh.devices.reshape(row_size // 4, 2, 2, col_size), ROW + ("col",))
    both = ROW + ("col",)
    placed = (P(both, None), P(both, None), P(both), P(both), P(), P())
    return jax.shard_map(shards, mesh=finer, in_specs=placed, out_specs=P(ROW), check_vma=False)
```

```python
import math

import jax
import jax.numpy as jnp
from jax import lax
from jax.experimental import pallas as pl
from jax.experimental.pallas import tpu as pltpu
from jax.sharding import PartitionSpec as P

ITERS = 4
LANES = 128
SUB = 8

entropy_scale = 0.05
UNIT = entropy_scale * math.log(2.0)

ROW = ("zh", "zl", "core")
COL = ("y", "x")

VMEM = pl.BlockSpec(memory_space=pltpu.VMEM)


def lse_lead(parts):
    high = jnp.max(parts, axis=0)
    return high + jnp.log2(jnp.sum(jnp.exp2(parts - high[None]), axis=0))


def merge(high, total):
    top = jnp.max(high, axis=0, keepdims=True)
    return top + jnp.log2(jnp.sum(total * jnp.exp2(high - top), axis=0, keepdims=True))


def spread_rows(values, out_ref):
    for a in range(values.shape[0]):
        block = jnp.broadcast_to(values[a : a + 1, :], (LANES, LANES))
        out_ref[a * LANES : (a + 1) * LANES, :] = block.T


def peak_and_sum(tiles):
    high = tiles[0]
    for tile in tiles[1:]:
        high = jnp.maximum(high, tile)
    total = jnp.exp2(tiles[0] - high)
    for tile in tiles[1:]:
        total = total + jnp.exp2(tile - high)
    return high, total


def col_partial(cost_ref, row_ref, high_ref, total_ref):
    rows, cols = cost_ref.shape
    blocks, chunks = rows // LANES, cols // LANES
    groups = LANES // SUB

    def block_step(q, carry):
        start = pl.multiple_of(q * LANES, LANES)
        bases = None if row_ref is None else [row_ref[pl.ds(start + g * SUB, SUB), :] for g in range(groups)]
        for k in range(chunks):
            cells = [cost_ref[pl.ds(start + g * SUB, SUB), k * LANES : (k + 1) * LANES] for g in range(groups)]
            tiles = [-cell for cell in cells] if bases is None else [base - cell for base, cell in zip(bases, cells)]
            high, total = peak_and_sum(tiles)
            here = (pl.ds(pl.multiple_of(q * SUB, SUB), SUB), slice(k * LANES, (k + 1) * LANES))
            high_ref[here] = high
            total_ref[here] = total
        return carry

    lax.fori_loop(0, blocks, block_step, 0)
    out = [merge(high_ref[:, k * LANES : (k + 1) * LANES], total_ref[:, k * LANES : (k + 1) * LANES]) for k in range(chunks)]
    return jnp.concatenate(out, axis=0)


def row_partial(cost_ref, col, high_ref, total_ref):
    rows, cols = cost_ref.shape
    chunks = cols // LANES
    bases = None if col is None else [jnp.broadcast_to(col[k : k + 1, :], (SUB, LANES)) for k in range(chunks)]

    def group_step(g, carry):
        here = pl.ds(pl.multiple_of(g * SUB, SUB), SUB)
        cells = [cost_ref[here, k * LANES : (k + 1) * LANES] for k in range(chunks)]
        tiles = [-cell for cell in cells] if bases is None else [base - cell for base, cell in zip(bases, cells)]
        high_ref[here, :], total_ref[here, :] = peak_and_sum(tiles)
        return carry

    lax.fori_loop(0, rows // SUB, group_step, 0, unroll=4)
    out = []
    for a in range(rows // LANES):
        block = slice(a * LANES, (a + 1) * LANES)
        out.append(merge(high_ref[block, :].T, total_ref[block, :].T))
    return jnp.concatenate(out, axis=0)


def split3(values):
    high = values.astype(jnp.bfloat16)
    rest = values - high.astype(jnp.float32)
    mid = rest.astype(jnp.bfloat16)
    low = (rest - mid.astype(jnp.float32)).astype(jnp.bfloat16)
    return high, mid, low


def dot(left, right, dims):
    return lax.dot_general(left, right, (dims, ((), ())), preferred_element_type=jnp.float32)


def pack_kernel(
    train_label_hbm, train_hbm, valid_hbm, valid_label_hbm, train_out, valid_out,
    train_label_ref, train_ref, valid_label_ref, sems
):
    count, embed = train_hbm.shape
    points = valid_hbm.shape[0]
    pairs = (
        (train_label_hbm, train_label_ref),
        (train_hbm, train_ref),
        (valid_label_hbm, valid_label_ref),
        (valid_hbm, valid_out.at[:points, :]),
    )
    copies = [pltpu.make_async_copy(source, target, sems.at[i]) for i, (source, target) in enumerate(pairs)]
    for copy in copies:
        copy.start()
    for copy in copies:
        copy.wait()
    row_ids = lax.broadcasted_iota(jnp.int32, (count, LANES), 0)
    shown = jnp.zeros((count, LANES), jnp.int32)
    for i in range(count):
        shown = jnp.where(row_ids == i, train_label_ref[i], shown)
    packed = jnp.concatenate([train_ref[...], shown.astype(jnp.float32).astype(jnp.bfloat16)], axis=1)
    train_out[...] = jnp.broadcast_to(packed[None], train_out.shape)
    row = jnp.broadcast_to(valid_label_ref[...].astype(jnp.float32), (valid_out.shape[0] - points, LANES))
    valid_out[points:, :] = jnp.concatenate([row] * (embed // LANES), axis=1).astype(jnp.bfloat16)


def start_kernel(
    where_ref, train_ref, table_ref, mine_ref, other_ref, cost_ref, partial_ref, left_ref, row_a, row_b, col_a, col_b
):
    steps, sides, block_rows, embed = mine_ref.shape
    packed = train_ref[...].reshape(cost_ref.shape[0], embed + LANES)
    train = packed[:, :embed]
    wide = train.astype(jnp.float32)
    train_sq = jnp.sum(wide * wide, axis=1, keepdims=True) * (1.0 / embed)
    labels = packed[:, embed:].astype(jnp.float32)
    lane_ids = lax.broadcasted_iota(jnp.int32, labels.shape, 1).astype(jnp.float32)
    train_hot = jnp.where(labels == lane_ids, 1.0, 0.0).astype(jnp.bfloat16)
    parts = [dot(train_hot, part, ((1,), (0,))).astype(jnp.bfloat16) for part in split3(table_ref[...])]
    table_parts = len(parts)
    left_ref[...] = jnp.concatenate([train * jnp.bfloat16(-2.0 / embed), *parts], axis=1)
    ones = jnp.ones((SUB, embed), jnp.bfloat16)
    class_ids = lax.broadcasted_iota(jnp.int32, (LANES, LANES), 0).astype(jnp.float32)
    step = sides * LANES
    for pair in range(2 * steps):
        core, z_pair = divmod(pair, steps)
        back = lax.rem(where_ref[0] - z_pair + steps, steps)
        own = where_ref[2] == core
        blocks = [jnp.where(own, mine_ref[back, side], other_ref[back, side]) for side in range(sides)]
        block = jnp.concatenate([b[:LANES, :] for b in blocks], axis=0)
        label_rows = [b[LANES:, :LANES].astype(jnp.float32)[:1, :] for b in blocks]
        hots = [jnp.where(class_ids == label_row, 1.0, 0.0).astype(jnp.bfloat16) for label_row in label_rows]
        hot = jnp.concatenate(hots, axis=1)
        wide = block.astype(jnp.float32)
        squares = wide * wide
        sq_high = squares.astype(jnp.bfloat16)
        sq_low = (squares - sq_high.astype(jnp.float32)).astype(jnp.bfloat16)
        block_sq = (dot(ones, sq_high, ((1,), (1,))) + dot(ones, sq_low, ((1,), (1,))))[:1, :]
        cost = dot(left_ref[:, :embed], block, ((1,), (1,)))
        cost = cost + dot(left_ref[:, embed:], jnp.concatenate([hot] * table_parts, axis=0), ((1,), (0,)))
        here = slice(pair * step, (pair + 1) * step)
        cost_ref[:, here] = (cost + (train_sq + block_sq * (1.0 / embed))) * (1.0 / UNIT)
    put_partials(partial_ref, row_partial(cost_ref, None, row_a, row_b), col_partial(cost_ref, None, col_a, col_b))


def put_partials(out_ref, row, col):
    unused = jnp.zeros((out_ref.shape[0] - col.shape[0] - row.shape[0], LANES), jnp.float32)
    out_ref[...] = jnp.concatenate([col, row, unused], axis=0)


def share_kernel(where_ref, partials_ref, out_ref, *, row_chunks):
    _, chunks, _ = out_ref.shape
    rows = [partials_ref[core, chunks : chunks + row_chunks, :] for core in range(2)]
    unused = jnp.zeros((chunks - 2 * row_chunks, LANES), jnp.float32)
    row_side = jnp.concatenate(rows + [unused], axis=0)
    col_side = lse_lead(partials_ref[:, :chunks, :])
    out_ref[...] = jnp.broadcast_to(jnp.where(where_ref[2] == 0, row_side, col_side)[None], out_ref.shape)


def settle_kernel(where_ref, parts_ref, out_ref, *, lines):
    parts = []
    for k in range(parts_ref.shape[0]):
        wanted = jnp.logical_or(where_ref[2] == 0, where_ref[3] == k % lines)
        parts.append(jnp.where(wanted, parts_ref[k], -jnp.inf))
    high = parts[0]
    for part in parts[1:]:
        high = jnp.maximum(high, part)
    total = jnp.exp2(parts[0] - high)
    for part in parts[1:]:
        total = total + jnp.exp2(part - high)
    out_ref[...] = high + jnp.log2(total)


def updated(pot_ref, lse, offset):
    return 0.5 * (pot_ref[...] + (offset - lse))


def both_updated(where_ref, lse_ref, row_pot, col_pot, row_offset, col_offset):
    chunks = row_pot.shape[0]
    rows = jnp.where(where_ref[2] == 0, lse_ref[0, :chunks, :], lse_ref[0, chunks : 2 * chunks, :])
    return updated(row_pot, rows, row_offset), updated(col_pot, lse_ref[1], col_offset)


def both_kernel(
    where_ref, cost_ref, lse_ref, row_pot, col_pot, partial_ref, row_new, col_new, row_a, row_b, col_a, col_b, spread_ref,
    *, row_offset, col_offset
):
    row, col = both_updated(where_ref, lse_ref, row_pot, col_pot, row_offset, col_offset)
    row_new[...] = row
    col_new[...] = col
    spread_rows(row, spread_ref)
    put_partials(
        partial_ref, row_partial(cost_ref, col, row_a, row_b), col_partial(cost_ref, spread_ref, col_a, col_b)
    )


def last_row_kernel(
    where_ref, cost_ref, lse_ref, row_pot, col_pot, row_out, row_new, row_a, row_b, *, row_offset, col_offset
):
    row, col = both_updated(where_ref, lse_ref, row_pot, col_pot, row_offset, col_offset)
    row_new[...] = row
    row_out[...] = jnp.broadcast_to(row_partial(cost_ref, col, row_a, row_b)[None], row_out.shape)


def last_kernel(parts_ref, pot_ref, out_ref, copies_ref, *, offset):
    pot = updated(pot_ref, lse_lead(parts_ref[...]), offset)
    out_ref[...] = pot
    copies_ref[...] = jnp.broadcast_to(pot[None], copies_ref.shape)


def calibrate_kernel(parts_ref, pot_ref, out_ref, *, count):
    total = jnp.sum(jnp.sum(parts_ref[...], axis=0), keepdims=True)
    out_ref[...] = (pot_ref[...] * count - total) * (UNIT / (count - 1))


def exchange(block, axis):
    copies = block if block.ndim == 3 else jnp.broadcast_to(block[None], (lax.axis_size(axis),) + block.shape)
    return lax.all_to_all(copies, axis, 0, 0, tiled=True)


def core_groups():
    z_size, y_size, x_size = lax.axis_size(ROW[:2]), lax.axis_size("y"), lax.axis_size("x")

    def index(z, core, y, x):
        return ((z * 2 + core) * y_size + y) * x_size + x

    ys, xs, zs = range(y_size), range(x_size), range(z_size)
    over_yx = [[index(z, 0, y, x) for y in ys for x in xs] for z in zs]
    over_zx = [[index(z, 1, y, x) for z in zs for x in xs] for y in ys]
    return over_yx + over_zx


def call(kernel, out_shape, scratch, *args, smem=(), hbm=(), limit=8, **static):
    body = kernel if not static else (lambda *refs: kernel(*refs, **static))
    smem_spec, hbm_spec = pl.BlockSpec(memory_space=pltpu.SMEM), pl.BlockSpec(memory_space=pl.ANY)
    specs = [smem_spec if i in smem else hbm_spec if i in hbm else VMEM for i in range(len(args))]
    return pl.pallas_call(
        body,
        out_shape=out_shape,
        in_specs=specs,
        out_specs=[VMEM] * len(out_shape),
        scratch_shapes=scratch,
        compiler_params=pltpu.CompilerParams(vmem_limit_bytes=limit * 2**20),
        cost_estimate=pl.CostEstimate(flops=2**24, bytes_accessed=4 * 2**20, transcendentals=2**20),
    )(*args)


def shards(train_embed, valid_embed, train_labels, valid_labels, pair_level, level_cost):
    row_size, col_size = lax.axis_size(ROW), lax.axis_size(COL)
    f32 = jnp.float32
    embed = train_embed.shape[1]
    train_copies, valid_pack = call(
        pack_kernel,
        (
            jax.ShapeDtypeStruct((col_size, train_embed.shape[0], embed + LANES), jnp.bfloat16),
            jax.ShapeDtypeStruct((valid_embed.shape[0] + 16, embed), jnp.bfloat16),
        ),
        [
            pltpu.SMEM(train_labels.shape, jnp.int32),
            pltpu.VMEM(train_embed.shape, train_embed.dtype),
            pltpu.VMEM((1,) + valid_labels.shape, jnp.int32),
            pltpu.SemaphoreType.DMA((4,)),
        ],
        train_labels,
        train_embed,
        valid_embed,
        valid_labels[None, :],
        hbm=(0, 1, 2, 3),
        limit=60,
    )
    train_all = exchange(train_copies, COL)
    pair = lax.all_gather(valid_pack, "zl", axis=0)
    steps = lax.axis_size("zh")
    turn = [[(i, (i + k) % steps) for i in range(steps)] for k in range(steps)]
    mine = jnp.stack([pair] + [lax.ppermute(pair, "zh", turn[k]) for k in range(1, steps)])
    other = lax.ppermute(mine, "core", [(0, 1), (1, 0)])
    where = jnp.stack([lax.axis_index(axis) for axis in ROW + ("x",)]).astype(jnp.int32)
    rows, cols = train_embed.shape[0] * col_size, valid_embed.shape[0] * row_size
    row_chunks, col_chunks = rows // LANES, cols // LANES
    classes = pair_level.shape[0]
    level_ids = jnp.arange(level_cost.shape[0], dtype=jnp.int32)
    chosen = (pair_level[:, :, None] == level_ids).astype(f32)
    table = jnp.pad(jnp.sum(chosen * level_cost, axis=2), ((0, LANES - classes), (0, LANES - classes)))
    tile = jax.ShapeDtypeStruct((rows, cols), f32)
    row_copies = jax.ShapeDtypeStruct((col_size, row_chunks, LANES), f32)
    part_shape = jax.ShapeDtypeStruct((-(-(row_chunks + col_chunks) // SUB) * SUB, LANES), f32)
    sent_shape = jax.ShapeDtypeStruct((col_size, col_chunks, LANES), f32)
    row_shape = jax.ShapeDtypeStruct((row_chunks, LANES), f32)
    col_shape = jax.ShapeDtypeStruct((col_chunks, LANES), f32)
    tall = [pltpu.VMEM((rows, LANES), f32)] * 2
    wide = [pltpu.VMEM((row_chunks * SUB, cols), f32)] * 2
    cost, partials = call(
        start_kernel,
        (tile, part_shape),
        [pltpu.VMEM((rows, embed + 3 * LANES), jnp.bfloat16)] + tall + wide,
        where,
        train_all,
        table,
        mine,
        other,
        smem=(0,),
        limit=16,
    )
    full_rows, full_cols = rows * row_size, cols * col_size
    offsets = {"row_offset": math.log2(full_cols), "col_offset": math.log2(full_rows)}
    row_pot = jnp.zeros(row_shape.shape, f32)
    col_pot = jnp.zeros(col_shape.shape, f32)
    groups = core_groups()
    for iteration in range(ITERS - 1):
        both_cores = lax.all_gather(partials, "core")
        (sent,) = call(share_kernel, (sent_shape,), [], where, both_cores, smem=(0,), row_chunks=row_chunks)
        got = lax.all_to_all(sent, ROW + COL, 0, 0, tiled=True, axis_index_groups=groups)
        (lse,) = call(settle_kernel, (col_shape,), [], where, got, smem=(0,), lines=lax.axis_size("x"))
        given = (where, cost, lax.all_gather(lse, "core"), row_pot, col_pot)
        if iteration < ITERS - 2:
            partials, row_pot, col_pot = call(
                both_kernel, (part_shape, row_shape, col_shape), tall + wide + tall[:1], *given, smem=(0,), **offsets
            )
        else:
            row_part, row_pot = call(last_row_kernel, (row_copies, row_shape), tall, *given, smem=(0,), **offsets)
    row_got = exchange(row_part, COL)
    final_shape = jax.ShapeDtypeStruct((row_size, row_chunks, LANES), f32)
    final, copies = call(
        last_kernel, (row_shape, final_shape), [], row_got, row_pot, offset=offsets["row_offset"]
    )
    (out,) = call(calibrate_kernel, (row_shape,), [], exchange(copies, ROW), final, count=full_rows)
    return out.reshape(rows)


def solution(mesh):
    row_size, col_size = mesh.shape["row"], mesh.shape["col"]
    finer = jax.sharding.Mesh(mesh.devices.reshape(row_size // 4, 2, 2, col_size // 4, 4), ROW + COL)
    both = ROW + COL
    placed = (P(both, None), P(both, None), P(both), P(both), P(), P())
    return jax.shard_map(shards, mesh=finer, in_specs=placed, out_specs=P(ROW), check_vma=False)
```

```python
import math

import jax
import jax.numpy as jnp
from jax import lax
from jax.experimental import pallas as pl
from jax.experimental.pallas import tpu as pltpu
from jax.sharding import PartitionSpec as P

ITERS = 4
LANES = 128
SUB = 8

entropy_scale = 0.05
UNIT = entropy_scale * math.log(2.0)

ROW = ("zh", "zl", "core")
COL = ("y", "x")

VMEM = pl.BlockSpec(memory_space=pltpu.VMEM)


def lse_lead(parts):
    high = jnp.max(parts, axis=0)
    return high + jnp.log2(jnp.sum(jnp.exp2(parts - high[None]), axis=0))


def merge(high, total):
    top = jnp.max(high, axis=0, keepdims=True)
    return top + jnp.log2(jnp.sum(total * jnp.exp2(high - top), axis=0, keepdims=True))


def spread_rows(values, out_ref):
    for a in range(values.shape[0]):
        block = jnp.broadcast_to(values[a : a + 1, :], (LANES, LANES))
        out_ref[a * LANES : (a + 1) * LANES, :] = block.T


def peak_and_sum(tiles):
    high = tiles[0]
    for tile in tiles[1:]:
        high = jnp.maximum(high, tile)
    total = jnp.exp2(tiles[0] - high)
    for tile in tiles[1:]:
        total = total + jnp.exp2(tile - high)
    return high, total


def col_partial(cost_ref, row_ref, high_ref, total_ref):
    rows, cols = cost_ref.shape
    blocks, chunks = rows // LANES, cols // LANES
    groups = LANES // SUB

    def block_step(q, carry):
        start = pl.multiple_of(q * LANES, LANES)
        bases = None if row_ref is None else [row_ref[pl.ds(start + g * SUB, SUB), :] for g in range(groups)]
        for k in range(chunks):
            cells = [cost_ref[pl.ds(start + g * SUB, SUB), k * LANES : (k + 1) * LANES] for g in range(groups)]
            tiles = [-cell for cell in cells] if bases is None else [base - cell for base, cell in zip(bases, cells)]
            high, total = peak_and_sum(tiles)
            here = (pl.ds(pl.multiple_of(q * SUB, SUB), SUB), slice(k * LANES, (k + 1) * LANES))
            high_ref[here] = high
            total_ref[here] = total
        return carry

    lax.fori_loop(0, blocks, block_step, 0, unroll=True)
    out = [merge(high_ref[:, k * LANES : (k + 1) * LANES], total_ref[:, k * LANES : (k + 1) * LANES]) for k in range(chunks)]
    return jnp.concatenate(out, axis=0)


def row_partial(cost_ref, col, high_ref, total_ref):
    rows, cols = cost_ref.shape
    chunks = cols // LANES
    bases = None if col is None else [jnp.broadcast_to(col[k : k + 1, :], (SUB, LANES)) for k in range(chunks)]

    def group_step(g, carry):
        here = pl.ds(pl.multiple_of(g * SUB, SUB), SUB)
        cells = [cost_ref[here, k * LANES : (k + 1) * LANES] for k in range(chunks)]
        tiles = [-cell for cell in cells] if bases is None else [base - cell for base, cell in zip(bases, cells)]
        high_ref[here, :], total_ref[here, :] = peak_and_sum(tiles)
        return carry

    lax.fori_loop(0, rows // SUB, group_step, 0, unroll=4)
    out = []
    for a in range(rows // LANES):
        block = slice(a * LANES, (a + 1) * LANES)
        out.append(merge(high_ref[block, :].T, total_ref[block, :].T))
    return jnp.concatenate(out, axis=0)


def split3(values):
    high = values.astype(jnp.bfloat16)
    rest = values - high.astype(jnp.float32)
    mid = rest.astype(jnp.bfloat16)
    low = (rest - mid.astype(jnp.float32)).astype(jnp.bfloat16)
    return high, mid, low


def dot(left, right, dims):
    return lax.dot_general(left, right, (dims, ((), ())), preferred_element_type=jnp.float32)


def pack_kernel(
    train_label_hbm, train_hbm, valid_hbm, valid_label_hbm, train_out, valid_out,
    train_label_ref, train_ref, valid_label_ref, sems
):
    count, embed = train_hbm.shape
    points = valid_hbm.shape[0]
    pairs = (
        (train_label_hbm, train_label_ref),
        (train_hbm, train_ref),
        (valid_label_hbm, valid_label_ref),
        (valid_hbm, valid_out.at[:points, :]),
    )
    copies = [pltpu.make_async_copy(source, target, sems.at[i]) for i, (source, target) in enumerate(pairs)]
    for copy in copies:
        copy.start()
    for copy in copies:
        copy.wait()
    row_ids = lax.broadcasted_iota(jnp.int32, (count, LANES), 0)
    shown = jnp.zeros((count, LANES), jnp.int32)
    for i in range(count):
        shown = jnp.where(row_ids == i, train_label_ref[i], shown)
    packed = jnp.concatenate([train_ref[...], shown.astype(jnp.float32).astype(jnp.bfloat16)], axis=1)
    train_out[...] = jnp.broadcast_to(packed[None], train_out.shape)
    row = jnp.broadcast_to(valid_label_ref[...].astype(jnp.float32), (valid_out.shape[0] - points, LANES))
    valid_out[points:, :] = jnp.concatenate([row] * (embed // LANES), axis=1).astype(jnp.bfloat16)


def start_kernel(
    where_ref, train_ref, table_ref, mine_ref, other_ref, cost_ref, partial_ref, left_ref, row_a, row_b, col_a, col_b
):
    steps, sides, block_rows, embed = mine_ref.shape
    packed = train_ref[...].reshape(cost_ref.shape[0], embed + LANES)
    train = packed[:, :embed]
    wide = train.astype(jnp.float32)
    train_sq = jnp.sum(wide * wide, axis=1, keepdims=True) * (1.0 / embed)
    labels = packed[:, embed:].astype(jnp.float32)
    lane_ids = lax.broadcasted_iota(jnp.int32, labels.shape, 1).astype(jnp.float32)
    train_hot = jnp.where(labels == lane_ids, 1.0, 0.0).astype(jnp.bfloat16)
    parts = [dot(train_hot, part, ((1,), (0,))).astype(jnp.bfloat16) for part in split3(table_ref[...])]
    table_parts = len(parts)
    left_ref[...] = jnp.concatenate([train * jnp.bfloat16(-2.0 / embed), *parts], axis=1)
    ones = jnp.ones((SUB, embed), jnp.bfloat16)
    class_ids = lax.broadcasted_iota(jnp.int32, (LANES, LANES), 0).astype(jnp.float32)
    step = sides * LANES
    for pair in range(2 * steps):
        core, z_pair = divmod(pair, steps)
        back = lax.rem(where_ref[0] - z_pair + steps, steps)
        own = where_ref[2] == core
        blocks = [jnp.where(own, mine_ref[back, side], other_ref[back, side]) for side in range(sides)]
        block = jnp.concatenate([b[:LANES, :] for b in blocks], axis=0)
        label_rows = [b[LANES:, :LANES].astype(jnp.float32)[:1, :] for b in blocks]
        hots = [jnp.where(class_ids == label_row, 1.0, 0.0).astype(jnp.bfloat16) for label_row in label_rows]
        hot = jnp.concatenate(hots, axis=1)
        wide = block.astype(jnp.float32)
        squares = wide * wide
        sq_high = squares.astype(jnp.bfloat16)
        sq_low = (squares - sq_high.astype(jnp.float32)).astype(jnp.bfloat16)
        block_sq = (dot(ones, sq_high, ((1,), (1,))) + dot(ones, sq_low, ((1,), (1,))))[:1, :]
        cost = dot(left_ref[:, :embed], block, ((1,), (1,)))
        cost = cost + dot(left_ref[:, embed:], jnp.concatenate([hot] * table_parts, axis=0), ((1,), (0,)))
        here = slice(pair * step, (pair + 1) * step)
        cost_ref[:, here] = (cost + (train_sq + block_sq * (1.0 / embed))) * (1.0 / UNIT)
    put_partials(partial_ref, row_partial(cost_ref, None, row_a, row_b), col_partial(cost_ref, None, col_a, col_b))


def put_partials(out_ref, row, col):
    unused = jnp.zeros((out_ref.shape[0] - col.shape[0] - row.shape[0], LANES), jnp.float32)
    out_ref[...] = jnp.concatenate([col, row, unused], axis=0)


def share_kernel(flags_ref, partials_ref, out_ref, *, row_chunks):
    _, chunks, _ = out_ref.shape
    rows = [partials_ref[core, chunks : chunks + row_chunks, :] for core in range(2)]
    unused = jnp.zeros((chunks - 2 * row_chunks, LANES), jnp.float32)
    row_side = jnp.concatenate(rows + [unused], axis=0)
    col_side = lse_lead(partials_ref[:, :chunks, :])
    first_core = jnp.concatenate([flags_ref[0]] * (chunks // SUB), axis=0) > 0.5
    out_ref[...] = jnp.broadcast_to(jnp.where(first_core, row_side, col_side)[None], out_ref.shape)


def settle_kernel(flags_ref, parts_ref, out_ref):
    repeats = parts_ref.shape[1] // SUB
    lines = flags_ref.shape[0] - 1
    wanted = [jnp.concatenate([flags_ref[1 + line]] * repeats, axis=0) > 0.5 for line in range(lines)]
    parts = [jnp.where(wanted[k % lines], parts_ref[k], -jnp.inf) for k in range(parts_ref.shape[0])]
    high = parts[0]
    for part in parts[1:]:
        high = jnp.maximum(high, part)
    total = jnp.exp2(parts[0] - high)
    for part in parts[1:]:
        total = total + jnp.exp2(part - high)
    out_ref[...] = high + jnp.log2(total)


def updated(pot_ref, lse, offset):
    return 0.5 * (pot_ref[...] + (offset - lse))


def both_updated(flags_ref, lse_ref, row_pot, col_pot, row_offset, col_offset):
    chunks = row_pot.shape[0]
    first_core = flags_ref[0, :chunks, :] > 0.5
    rows = jnp.where(first_core, lse_ref[0, :chunks, :], lse_ref[0, chunks : 2 * chunks, :])
    return updated(row_pot, rows, row_offset), updated(col_pot, lse_ref[1], col_offset)


def both_kernel(
    flags_ref, cost_ref, lse_ref, row_pot, col_pot, partial_ref, row_new, col_new, row_a, row_b, col_a, col_b, spread_ref,
    *, row_offset, col_offset
):
    row, col = both_updated(flags_ref, lse_ref, row_pot, col_pot, row_offset, col_offset)
    row_new[...] = row
    col_new[...] = col
    spread_rows(row, spread_ref)
    put_partials(
        partial_ref, row_partial(cost_ref, col, row_a, row_b), col_partial(cost_ref, spread_ref, col_a, col_b)
    )


def last_row_kernel(
    flags_ref, cost_ref, lse_ref, row_pot, col_pot, row_out, row_new, row_a, row_b, *, row_offset, col_offset
):
    row, col = both_updated(flags_ref, lse_ref, row_pot, col_pot, row_offset, col_offset)
    row_new[...] = row
    row_out[...] = jnp.broadcast_to(row_partial(cost_ref, col, row_a, row_b)[None], row_out.shape)


def last_kernel(parts_ref, pot_ref, out_ref, copies_ref, *, offset):
    pot = updated(pot_ref, lse_lead(parts_ref[...]), offset)
    out_ref[...] = pot
    copies_ref[...] = jnp.broadcast_to(pot[None], copies_ref.shape)


def calibrate_kernel(parts_ref, pot_ref, out_ref, *, count):
    total = jnp.sum(jnp.sum(parts_ref[...], axis=0), keepdims=True)
    out_ref[...] = (pot_ref[...] * count - total) * (UNIT / (count - 1))


def exchange(block, axis):
    copies = block if block.ndim == 3 else jnp.broadcast_to(block[None], (lax.axis_size(axis),) + block.shape)
    return lax.all_to_all(copies, axis, 0, 0, tiled=True)


def core_groups():
    z_size, y_size, x_size = lax.axis_size(ROW[:2]), lax.axis_size("y"), lax.axis_size("x")

    def index(z, core, y, x):
        return ((z * 2 + core) * y_size + y) * x_size + x

    ys, xs, zs = range(y_size), range(x_size), range(z_size)
    over_yx = [[index(z, 0, y, x) for y in ys for x in xs] for z in zs]
    over_zx = [[index(z, 1, y, x) for z in zs for x in xs] for y in ys]
    return over_yx + over_zx


def call(kernel, out_shape, scratch, *args, smem=(), hbm=(), limit=8, **static):
    body = kernel if not static else (lambda *refs: kernel(*refs, **static))
    smem_spec, hbm_spec = pl.BlockSpec(memory_space=pltpu.SMEM), pl.BlockSpec(memory_space=pl.ANY)
    specs = [smem_spec if i in smem else hbm_spec if i in hbm else VMEM for i in range(len(args))]
    return pl.pallas_call(
        body,
        out_shape=out_shape,
        in_specs=specs,
        out_specs=[VMEM] * len(out_shape),
        scratch_shapes=scratch,
        compiler_params=pltpu.CompilerParams(vmem_limit_bytes=limit * 2**20),
        cost_estimate=pl.CostEstimate(flops=2**24, bytes_accessed=4 * 2**20, transcendentals=2**20),
    )(*args)


def shards(train_embed, valid_embed, train_labels, valid_labels, pair_level, level_cost):
    row_size, col_size = lax.axis_size(ROW), lax.axis_size(COL)
    f32 = jnp.float32
    embed = train_embed.shape[1]
    train_copies, valid_pack = call(
        pack_kernel,
        (
            jax.ShapeDtypeStruct((col_size, train_embed.shape[0], embed + LANES), jnp.bfloat16),
            jax.ShapeDtypeStruct((valid_embed.shape[0] + 16, embed), jnp.bfloat16),
        ),
        [
            pltpu.SMEM(train_labels.shape, jnp.int32),
            pltpu.VMEM(train_embed.shape, train_embed.dtype),
            pltpu.VMEM((1,) + valid_labels.shape, jnp.int32),
            pltpu.SemaphoreType.DMA((4,)),
        ],
        train_labels,
        train_embed,
        valid_embed,
        valid_labels[None, :],
        hbm=(0, 1, 2, 3),
        limit=60,
    )
    train_all = exchange(train_copies, COL)
    pair = lax.all_gather(valid_pack, "zl", axis=0)
    steps = lax.axis_size("zh")
    turn = [[(i, (i + k) % steps) for i in range(steps)] for k in range(steps)]
    mine = jnp.stack([pair] + [lax.ppermute(pair, "zh", turn[k]) for k in range(1, steps)])
    other = lax.ppermute(mine, "core", [(0, 1), (1, 0)])
    where = jnp.stack([lax.axis_index(axis) for axis in ROW + ("x",)]).astype(jnp.int32)
    rows, cols = train_embed.shape[0] * col_size, valid_embed.shape[0] * row_size
    row_chunks, col_chunks = rows // LANES, cols // LANES
    classes = pair_level.shape[0]
    level_ids = jnp.arange(level_cost.shape[0], dtype=jnp.int32)
    chosen = (pair_level[:, :, None] == level_ids).astype(f32)
    table = jnp.pad(jnp.sum(chosen * level_cost, axis=2), ((0, LANES - classes), (0, LANES - classes)))
    tile = jax.ShapeDtypeStruct((rows, cols), f32)
    row_copies = jax.ShapeDtypeStruct((col_size, row_chunks, LANES), f32)
    part_shape = jax.ShapeDtypeStruct((-(-(row_chunks + col_chunks) // SUB) * SUB, LANES), f32)
    sent_shape = jax.ShapeDtypeStruct((col_size, col_chunks, LANES), f32)
    row_shape = jax.ShapeDtypeStruct((row_chunks, LANES), f32)
    col_shape = jax.ShapeDtypeStruct((col_chunks, LANES), f32)
    tall = [pltpu.VMEM((rows, LANES), f32)] * 2
    wide = [pltpu.VMEM((row_chunks * SUB, cols), f32)] * 2
    cost, partials = call(
        start_kernel,
        (tile, part_shape),
        [pltpu.VMEM((rows, embed + 3 * LANES), jnp.bfloat16)] + tall + wide,
        where,
        train_all,
        table,
        mine,
        other,
        smem=(0,),
        limit=16,
    )
    full_rows, full_cols = rows * row_size, cols * col_size
    offsets = {"row_offset": math.log2(full_cols), "col_offset": math.log2(full_rows)}
    row_pot = jnp.zeros(row_shape.shape, f32)
    col_pot = jnp.zeros(col_shape.shape, f32)
    groups = core_groups()
    lines = jnp.arange(lax.axis_size("x"), dtype=jnp.int32)
    counts = jnp.logical_or(where[2] == 0, lines == where[3])
    flags = jnp.concatenate([where[2:3] == 0, counts]).astype(f32)
    flags = jnp.broadcast_to(flags[:, None, None], (lines.shape[0] + 1, SUB, LANES))
    for iteration in range(ITERS - 1):
        both_cores = lax.all_gather(partials, "core")
        (sent,) = call(share_kernel, (sent_shape,), [], flags, both_cores, row_chunks=row_chunks)
        got = lax.all_to_all(sent, ROW + COL, 0, 0, tiled=True, axis_index_groups=groups)
        (lse,) = call(settle_kernel, (col_shape,), [], flags, got)
        given = (flags, cost, lax.all_gather(lse, "core"), row_pot, col_pot)
        if iteration < ITERS - 2:
            partials, row_pot, col_pot = call(
                both_kernel, (part_shape, row_shape, col_shape), tall + wide + tall[:1], *given, **offsets
            )
        else:
            row_part, row_pot = call(last_row_kernel, (row_copies, row_shape), tall, *given, **offsets)
    row_got = exchange(row_part, COL)
    final_shape = jax.ShapeDtypeStruct((row_size, row_chunks, LANES), f32)
    final, copies = call(
        last_kernel, (row_shape, final_shape), [], row_got, row_pot, offset=offsets["row_offset"]
    )
    (out,) = call(calibrate_kernel, (row_shape,), [], exchange(copies, ROW), final, count=full_rows)
    return out.reshape(rows)


def solution(mesh):
    row_size, col_size = mesh.shape["row"], mesh.shape["col"]
    finer = jax.sharding.Mesh(mesh.devices.reshape(row_size // 4, 2, 2, col_size // 4, 4), ROW + COL)
    both = ROW + COL
    placed = (P(both, None), P(both, None), P(both), P(both), P(), P())
    return jax.shard_map(shards, mesh=finer, in_specs=placed, out_specs=P(ROW), check_vma=False)
```

```python
import math

import jax
import jax.numpy as jnp
from jax import lax
from jax.experimental import pallas as pl
from jax.experimental.pallas import tpu as pltpu
from jax.sharding import PartitionSpec as P

ITERS = 4
LANES = 128
SUB = 8

entropy_scale = 0.05
UNIT = entropy_scale * math.log(2.0)

ROW = ("zh", "zl", "core")
COL = ("y", "x")

VMEM = pl.BlockSpec(memory_space=pltpu.VMEM)


def lse_lead(parts):
    high = jnp.max(parts, axis=0)
    return high + jnp.log2(jnp.sum(jnp.exp2(parts - high[None]), axis=0))


def merge(high, total):
    top = jnp.max(high, axis=0, keepdims=True)
    return top + jnp.log2(jnp.sum(total * jnp.exp2(high - top), axis=0, keepdims=True))


def spread_rows(values, out_ref):
    for a in range(values.shape[0]):
        block = jnp.broadcast_to(values[a : a + 1, :], (LANES, LANES))
        out_ref[a * LANES : (a + 1) * LANES, :] = block.T


def peak_and_sum(tiles):
    high = tiles[0]
    for tile in tiles[1:]:
        high = jnp.maximum(high, tile)
    total = jnp.exp2(tiles[0] - high)
    for tile in tiles[1:]:
        total = total + jnp.exp2(tile - high)
    return high, total


def col_partial(cost_ref, row_ref, high_ref, total_ref):
    rows, cols = cost_ref.shape
    blocks, chunks = rows // LANES, cols // LANES
    groups = LANES // SUB

    def block_step(q, carry):
        start = pl.multiple_of(q * LANES, LANES)
        bases = None if row_ref is None else [row_ref[pl.ds(start + g * SUB, SUB), :] for g in range(groups)]
        for k in range(chunks):
            cells = [cost_ref[pl.ds(start + g * SUB, SUB), k * LANES : (k + 1) * LANES] for g in range(groups)]
            tiles = [-cell for cell in cells] if bases is None else [base - cell for base, cell in zip(bases, cells)]
            high, total = peak_and_sum(tiles)
            here = (pl.ds(pl.multiple_of(q * SUB, SUB), SUB), slice(k * LANES, (k + 1) * LANES))
            high_ref[here] = high
            total_ref[here] = total
        return carry

    lax.fori_loop(0, blocks, block_step, 0, unroll=True)
    out = [merge(high_ref[:, k * LANES : (k + 1) * LANES], total_ref[:, k * LANES : (k + 1) * LANES]) for k in range(chunks)]
    return jnp.concatenate(out, axis=0)


def row_partial(cost_ref, col, high_ref, total_ref):
    rows, cols = cost_ref.shape
    chunks = cols // LANES
    bases = None if col is None else [jnp.broadcast_to(col[k : k + 1, :], (SUB, LANES)) for k in range(chunks)]

    def group_step(g, carry):
        here = pl.ds(pl.multiple_of(g * SUB, SUB), SUB)
        cells = [cost_ref[here, k * LANES : (k + 1) * LANES] for k in range(chunks)]
        tiles = [-cell for cell in cells] if bases is None else [base - cell for base, cell in zip(bases, cells)]
        high_ref[here, :], total_ref[here, :] = peak_and_sum(tiles)
        return carry

    lax.fori_loop(0, rows // SUB, group_step, 0, unroll=4)
    out = []
    for a in range(rows // LANES):
        block = slice(a * LANES, (a + 1) * LANES)
        out.append(merge(high_ref[block, :].T, total_ref[block, :].T))
    return jnp.concatenate(out, axis=0)


def split3(values):
    high = values.astype(jnp.bfloat16)
    rest = values - high.astype(jnp.float32)
    mid = rest.astype(jnp.bfloat16)
    low = (rest - mid.astype(jnp.float32)).astype(jnp.bfloat16)
    return high, mid, low


def dot(left, right, dims):
    return lax.dot_general(left, right, (dims, ((), ())), preferred_element_type=jnp.float32)


def pack_kernel(
    train_label_hbm, train_hbm, valid_hbm, valid_label_hbm, train_out, valid_out,
    train_label_ref, train_ref, valid_label_ref, sems
):
    count, embed = train_hbm.shape
    points = valid_hbm.shape[0]
    pairs = (
        (train_label_hbm, train_label_ref),
        (train_hbm, train_ref),
        (valid_label_hbm, valid_label_ref),
        (valid_hbm, valid_out.at[:points, :]),
    )
    copies = [pltpu.make_async_copy(source, target, sems.at[i]) for i, (source, target) in enumerate(pairs)]
    for copy in copies:
        copy.start()
    for copy in copies:
        copy.wait()
    row_ids = lax.broadcasted_iota(jnp.int32, (count, LANES), 0)
    shown = jnp.zeros((count, LANES), jnp.int32)
    for i in range(count):
        shown = jnp.where(row_ids == i, train_label_ref[i], shown)
    packed = jnp.concatenate([train_ref[...], shown.astype(jnp.float32).astype(jnp.bfloat16)], axis=1)
    train_out[...] = jnp.broadcast_to(packed[None], train_out.shape)
    row = jnp.broadcast_to(valid_label_ref[...].astype(jnp.float32), (valid_out.shape[0] - points, LANES))
    valid_out[points:, :] = jnp.concatenate([row] * (embed // LANES), axis=1).astype(jnp.bfloat16)


def squared_sums(rows, ones, swap):
    wide = rows.astype(jnp.float32)
    squares = wide * wide
    high = squares.astype(jnp.bfloat16)
    low = (squares - high.astype(jnp.float32)).astype(jnp.bfloat16)
    if swap:
        return dot(ones, high, ((1,), (1,))) + dot(ones, low, ((1,), (1,)))
    return dot(high, ones, ((1,), (1,))) + dot(low, ones, ((1,), (1,)))


def valid_kernel(where_ref, mine_ref, other_ref, valid_ref, hot_ref, sq_ref):
    steps, sides, _, embed = mine_ref.shape
    ones = jnp.ones((SUB, embed), jnp.bfloat16)
    class_ids = lax.broadcasted_iota(jnp.int32, (LANES, LANES), 0).astype(jnp.float32)
    for k in range(2 * steps * sides):
        core, z_pair, side = k // (steps * sides), k // sides % steps, k % sides
        back = lax.rem(where_ref[0] - z_pair + steps, steps)
        block = jnp.where(where_ref[2] == core, mine_ref[back, side], other_ref[back, side])
        here = slice(k * LANES, (k + 1) * LANES)
        points = block[:LANES, :]
        label_row = block[LANES:, :LANES].astype(jnp.float32)[:1, :]
        valid_ref[here, :] = points
        hot_ref[:, here] = jnp.where(class_ids == label_row, 1.0, 0.0).astype(jnp.bfloat16)
        sq_ref[:, here] = squared_sums(points, ones, True) * (1.0 / embed)


def start_kernel(
    train_ref, table_ref, valid_ref, hot_ref, sq_ref, cost_ref, partial_ref, left_ref, row_a, row_b, col_a, col_b
):
    embed = valid_ref.shape[1]
    packed = train_ref[...].reshape(cost_ref.shape[0], embed + LANES)
    train = packed[:, :embed]
    train_sq = squared_sums(train, jnp.ones((LANES, embed), jnp.bfloat16), False) * (1.0 / embed)
    labels = packed[:, embed:].astype(jnp.float32)
    lane_ids = lax.broadcasted_iota(jnp.int32, labels.shape, 1).astype(jnp.float32)
    train_hot = jnp.where(labels == lane_ids, 1.0, 0.0).astype(jnp.bfloat16)
    table_parts = split3(table_ref[...])
    table_rows = dot(train_hot, jnp.concatenate(table_parts, axis=1), ((1,), (0,))).astype(jnp.bfloat16)
    left_ref[...] = jnp.concatenate([train * jnp.bfloat16(-2.0 / embed), table_rows], axis=1)
    step = 2 * LANES
    train_sq = jnp.concatenate([train_sq] * 2, axis=1)
    for pair in range(valid_ref.shape[0] // step):
        here = slice(pair * step, (pair + 1) * step)
        cost = dot(left_ref[:, :embed], valid_ref[here, :], ((1,), (1,)))
        hot = jnp.concatenate([hot_ref[:, here]] * len(table_parts), axis=0)
        cost = cost + dot(left_ref[:, embed:], hot, ((1,), (0,)))
        cost_ref[:, here] = (cost + (train_sq + sq_ref[:1, here])) * (1.0 / UNIT)
    put_partials(partial_ref, row_partial(cost_ref, None, row_a, row_b), col_partial(cost_ref, None, col_a, col_b))


def put_partials(out_ref, row, col):
    unused = jnp.zeros((out_ref.shape[0] - col.shape[0] - row.shape[0], LANES), jnp.float32)
    out_ref[...] = jnp.concatenate([col, row, unused], axis=0)


def share_kernel(flags_ref, partials_ref, out_ref, *, row_chunks):
    _, chunks, _ = out_ref.shape
    rows = [partials_ref[core, chunks : chunks + row_chunks, :] for core in range(2)]
    unused = jnp.zeros((chunks - 2 * row_chunks, LANES), jnp.float32)
    row_side = jnp.concatenate(rows + [unused], axis=0)
    col_side = lse_lead(partials_ref[:, :chunks, :])
    first_core = jnp.concatenate([flags_ref[0]] * (chunks // SUB), axis=0) > 0.5
    out_ref[...] = jnp.broadcast_to(jnp.where(first_core, row_side, col_side)[None], out_ref.shape)


def settle_kernel(flags_ref, parts_ref, out_ref):
    repeats = parts_ref.shape[1] // SUB
    lines = flags_ref.shape[0] - 1
    wanted = [jnp.concatenate([flags_ref[1 + line]] * repeats, axis=0) > 0.5 for line in range(lines)]
    parts = [jnp.where(wanted[k % lines], parts_ref[k], -jnp.inf) for k in range(parts_ref.shape[0])]
    high = parts[0]
    for part in parts[1:]:
        high = jnp.maximum(high, part)
    total = jnp.exp2(parts[0] - high)
    for part in parts[1:]:
        total = total + jnp.exp2(part - high)
    out_ref[...] = high + jnp.log2(total)


def updated(pot_ref, lse, offset):
    return 0.5 * (pot_ref[...] + (offset - lse))


def both_updated(flags_ref, lse_ref, row_pot, col_pot, row_offset, col_offset):
    chunks = row_pot.shape[0]
    first_core = flags_ref[0, :chunks, :] > 0.5
    rows = jnp.where(first_core, lse_ref[0, :chunks, :], lse_ref[0, chunks : 2 * chunks, :])
    return updated(row_pot, rows, row_offset), updated(col_pot, lse_ref[1], col_offset)


def both_kernel(
    flags_ref, cost_ref, lse_ref, row_pot, col_pot, partial_ref, row_new, col_new, row_a, row_b, col_a, col_b, spread_ref,
    *, row_offset, col_offset
):
    row, col = both_updated(flags_ref, lse_ref, row_pot, col_pot, row_offset, col_offset)
    row_new[...] = row
    col_new[...] = col
    spread_rows(row, spread_ref)
    put_partials(
        partial_ref, row_partial(cost_ref, col, row_a, row_b), col_partial(cost_ref, spread_ref, col_a, col_b)
    )


def last_row_kernel(
    flags_ref, cost_ref, lse_ref, row_pot, col_pot, row_out, row_new, row_a, row_b, *, row_offset, col_offset
):
    row, col = both_updated(flags_ref, lse_ref, row_pot, col_pot, row_offset, col_offset)
    row_new[...] = row
    row_out[...] = jnp.broadcast_to(row_partial(cost_ref, col, row_a, row_b)[None], row_out.shape)


def last_kernel(parts_ref, pot_ref, out_ref, copies_ref, *, offset):
    pot = updated(pot_ref, lse_lead(parts_ref[...]), offset)
    out_ref[...] = pot
    copies_ref[...] = jnp.broadcast_to(pot[None], copies_ref.shape)


def calibrate_kernel(parts_ref, pot_ref, out_ref, *, count):
    total = jnp.sum(jnp.sum(parts_ref[...], axis=0), keepdims=True)
    out_ref[...] = (pot_ref[...] * count - total) * (UNIT / (count - 1))


def exchange(block, axis):
    copies = block if block.ndim == 3 else jnp.broadcast_to(block[None], (lax.axis_size(axis),) + block.shape)
    return lax.all_to_all(copies, axis, 0, 0, tiled=True)


def core_groups():
    z_size, y_size, x_size = lax.axis_size(ROW[:2]), lax.axis_size("y"), lax.axis_size("x")

    def index(z, core, y, x):
        return ((z * 2 + core) * y_size + y) * x_size + x

    ys, xs, zs = range(y_size), range(x_size), range(z_size)
    over_yx = [[index(z, 0, y, x) for y in ys for x in xs] for z in zs]
    over_zx = [[index(z, 1, y, x) for z in zs for x in xs] for y in ys]
    return over_yx + over_zx


def call(kernel, out_shape, scratch, *args, smem=(), hbm=(), limit=8, **static):
    body = kernel if not static else (lambda *refs: kernel(*refs, **static))
    smem_spec, hbm_spec = pl.BlockSpec(memory_space=pltpu.SMEM), pl.BlockSpec(memory_space=pl.ANY)
    specs = [smem_spec if i in smem else hbm_spec if i in hbm else VMEM for i in range(len(args))]
    return pl.pallas_call(
        body,
        out_shape=out_shape,
        in_specs=specs,
        out_specs=[VMEM] * len(out_shape),
        scratch_shapes=scratch,
        compiler_params=pltpu.CompilerParams(vmem_limit_bytes=limit * 2**20),
        cost_estimate=pl.CostEstimate(flops=2**24, bytes_accessed=4 * 2**20, transcendentals=2**20),
    )(*args)


def shards(train_embed, valid_embed, train_labels, valid_labels, pair_level, level_cost):
    row_size, col_size = lax.axis_size(ROW), lax.axis_size(COL)
    f32 = jnp.float32
    embed = train_embed.shape[1]
    train_copies, valid_pack = call(
        pack_kernel,
        (
            jax.ShapeDtypeStruct((col_size, train_embed.shape[0], embed + LANES), jnp.bfloat16),
            jax.ShapeDtypeStruct((valid_embed.shape[0] + 16, embed), jnp.bfloat16),
        ),
        [
            pltpu.SMEM(train_labels.shape, jnp.int32),
            pltpu.VMEM(train_embed.shape, train_embed.dtype),
            pltpu.VMEM((1,) + valid_labels.shape, jnp.int32),
            pltpu.SemaphoreType.DMA((4,)),
        ],
        train_labels,
        train_embed,
        valid_embed,
        valid_labels[None, :],
        hbm=(0, 1, 2, 3),
        limit=60,
    )
    train_all = exchange(train_copies, COL)
    pair = lax.all_gather(valid_pack, "zl", axis=0)
    steps = lax.axis_size("zh")
    turn = [[(i, (i + k) % steps) for i in range(steps)] for k in range(steps)]
    mine = jnp.stack([pair] + [lax.ppermute(pair, "zh", turn[k]) for k in range(1, steps)])
    other = lax.ppermute(mine, "core", [(0, 1), (1, 0)])
    where = jnp.stack([lax.axis_index(axis) for axis in ROW + ("x",)]).astype(jnp.int32)
    rows, cols = train_embed.shape[0] * col_size, valid_embed.shape[0] * row_size
    row_chunks, col_chunks = rows // LANES, cols // LANES
    classes = pair_level.shape[0]
    level_ids = jnp.arange(level_cost.shape[0], dtype=jnp.int32)
    chosen = (pair_level[:, :, None] == level_ids).astype(f32)
    table = jnp.pad(jnp.sum(chosen * level_cost, axis=2), ((0, LANES - classes), (0, LANES - classes)))
    tile = jax.ShapeDtypeStruct((rows, cols), f32)
    row_copies = jax.ShapeDtypeStruct((col_size, row_chunks, LANES), f32)
    part_shape = jax.ShapeDtypeStruct((-(-(row_chunks + col_chunks) // SUB) * SUB, LANES), f32)
    sent_shape = jax.ShapeDtypeStruct((col_size, col_chunks, LANES), f32)
    row_shape = jax.ShapeDtypeStruct((row_chunks, LANES), f32)
    col_shape = jax.ShapeDtypeStruct((col_chunks, LANES), f32)
    tall = [pltpu.VMEM((rows, LANES), f32)] * 2
    wide = [pltpu.VMEM((row_chunks * SUB, cols), f32)] * 2
    valid_side = call(
        valid_kernel,
        (
            jax.ShapeDtypeStruct((cols, embed), jnp.bfloat16),
            jax.ShapeDtypeStruct((LANES, cols), jnp.bfloat16),
            jax.ShapeDtypeStruct((SUB, cols), f32),
        ),
        [],
        where,
        mine,
        other,
        smem=(0,),
    )
    cost, partials = call(
        start_kernel,
        (tile, part_shape),
        [pltpu.VMEM((rows, embed + 3 * LANES), jnp.bfloat16)] + tall + wide,
        train_all,
        table,
        *valid_side,
        limit=16,
    )
    full_rows, full_cols = rows * row_size, cols * col_size
    offsets = {"row_offset": math.log2(full_cols), "col_offset": math.log2(full_rows)}
    row_pot = jnp.zeros(row_shape.shape, f32)
    col_pot = jnp.zeros(col_shape.shape, f32)
    groups = core_groups()
    lines = jnp.arange(lax.axis_size("x"), dtype=jnp.int32)
    counts = jnp.logical_or(where[2] == 0, lines == where[3])
    flags = jnp.concatenate([where[2:3] == 0, counts]).astype(f32)
    flags = jnp.broadcast_to(flags[:, None, None], (lines.shape[0] + 1, SUB, LANES))
    for iteration in range(ITERS - 1):
        both_cores = lax.all_gather(partials, "core")
        (sent,) = call(share_kernel, (sent_shape,), [], flags, both_cores, row_chunks=row_chunks)
        got = lax.all_to_all(sent, ROW + COL, 0, 0, tiled=True, axis_index_groups=groups)
        (lse,) = call(settle_kernel, (col_shape,), [], flags, got)
        given = (flags, cost, lax.all_gather(lse, "core"), row_pot, col_pot)
        if iteration < ITERS - 2:
            partials, row_pot, col_pot = call(
                both_kernel, (part_shape, row_shape, col_shape), tall + wide + tall[:1], *given, **offsets
            )
        else:
            row_part, row_pot = call(last_row_kernel, (row_copies, row_shape), tall, *given, **offsets)
    row_got = exchange(row_part, COL)
    final_shape = jax.ShapeDtypeStruct((row_size, row_chunks, LANES), f32)
    final, copies = call(
        last_kernel, (row_shape, final_shape), [], row_got, row_pot, offset=offsets["row_offset"]
    )
    (out,) = call(calibrate_kernel, (row_shape,), [], exchange(copies, ROW), final, count=full_rows)
    return out.reshape(rows)


def solution(mesh):
    row_size, col_size = mesh.shape["row"], mesh.shape["col"]
    finer = jax.sharding.Mesh(mesh.devices.reshape(row_size // 4, 2, 2, col_size // 4, 4), ROW + COL)
    both = ROW + COL
    placed = (P(both, None), P(both, None), P(both), P(both), P(), P())
    return jax.shard_map(shards, mesh=finer, in_specs=placed, out_specs=P(ROW), check_vma=False)
```

```python
import math

import jax
import jax.numpy as jnp
from jax import lax
from jax.experimental import pallas as pl
from jax.experimental.pallas import tpu as pltpu
from jax.sharding import PartitionSpec as P

ITERS = 4
LANES = 128
SUB = 8

entropy_scale = 0.05
UNIT = entropy_scale * math.log(2.0)

ROW = ("half", "place", "core")
COL = ("y", "x")

VMEM = pl.BlockSpec(memory_space=pltpu.VMEM)


def lse_lead(parts):
    high = jnp.max(parts, axis=0)
    return high + jnp.log2(jnp.sum(jnp.exp2(parts - high[None]), axis=0))


def merge(high, total):
    top = jnp.max(high, axis=0, keepdims=True)
    return top + jnp.log2(jnp.sum(total * jnp.exp2(high - top), axis=0, keepdims=True))


def spread_rows(values, out_ref):
    for a in range(values.shape[0]):
        block = jnp.broadcast_to(values[a : a + 1, :], (LANES, LANES))
        out_ref[a * LANES : (a + 1) * LANES, :] = block.T


def peak_and_sum(tiles):
    high = tiles[0]
    for tile in tiles[1:]:
        high = jnp.maximum(high, tile)
    total = jnp.exp2(tiles[0] - high)
    for tile in tiles[1:]:
        total = total + jnp.exp2(tile - high)
    return high, total


def col_partial(cost_ref, row_ref, high_ref, total_ref):
    rows, cols = cost_ref.shape
    blocks, chunks = rows // LANES, cols // LANES
    groups = LANES // SUB

    def block_step(q, carry):
        start = pl.multiple_of(q * LANES, LANES)
        bases = None if row_ref is None else [row_ref[pl.ds(start + g * SUB, SUB), :] for g in range(groups)]
        for k in range(chunks):
            cells = [cost_ref[pl.ds(start + g * SUB, SUB), k * LANES : (k + 1) * LANES] for g in range(groups)]
            tiles = [-cell for cell in cells] if bases is None else [base - cell for base, cell in zip(bases, cells)]
            high, total = peak_and_sum(tiles)
            here = (pl.ds(pl.multiple_of(q * SUB, SUB), SUB), slice(k * LANES, (k + 1) * LANES))
            high_ref[here] = high
            total_ref[here] = total
        return carry

    lax.fori_loop(0, blocks, block_step, 0, unroll=True)
    out = [merge(high_ref[:, k * LANES : (k + 1) * LANES], total_ref[:, k * LANES : (k + 1) * LANES]) for k in range(chunks)]
    return jnp.concatenate(out, axis=0)


def row_partial(cost_ref, col, high_ref, total_ref):
    rows, cols = cost_ref.shape
    chunks = cols // LANES
    bases = None if col is None else [jnp.broadcast_to(col[k : k + 1, :], (SUB, LANES)) for k in range(chunks)]

    def group_step(g, carry):
        here = pl.ds(pl.multiple_of(g * SUB, SUB), SUB)
        cells = [cost_ref[here, k * LANES : (k + 1) * LANES] for k in range(chunks)]
        tiles = [-cell for cell in cells] if bases is None else [base - cell for base, cell in zip(bases, cells)]
        high_ref[here, :], total_ref[here, :] = peak_and_sum(tiles)
        return carry

    lax.fori_loop(0, rows // SUB, group_step, 0, unroll=4)
    out = []
    for a in range(rows // LANES):
        block = slice(a * LANES, (a + 1) * LANES)
        out.append(merge(high_ref[block, :].T, total_ref[block, :].T))
    return jnp.concatenate(out, axis=0)


def split3(values):
    high = values.astype(jnp.bfloat16)
    rest = values - high.astype(jnp.float32)
    mid = rest.astype(jnp.bfloat16)
    low = (rest - mid.astype(jnp.float32)).astype(jnp.bfloat16)
    return high, mid, low


def dot(left, right, dims):
    return lax.dot_general(left, right, (dims, ((), ())), preferred_element_type=jnp.float32)


def pack_kernel(
    train_label_hbm, train_hbm, valid_hbm, valid_label_hbm, train_out, valid_out,
    train_label_ref, train_ref, valid_label_ref, sems
):
    count, embed = train_hbm.shape
    points = valid_hbm.shape[0]
    pairs = (
        (train_label_hbm, train_label_ref),
        (train_hbm, train_ref),
        (valid_label_hbm, valid_label_ref),
        (valid_hbm, valid_out.at[:points, :]),
    )
    copies = [pltpu.make_async_copy(source, target, sems.at[i]) for i, (source, target) in enumerate(pairs)]
    for copy in copies:
        copy.start()
    for copy in copies:
        copy.wait()
    row_ids = lax.broadcasted_iota(jnp.int32, (count, LANES), 0)
    shown = jnp.zeros((count, LANES), jnp.int32)
    for i in range(count):
        shown = jnp.where(row_ids == i, train_label_ref[i], shown)
    packed = jnp.concatenate([train_ref[...], shown.astype(jnp.float32).astype(jnp.bfloat16)], axis=1)
    train_out[...] = jnp.broadcast_to(packed[None], train_out.shape)
    row = jnp.broadcast_to(valid_label_ref[...].astype(jnp.float32), (valid_out.shape[0] - points, LANES))
    valid_out[points:, :] = jnp.concatenate([row] * (embed // LANES), axis=1).astype(jnp.bfloat16)


def squared_sums(rows, ones, swap):
    wide = rows.astype(jnp.float32)
    squares = wide * wide
    high = squares.astype(jnp.bfloat16)
    low = (squares - high.astype(jnp.float32)).astype(jnp.bfloat16)
    if swap:
        return dot(ones, high, ((1,), (1,))) + dot(ones, low, ((1,), (1,)))
    return dot(high, ones, ((1,), (1,))) + dot(low, ones, ((1,), (1,)))


def valid_kernel(where_ref, mine_ref, other_ref, valid_ref, hot_ref, sq_ref):
    steps, sides, _, embed = mine_ref.shape
    ones = jnp.ones((SUB, embed), jnp.bfloat16)
    class_ids = lax.broadcasted_iota(jnp.int32, (LANES, LANES), 0).astype(jnp.float32)
    for k in range(2 * steps * sides):
        core, z_pair, side = k // (steps * sides), k // sides % steps, k % sides
        back = lax.rem(where_ref[1] - z_pair + steps, steps)
        block = jnp.where(where_ref[2] == core, mine_ref[back, side], other_ref[back, side])
        here = slice(k * LANES, (k + 1) * LANES)
        points = block[:LANES, :]
        label_row = block[LANES:, :LANES].astype(jnp.float32)[:1, :]
        valid_ref[here, :] = points
        hot_ref[:, here] = jnp.where(class_ids == label_row, 1.0, 0.0).astype(jnp.bfloat16)
        sq_ref[:, here] = squared_sums(points, ones, True) * (1.0 / embed)


def start_kernel(
    train_ref, table_ref, valid_ref, hot_ref, sq_ref, cost_ref, partial_ref, left_ref, row_a, row_b, col_a, col_b
):
    embed = valid_ref.shape[1]
    packed = train_ref[...].reshape(cost_ref.shape[0], embed + LANES)
    train = packed[:, :embed]
    train_sq = squared_sums(train, jnp.ones((LANES, embed), jnp.bfloat16), False) * (1.0 / embed)
    labels = packed[:, embed:].astype(jnp.float32)
    lane_ids = lax.broadcasted_iota(jnp.int32, labels.shape, 1).astype(jnp.float32)
    train_hot = jnp.where(labels == lane_ids, 1.0, 0.0).astype(jnp.bfloat16)
    table_parts = split3(table_ref[...])
    table_rows = dot(train_hot, jnp.concatenate(table_parts, axis=1), ((1,), (0,))).astype(jnp.bfloat16)
    left_ref[...] = jnp.concatenate([train * jnp.bfloat16(-2.0 / embed), table_rows], axis=1)
    step = 2 * LANES
    train_sq = jnp.concatenate([train_sq] * 2, axis=1)
    for pair in range(valid_ref.shape[0] // step):
        here = slice(pair * step, (pair + 1) * step)
        cost = dot(left_ref[:, :embed], valid_ref[here, :], ((1,), (1,)))
        hot = jnp.concatenate([hot_ref[:, here]] * len(table_parts), axis=0)
        cost = cost + dot(left_ref[:, embed:], hot, ((1,), (0,)))
        cost_ref[:, here] = (cost + (train_sq + sq_ref[:1, here])) * (1.0 / UNIT)
    put_partials(partial_ref, row_partial(cost_ref, None, row_a, row_b), col_partial(cost_ref, None, col_a, col_b))


def put_partials(out_ref, row, col):
    unused = jnp.zeros((out_ref.shape[0] - col.shape[0] - row.shape[0], LANES), jnp.float32)
    out_ref[...] = jnp.concatenate([col, row, unused], axis=0)


def share_kernel(flags_ref, partials_ref, out_ref, *, row_chunks):
    _, chunks, _ = out_ref.shape
    rows = [partials_ref[core, chunks : chunks + row_chunks, :] for core in range(2)]
    unused = jnp.zeros((chunks - 2 * row_chunks, LANES), jnp.float32)
    row_side = jnp.concatenate(rows + [unused], axis=0)
    col_side = lse_lead(partials_ref[:, :chunks, :])
    first_core = jnp.concatenate([flags_ref[0]] * (chunks // SUB), axis=0) > 0.5
    out_ref[...] = jnp.broadcast_to(jnp.where(first_core, row_side, col_side)[None], out_ref.shape)


def settle_kernel(flags_ref, parts_ref, out_ref):
    repeats = parts_ref.shape[1] // SUB
    lines = flags_ref.shape[0] - 1
    wanted = [jnp.concatenate([flags_ref[1 + line]] * repeats, axis=0) > 0.5 for line in range(lines)]
    parts = [jnp.where(wanted[k % lines], parts_ref[k], -jnp.inf) for k in range(parts_ref.shape[0])]
    high = parts[0]
    for part in parts[1:]:
        high = jnp.maximum(high, part)
    total = jnp.exp2(parts[0] - high)
    for part in parts[1:]:
        total = total + jnp.exp2(part - high)
    out_ref[...] = high + jnp.log2(total)


def updated(pot_ref, lse, offset):
    return 0.5 * (pot_ref[...] + (offset - lse))


def both_updated(flags_ref, lse_ref, row_pot, col_pot, row_offset, col_offset):
    chunks = row_pot.shape[0]
    first_core = flags_ref[0, :chunks, :] > 0.5
    rows = jnp.where(first_core, lse_ref[0, :chunks, :], lse_ref[0, chunks : 2 * chunks, :])
    return updated(row_pot, rows, row_offset), updated(col_pot, lse_ref[1], col_offset)


def both_kernel(
    flags_ref, cost_ref, lse_ref, row_pot, col_pot, partial_ref, row_new, col_new, row_a, row_b, col_a, col_b, spread_ref,
    *, row_offset, col_offset
):
    row, col = both_updated(flags_ref, lse_ref, row_pot, col_pot, row_offset, col_offset)
    row_new[...] = row
    col_new[...] = col
    spread_rows(row, spread_ref)
    put_partials(
        partial_ref, row_partial(cost_ref, col, row_a, row_b), col_partial(cost_ref, spread_ref, col_a, col_b)
    )


def last_row_kernel(
    flags_ref, cost_ref, lse_ref, row_pot, col_pot, row_out, row_new, row_a, row_b, *, row_offset, col_offset
):
    row, col = both_updated(flags_ref, lse_ref, row_pot, col_pot, row_offset, col_offset)
    row_new[...] = row
    row_out[...] = jnp.broadcast_to(row_partial(cost_ref, col, row_a, row_b)[None], row_out.shape)


def last_kernel(parts_ref, pot_ref, out_ref, copies_ref, *, offset):
    pot = updated(pot_ref, lse_lead(parts_ref[...]), offset)
    out_ref[...] = pot
    copies_ref[...] = jnp.broadcast_to(pot[None], copies_ref.shape)


def calibrate_kernel(parts_ref, pot_ref, out_ref, *, count):
    total = jnp.sum(jnp.sum(parts_ref[...], axis=0), keepdims=True)
    out_ref[...] = (pot_ref[...] * count - total) * (UNIT / (count - 1))


def exchange(block, axis):
    copies = block if block.ndim == 3 else jnp.broadcast_to(block[None], (lax.axis_size(axis),) + block.shape)
    return lax.all_to_all(copies, axis, 0, 0, tiled=True)


def core_groups():
    z_size, y_size, x_size = lax.axis_size(ROW[:2]), lax.axis_size("y"), lax.axis_size("x")

    def index(z, core, y, x):
        return ((z * 2 + core) * y_size + y) * x_size + x

    ys, xs, zs = range(y_size), range(x_size), range(z_size)
    over_yx = [[index(z, 0, y, x) for y in ys for x in xs] for z in zs]
    over_zx = [[index(z, 1, y, x) for z in zs for x in xs] for y in ys]
    return over_yx + over_zx


def call(kernel, out_shape, scratch, *args, smem=(), hbm=(), limit=8, **static):
    body = kernel if not static else (lambda *refs: kernel(*refs, **static))
    smem_spec, hbm_spec = pl.BlockSpec(memory_space=pltpu.SMEM), pl.BlockSpec(memory_space=pl.ANY)
    specs = [smem_spec if i in smem else hbm_spec if i in hbm else VMEM for i in range(len(args))]
    return pl.pallas_call(
        body,
        out_shape=out_shape,
        in_specs=specs,
        out_specs=[VMEM] * len(out_shape),
        scratch_shapes=scratch,
        compiler_params=pltpu.CompilerParams(vmem_limit_bytes=limit * 2**20),
        cost_estimate=pl.CostEstimate(flops=2**24, bytes_accessed=4 * 2**20, transcendentals=2**20),
    )(*args)


def shards(train_embed, valid_embed, train_labels, valid_labels, pair_level, level_cost):
    row_size, col_size = lax.axis_size(ROW), lax.axis_size(COL)
    f32 = jnp.float32
    embed = train_embed.shape[1]
    train_copies, valid_pack = call(
        pack_kernel,
        (
            jax.ShapeDtypeStruct((col_size, train_embed.shape[0], embed + LANES), jnp.bfloat16),
            jax.ShapeDtypeStruct((valid_embed.shape[0] + 16, embed), jnp.bfloat16),
        ),
        [
            pltpu.SMEM(train_labels.shape, jnp.int32),
            pltpu.VMEM(train_embed.shape, train_embed.dtype),
            pltpu.VMEM((1,) + valid_labels.shape, jnp.int32),
            pltpu.SemaphoreType.DMA((4,)),
        ],
        train_labels,
        train_embed,
        valid_embed,
        valid_labels[None, :],
        hbm=(0, 1, 2, 3),
        limit=60,
    )
    train_all = exchange(train_copies, COL)
    pair = lax.all_gather(valid_pack, "half", axis=0)
    steps, ring = lax.axis_size("place"), lax.axis_size(ROW[:2])
    turn = [[(i, (i + k) % ring) for i in range(ring)] for k in (1, 2, -1)]
    mine = jnp.stack([pair] + [lax.ppermute(pair, ROW[:2], there) for there in turn])
    other = lax.ppermute(mine, "core", [(0, 1), (1, 0)])
    where = jnp.stack([lax.axis_index(axis) for axis in ROW + ("x",)]).astype(jnp.int32)
    rows, cols = train_embed.shape[0] * col_size, valid_embed.shape[0] * row_size
    row_chunks, col_chunks = rows // LANES, cols // LANES
    classes = pair_level.shape[0]
    level_ids = jnp.arange(level_cost.shape[0], dtype=jnp.int32)
    chosen = (pair_level[:, :, None] == level_ids).astype(f32)
    table = jnp.pad(jnp.sum(chosen * level_cost, axis=2), ((0, LANES - classes), (0, LANES - classes)))
    tile = jax.ShapeDtypeStruct((rows, cols), f32)
    row_copies = jax.ShapeDtypeStruct((col_size, row_chunks, LANES), f32)
    part_shape = jax.ShapeDtypeStruct((-(-(row_chunks + col_chunks) // SUB) * SUB, LANES), f32)
    sent_shape = jax.ShapeDtypeStruct((col_size, col_chunks, LANES), f32)
    row_shape = jax.ShapeDtypeStruct((row_chunks, LANES), f32)
    col_shape = jax.ShapeDtypeStruct((col_chunks, LANES), f32)
    tall = [pltpu.VMEM((rows, LANES), f32)] * 2
    wide = [pltpu.VMEM((row_chunks * SUB, cols), f32)] * 2
    valid_side = call(
        valid_kernel,
        (
            jax.ShapeDtypeStruct((cols, embed), jnp.bfloat16),
            jax.ShapeDtypeStruct((LANES, cols), jnp.bfloat16),
            jax.ShapeDtypeStruct((SUB, cols), f32),
        ),
        [],
        where,
        mine,
        other,
        smem=(0,),
    )
    cost, partials = call(
        start_kernel,
        (tile, part_shape),
        [pltpu.VMEM((rows, embed + 3 * LANES), jnp.bfloat16)] + tall + wide,
        train_all,
        table,
        *valid_side,
        limit=16,
    )
    full_rows, full_cols = rows * row_size, cols * col_size
    offsets = {"row_offset": math.log2(full_cols), "col_offset": math.log2(full_rows)}
    row_pot = jnp.zeros(row_shape.shape, f32)
    col_pot = jnp.zeros(col_shape.shape, f32)
    groups = core_groups()
    lines = jnp.arange(lax.axis_size("x"), dtype=jnp.int32)
    counts = jnp.logical_or(where[2] == 0, lines == where[3])
    flags = jnp.concatenate([where[2:3] == 0, counts]).astype(f32)
    flags = jnp.broadcast_to(flags[:, None, None], (lines.shape[0] + 1, SUB, LANES))
    for iteration in range(ITERS - 1):
        both_cores = lax.all_gather(partials, "core")
        (sent,) = call(share_kernel, (sent_shape,), [], flags, both_cores, row_chunks=row_chunks)
        got = lax.all_to_all(sent, ROW + COL, 0, 0, tiled=True, axis_index_groups=groups)
        (lse,) = call(settle_kernel, (col_shape,), [], flags, got)
        given = (flags, cost, lax.all_gather(lse, "core"), row_pot, col_pot)
        if iteration < ITERS - 2:
            partials, row_pot, col_pot = call(
                both_kernel, (part_shape, row_shape, col_shape), tall + wide + tall[:1], *given, **offsets
            )
        else:
            row_part, row_pot = call(last_row_kernel, (row_copies, row_shape), tall, *given, **offsets)
    row_got = exchange(row_part, COL)
    final_shape = jax.ShapeDtypeStruct((row_size, row_chunks, LANES), f32)
    final, copies = call(
        last_kernel, (row_shape, final_shape), [], row_got, row_pot, offset=offsets["row_offset"]
    )
    (out,) = call(calibrate_kernel, (row_shape,), [], exchange(copies, ROW), final, count=full_rows)
    return out.reshape(rows)


def solution(mesh):
    row_size, col_size = mesh.shape["row"], mesh.shape["col"]
    finer = jax.sharding.Mesh(mesh.devices.reshape(2, row_size // 4, 2, col_size // 4, 4), ROW + COL)
    both = ROW + COL
    placed = (P(both, None), P(both, None), P(both), P(both), P(), P())
    return jax.shard_map(shards, mesh=finer, in_specs=placed, out_specs=P(ROW), check_vma=False)
```

```python
import math

import jax
import jax.numpy as jnp
from jax import lax
from jax.experimental import pallas as pl
from jax.experimental.pallas import tpu as pltpu
from jax.sharding import PartitionSpec as P

ITERS = 4
LANES = 128
SUB = 8

entropy_scale = 0.05
UNIT = entropy_scale * math.log(2.0)

ROW = ("zh", "zl", "core")
COL = ("y", "x")

VMEM = pl.BlockSpec(memory_space=pltpu.VMEM)


def lse_lead(parts):
    high = jnp.max(parts, axis=0)
    return high + jnp.log2(jnp.sum(jnp.exp2(parts - high[None]), axis=0))


def merge(high, total):
    top = jnp.max(high, axis=0, keepdims=True)
    return top + jnp.log2(jnp.sum(total * jnp.exp2(high - top), axis=0, keepdims=True))


def spread_rows(values, out_ref):
    for a in range(values.shape[0]):
        block = jnp.broadcast_to(values[a : a + 1, :], (LANES, LANES))
        out_ref[a * LANES : (a + 1) * LANES, :] = block.T


def peak_and_sum(tiles):
    high = tiles[0]
    for tile in tiles[1:]:
        high = jnp.maximum(high, tile)
    total = jnp.exp2(tiles[0] - high)
    for tile in tiles[1:]:
        total = total + jnp.exp2(tile - high)
    return high, total


def col_partial(cost_ref, row_ref, high_ref, total_ref):
    rows, cols = cost_ref.shape
    blocks, chunks = rows // LANES, cols // LANES
    groups = LANES // SUB

    def block_step(q, carry):
        start = pl.multiple_of(q * LANES, LANES)
        bases = None if row_ref is None else [row_ref[pl.ds(start + g * SUB, SUB), :] for g in range(groups)]
        for k in range(chunks):
            cells = [cost_ref[pl.ds(start + g * SUB, SUB), k * LANES : (k + 1) * LANES] for g in range(groups)]
            tiles = [-cell for cell in cells] if bases is None else [base - cell for base, cell in zip(bases, cells)]
            high, total = peak_and_sum(tiles)
            here = (pl.ds(pl.multiple_of(q * SUB, SUB), SUB), slice(k * LANES, (k + 1) * LANES))
            high_ref[here] = high
            total_ref[here] = total
        return carry

    lax.fori_loop(0, blocks, block_step, 0, unroll=True)
    out = [merge(high_ref[:, k * LANES : (k + 1) * LANES], total_ref[:, k * LANES : (k + 1) * LANES]) for k in range(chunks)]
    return jnp.concatenate(out, axis=0)


def row_partial(cost_ref, col, high_ref, total_ref):
    rows, cols = cost_ref.shape
    chunks = cols // LANES
    bases = None if col is None else [jnp.broadcast_to(col[k : k + 1, :], (SUB, LANES)) for k in range(chunks)]

    def group_step(g, carry):
        here = pl.ds(pl.multiple_of(g * SUB, SUB), SUB)
        cells = [cost_ref[here, k * LANES : (k + 1) * LANES] for k in range(chunks)]
        tiles = [-cell for cell in cells] if bases is None else [base - cell for base, cell in zip(bases, cells)]
        high_ref[here, :], total_ref[here, :] = peak_and_sum(tiles)
        return carry

    lax.fori_loop(0, rows // SUB, group_step, 0, unroll=4)
    out = []
    for a in range(rows // LANES):
        block = slice(a * LANES, (a + 1) * LANES)
        out.append(merge(high_ref[block, :].T, total_ref[block, :].T))
    return jnp.concatenate(out, axis=0)


def split3(values):
    high = values.astype(jnp.bfloat16)
    rest = values - high.astype(jnp.float32)
    mid = rest.astype(jnp.bfloat16)
    low = (rest - mid.astype(jnp.float32)).astype(jnp.bfloat16)
    return high, mid, low


def dot(left, right, dims):
    return lax.dot_general(left, right, (dims, ((), ())), preferred_element_type=jnp.float32)


def pack_kernel(
    train_label_hbm, train_hbm, valid_hbm, valid_label_hbm, train_out, valid_out,
    train_label_ref, train_ref, valid_label_ref, sems
):
    count, embed = train_hbm.shape
    points = valid_hbm.shape[0]
    pairs = (
        (train_label_hbm, train_label_ref),
        (train_hbm, train_ref),
        (valid_label_hbm, valid_label_ref),
        (valid_hbm, valid_out.at[:points, :]),
    )
    copies = [pltpu.make_async_copy(source, target, sems.at[i]) for i, (source, target) in enumerate(pairs)]
    for copy in copies:
        copy.start()
    for copy in copies:
        copy.wait()
    row_ids = lax.broadcasted_iota(jnp.int32, (count, LANES), 0)
    shown = jnp.zeros((count, LANES), jnp.int32)
    for i in range(count):
        shown = jnp.where(row_ids == i, train_label_ref[i], shown)
    packed = jnp.concatenate([train_ref[...], shown.astype(jnp.float32).astype(jnp.bfloat16)], axis=1)
    train_out[...] = jnp.broadcast_to(packed[None], train_out.shape)
    row = jnp.broadcast_to(valid_label_ref[...].astype(jnp.float32), (valid_out.shape[0] - points, LANES))
    valid_out[points:, :] = jnp.concatenate([row] * (embed // LANES), axis=1).astype(jnp.bfloat16)


def squared_sums(rows, ones, swap):
    wide = rows.astype(jnp.float32)
    squares = wide * wide
    high = squares.astype(jnp.bfloat16)
    low = (squares - high.astype(jnp.float32)).astype(jnp.bfloat16)
    if swap:
        return dot(ones, high, ((1,), (1,))) + dot(ones, low, ((1,), (1,)))
    return dot(high, ones, ((1,), (1,))) + dot(low, ones, ((1,), (1,)))


def valid_kernel(where_ref, mine_ref, other_ref, valid_ref, hot_ref, sq_ref):
    steps, sides, _, embed = mine_ref.shape
    ones = jnp.ones((SUB, embed), jnp.bfloat16)
    class_ids = lax.broadcasted_iota(jnp.int32, (LANES, LANES), 0).astype(jnp.float32)
    for k in range(2 * steps * sides):
        core, z_pair, side = k // (steps * sides), k // sides % steps, k % sides
        back = lax.rem(where_ref[0] - z_pair + steps, steps)
        slot = jnp.where(back < 2, back, 5 - back)
        block = jnp.where(where_ref[2] == core, mine_ref[slot, side], other_ref[slot, side])
        here = slice(k * LANES, (k + 1) * LANES)
        points = block[:LANES, :]
        label_row = block[LANES:, :LANES].astype(jnp.float32)[:1, :]
        valid_ref[here, :] = points
        hot_ref[:, here] = jnp.where(class_ids == label_row, 1.0, 0.0).astype(jnp.bfloat16)
        sq_ref[:, here] = squared_sums(points, ones, True) * (1.0 / embed)


def start_kernel(
    train_ref, table_ref, valid_ref, hot_ref, sq_ref, cost_ref, partial_ref, left_ref, row_a, row_b, col_a, col_b
):
    embed = valid_ref.shape[1]
    packed = train_ref[...].reshape(cost_ref.shape[0], embed + LANES)
    train = packed[:, :embed]
    train_sq = squared_sums(train, jnp.ones((LANES, embed), jnp.bfloat16), False) * (1.0 / embed)
    labels = packed[:, embed:].astype(jnp.float32)
    lane_ids = lax.broadcasted_iota(jnp.int32, labels.shape, 1).astype(jnp.float32)
    train_hot = jnp.where(labels == lane_ids, 1.0, 0.0).astype(jnp.bfloat16)
    table_parts = split3(table_ref[...])
    table_rows = dot(train_hot, jnp.concatenate(table_parts, axis=1), ((1,), (0,))).astype(jnp.bfloat16)
    left_ref[...] = jnp.concatenate([train * jnp.bfloat16(-2.0 / embed), table_rows], axis=1)
    step = 2 * LANES
    train_sq = jnp.concatenate([train_sq] * 2, axis=1)
    for pair in range(valid_ref.shape[0] // step):
        here = slice(pair * step, (pair + 1) * step)
        cost = dot(left_ref[:, :embed], valid_ref[here, :], ((1,), (1,)))
        hot = jnp.concatenate([hot_ref[:, here]] * len(table_parts), axis=0)
        cost = cost + dot(left_ref[:, embed:], hot, ((1,), (0,)))
        cost_ref[:, here] = (cost + (train_sq + sq_ref[:1, here])) * (1.0 / UNIT)
    put_partials(partial_ref, row_partial(cost_ref, None, row_a, row_b), col_partial(cost_ref, None, col_a, col_b))


def put_partials(out_ref, row, col):
    unused = jnp.zeros((out_ref.shape[0] - col.shape[0] - row.shape[0], LANES), jnp.float32)
    out_ref[...] = jnp.concatenate([col, row, unused], axis=0)


def share_kernel(flags_ref, partials_ref, out_ref, *, row_chunks):
    _, chunks, _ = out_ref.shape
    rows = [partials_ref[core, chunks : chunks + row_chunks, :] for core in range(2)]
    unused = jnp.zeros((chunks - 2 * row_chunks, LANES), jnp.float32)
    row_side = jnp.concatenate(rows + [unused], axis=0)
    col_side = lse_lead(partials_ref[:, :chunks, :])
    first_core = jnp.concatenate([flags_ref[0]] * (chunks // SUB), axis=0) > 0.5
    out_ref[...] = jnp.broadcast_to(jnp.where(first_core, row_side, col_side)[None], out_ref.shape)


def settle_kernel(flags_ref, parts_ref, out_ref):
    repeats = parts_ref.shape[1] // SUB
    lines = flags_ref.shape[0] - 1
    wanted = [jnp.concatenate([flags_ref[1 + line]] * repeats, axis=0) > 0.5 for line in range(lines)]
    parts = [jnp.where(wanted[k % lines], parts_ref[k], -jnp.inf) for k in range(parts_ref.shape[0])]
    high = parts[0]
    for part in parts[1:]:
        high = jnp.maximum(high, part)
    total = jnp.exp2(parts[0] - high)
    for part in parts[1:]:
        total = total + jnp.exp2(part - high)
    out_ref[...] = high + jnp.log2(total)


def updated(pot_ref, lse, offset):
    return 0.5 * (pot_ref[...] + (offset - lse))


def both_updated(flags_ref, lse_ref, row_pot, col_pot, row_offset, col_offset):
    chunks = row_pot.shape[0]
    first_core = flags_ref[0, :chunks, :] > 0.5
    rows = jnp.where(first_core, lse_ref[0, :chunks, :], lse_ref[0, chunks : 2 * chunks, :])
    return updated(row_pot, rows, row_offset), updated(col_pot, lse_ref[1], col_offset)


def both_kernel(
    flags_ref, cost_ref, lse_ref, row_pot, col_pot, partial_ref, row_new, col_new, row_a, row_b, col_a, col_b, spread_ref,
    *, row_offset, col_offset
):
    row, col = both_updated(flags_ref, lse_ref, row_pot, col_pot, row_offset, col_offset)
    row_new[...] = row
    col_new[...] = col
    spread_rows(row, spread_ref)
    put_partials(
        partial_ref, row_partial(cost_ref, col, row_a, row_b), col_partial(cost_ref, spread_ref, col_a, col_b)
    )


def last_row_kernel(
    flags_ref, cost_ref, lse_ref, row_pot, col_pot, row_out, row_new, row_a, row_b, *, row_offset, col_offset
):
    row, col = both_updated(flags_ref, lse_ref, row_pot, col_pot, row_offset, col_offset)
    row_new[...] = row
    row_out[...] = jnp.broadcast_to(row_partial(cost_ref, col, row_a, row_b)[None], row_out.shape)


def last_kernel(parts_ref, pot_ref, out_ref, copies_ref, *, offset):
    pot = updated(pot_ref, lse_lead(parts_ref[...]), offset)
    out_ref[...] = pot
    copies_ref[...] = jnp.broadcast_to(pot[None], copies_ref.shape)


def calibrate_kernel(parts_ref, pot_ref, out_ref, *, count):
    total = jnp.sum(jnp.sum(parts_ref[...], axis=0), keepdims=True)
    out_ref[...] = (pot_ref[...] * count - total) * (UNIT / (count - 1))


def exchange(block, axis):
    copies = block if block.ndim == 3 else jnp.broadcast_to(block[None], (lax.axis_size(axis),) + block.shape)
    return lax.all_to_all(copies, axis, 0, 0, tiled=True)


def core_groups():
    z_size, y_size, x_size = lax.axis_size(ROW[:2]), lax.axis_size("y"), lax.axis_size("x")

    def index(z, core, y, x):
        return ((z * 2 + core) * y_size + y) * x_size + x

    ys, xs, zs = range(y_size), range(x_size), range(z_size)
    over_yx = [[index(z, 0, y, x) for y in ys for x in xs] for z in zs]
    over_zx = [[index(z, 1, y, x) for z in zs for x in xs] for y in ys]
    return over_yx + over_zx


def call(kernel, out_shape, scratch, *args, smem=(), hbm=(), limit=8, **static):
    body = kernel if not static else (lambda *refs: kernel(*refs, **static))
    smem_spec, hbm_spec = pl.BlockSpec(memory_space=pltpu.SMEM), pl.BlockSpec(memory_space=pl.ANY)
    specs = [smem_spec if i in smem else hbm_spec if i in hbm else VMEM for i in range(len(args))]
    return pl.pallas_call(
        body,
        out_shape=out_shape,
        in_specs=specs,
        out_specs=[VMEM] * len(out_shape),
        scratch_shapes=scratch,
        compiler_params=pltpu.CompilerParams(vmem_limit_bytes=limit * 2**20),
        cost_estimate=pl.CostEstimate(flops=2**24, bytes_accessed=4 * 2**20, transcendentals=2**20),
    )(*args)


def shards(train_embed, valid_embed, train_labels, valid_labels, pair_level, level_cost):
    row_size, col_size = lax.axis_size(ROW), lax.axis_size(COL)
    f32 = jnp.float32
    embed = train_embed.shape[1]
    train_copies, valid_pack = call(
        pack_kernel,
        (
            jax.ShapeDtypeStruct((col_size, train_embed.shape[0], embed + LANES), jnp.bfloat16),
            jax.ShapeDtypeStruct((valid_embed.shape[0] + 16, embed), jnp.bfloat16),
        ),
        [
            pltpu.SMEM(train_labels.shape, jnp.int32),
            pltpu.VMEM(train_embed.shape, train_embed.dtype),
            pltpu.VMEM((1,) + valid_labels.shape, jnp.int32),
            pltpu.SemaphoreType.DMA((4,)),
        ],
        train_labels,
        train_embed,
        valid_embed,
        valid_labels[None, :],
        hbm=(0, 1, 2, 3),
        limit=60,
    )
    train_all = exchange(train_copies, COL)
    pair = lax.all_gather(valid_pack, "zl", axis=0)
    steps = lax.axis_size("zh")
    turn = [[(i, (i + k) % steps) for i in range(steps)] for k in range(steps)]
    mine = jnp.stack([pair] + [lax.ppermute(pair, "zh", turn[k]) for k in (1, 3, 2)])
    other = lax.ppermute(mine, "core", [(0, 1), (1, 0)])
    where = jnp.stack([lax.axis_index(axis) for axis in ROW + ("x",)]).astype(jnp.int32)
    rows, cols = train_embed.shape[0] * col_size, valid_embed.shape[0] * row_size
    row_chunks, col_chunks = rows // LANES, cols // LANES
    classes = pair_level.shape[0]
    level_ids = jnp.arange(level_cost.shape[0], dtype=jnp.int32)
    chosen = (pair_level[:, :, None] == level_ids).astype(f32)
    table = jnp.pad(jnp.sum(chosen * level_cost, axis=2), ((0, LANES - classes), (0, LANES - classes)))
    tile = jax.ShapeDtypeStruct((rows, cols), f32)
    row_copies = jax.ShapeDtypeStruct((col_size, row_chunks, LANES), f32)
    part_shape = jax.ShapeDtypeStruct((-(-(row_chunks + col_chunks) // SUB) * SUB, LANES), f32)
    sent_shape = jax.ShapeDtypeStruct((col_size, col_chunks, LANES), f32)
    row_shape = jax.ShapeDtypeStruct((row_chunks, LANES), f32)
    col_shape = jax.ShapeDtypeStruct((col_chunks, LANES), f32)
    tall = [pltpu.VMEM((rows, LANES), f32)] * 2
    wide = [pltpu.VMEM((row_chunks * SUB, cols), f32)] * 2
    valid_side = call(
        valid_kernel,
        (
            jax.ShapeDtypeStruct((cols, embed), jnp.bfloat16),
            jax.ShapeDtypeStruct((LANES, cols), jnp.bfloat16),
            jax.ShapeDtypeStruct((SUB, cols), f32),
        ),
        [],
        where,
        mine,
        other,
        smem=(0,),
    )
    cost, partials = call(
        start_kernel,
        (tile, part_shape),
        [pltpu.VMEM((rows, embed + 3 * LANES), jnp.bfloat16)] + tall + wide,
        train_all,
        table,
        *valid_side,
        limit=16,
    )
    full_rows, full_cols = rows * row_size, cols * col_size
    offsets = {"row_offset": math.log2(full_cols), "col_offset": math.log2(full_rows)}
    row_pot = jnp.zeros(row_shape.shape, f32)
    col_pot = jnp.zeros(col_shape.shape, f32)
    groups = core_groups()
    lines = jnp.arange(lax.axis_size("x"), dtype=jnp.int32)
    counts = jnp.logical_or(where[2] == 0, lines == where[3])
    flags = jnp.concatenate([where[2:3] == 0, counts]).astype(f32)
    flags = jnp.broadcast_to(flags[:, None, None], (lines.shape[0] + 1, SUB, LANES))
    for iteration in range(ITERS - 1):
        both_cores = lax.all_gather(partials, "core")
        (sent,) = call(share_kernel, (sent_shape,), [], flags, both_cores, row_chunks=row_chunks)
        got = lax.all_to_all(sent, ROW + COL, 0, 0, tiled=True, axis_index_groups=groups)
        (lse,) = call(settle_kernel, (col_shape,), [], flags, got)
        given = (flags, cost, lax.all_gather(lse, "core"), row_pot, col_pot)
        if iteration < ITERS - 2:
            partials, row_pot, col_pot = call(
                both_kernel, (part_shape, row_shape, col_shape), tall + wide + tall[:1], *given, **offsets
            )
        else:
            row_part, row_pot = call(last_row_kernel, (row_copies, row_shape), tall, *given, **offsets)
    row_got = exchange(row_part, COL)
    final_shape = jax.ShapeDtypeStruct((row_size, row_chunks, LANES), f32)
    final, copies = call(
        last_kernel, (row_shape, final_shape), [], row_got, row_pot, offset=offsets["row_offset"]
    )
    (out,) = call(calibrate_kernel, (row_shape,), [], exchange(copies, ROW), final, count=full_rows)
    return out.reshape(rows)


def solution(mesh):
    row_size, col_size = mesh.shape["row"], mesh.shape["col"]
    finer = jax.sharding.Mesh(mesh.devices.reshape(row_size // 4, 2, 2, col_size // 4, 4), ROW + COL)
    both = ROW + COL
    placed = (P(both, None), P(both, None), P(both), P(both), P(), P())
    return jax.shard_map(shards, mesh=finer, in_specs=placed, out_specs=P(ROW), check_vma=False)
```

```python
import math

import jax
import jax.numpy as jnp
from jax import lax
from jax.experimental import pallas as pl
from jax.experimental.pallas import tpu as pltpu
from jax.sharding import PartitionSpec as P

ITERS = 4
LANES = 128
SUB = 8

entropy_scale = 0.05
UNIT = entropy_scale * math.log(2.0)

ROW = ("zh", "zl", "core")
COL = ("y", "x")

VMEM = pl.BlockSpec(memory_space=pltpu.VMEM)


def lse_lead(parts):
    high = jnp.max(parts, axis=0)
    return high + jnp.log2(jnp.sum(jnp.exp2(parts - high[None]), axis=0))


def merge(high, total):
    top = jnp.max(high, axis=0, keepdims=True)
    return top + jnp.log2(jnp.sum(total * jnp.exp2(high - top), axis=0, keepdims=True))


def spread_rows(values, out_ref):
    for a in range(values.shape[0]):
        block = jnp.broadcast_to(values[a : a + 1, :], (LANES, LANES))
        out_ref[a * LANES : (a + 1) * LANES, :] = block.T


def tree(combine, tiles):
    while len(tiles) > 1:
        odd = tiles[len(tiles) // 2 * 2 :]
        tiles = [combine(left, right) for left, right in zip(tiles[::2], tiles[1::2])] + odd
    return tiles[0]


def peak_and_sum(tiles):
    high = tree(jnp.maximum, tiles)
    return high, tree(jnp.add, [jnp.exp2(tile - high) for tile in tiles])


def col_partial(cost_ref, row_ref, high_ref, total_ref):
    rows, cols = cost_ref.shape
    blocks, chunks = rows // LANES, cols // LANES
    groups = LANES // SUB

    def block_step(q, carry):
        start = pl.multiple_of(q * LANES, LANES)
        bases = None if row_ref is None else [row_ref[pl.ds(start + g * SUB, SUB), :] for g in range(groups)]
        for k in range(chunks):
            cells = [cost_ref[pl.ds(start + g * SUB, SUB), k * LANES : (k + 1) * LANES] for g in range(groups)]
            tiles = [-cell for cell in cells] if bases is None else [base - cell for base, cell in zip(bases, cells)]
            high, total = peak_and_sum(tiles)
            here = (pl.ds(pl.multiple_of(q * SUB, SUB), SUB), slice(k * LANES, (k + 1) * LANES))
            high_ref[here] = high
            total_ref[here] = total
        return carry

    lax.fori_loop(0, blocks, block_step, 0, unroll=True)
    out = [merge(high_ref[:, k * LANES : (k + 1) * LANES], total_ref[:, k * LANES : (k + 1) * LANES]) for k in range(chunks)]
    return jnp.concatenate(out, axis=0)


def row_partial(cost_ref, col, high_ref, total_ref):
    rows, cols = cost_ref.shape
    chunks = cols // LANES
    bases = None if col is None else [jnp.broadcast_to(col[k : k + 1, :], (SUB, LANES)) for k in range(chunks)]

    def group_step(g, carry):
        here = pl.ds(pl.multiple_of(g * SUB, SUB), SUB)
        cells = [cost_ref[here, k * LANES : (k + 1) * LANES] for k in range(chunks)]
        tiles = [-cell for cell in cells] if bases is None else [base - cell for base, cell in zip(bases, cells)]
        high_ref[here, :], total_ref[here, :] = peak_and_sum(tiles)
        return carry

    lax.fori_loop(0, rows // SUB, group_step, 0, unroll=4)
    out = []
    for a in range(rows // LANES):
        block = slice(a * LANES, (a + 1) * LANES)
        out.append(merge(high_ref[block, :].T, total_ref[block, :].T))
    return jnp.concatenate(out, axis=0)


def split3(values):
    high = values.astype(jnp.bfloat16)
    rest = values - high.astype(jnp.float32)
    mid = rest.astype(jnp.bfloat16)
    low = (rest - mid.astype(jnp.float32)).astype(jnp.bfloat16)
    return high, mid, low


def dot(left, right, dims):
    return lax.dot_general(left, right, (dims, ((), ())), preferred_element_type=jnp.float32)


def pack_kernel(
    train_label_hbm, train_hbm, valid_hbm, valid_label_hbm, train_out, valid_out,
    train_label_ref, train_ref, valid_label_ref, sems
):
    count, embed = train_hbm.shape
    points = valid_hbm.shape[0]
    pairs = (
        (train_label_hbm, train_label_ref),
        (train_hbm, train_ref),
        (valid_label_hbm, valid_label_ref),
        (valid_hbm, valid_out.at[:points, :]),
    )
    copies = [pltpu.make_async_copy(source, target, sems.at[i]) for i, (source, target) in enumerate(pairs)]
    for copy in copies:
        copy.start()
    for copy in copies:
        copy.wait()
    row_ids = lax.broadcasted_iota(jnp.int32, (count, LANES), 0)
    shown = jnp.zeros((count, LANES), jnp.int32)
    for i in range(count):
        shown = jnp.where(row_ids == i, train_label_ref[i], shown)
    packed = jnp.concatenate([train_ref[...], shown.astype(jnp.float32).astype(jnp.bfloat16)], axis=1)
    train_out[...] = jnp.broadcast_to(packed[None], train_out.shape)
    row = jnp.broadcast_to(valid_label_ref[...].astype(jnp.float32), (valid_out.shape[0] - points, LANES))
    valid_out[points:, :] = jnp.concatenate([row] * (embed // LANES), axis=1).astype(jnp.bfloat16)


def squared_sums(rows, ones, swap):
    wide = rows.astype(jnp.float32)
    squares = wide * wide
    high = squares.astype(jnp.bfloat16)
    low = (squares - high.astype(jnp.float32)).astype(jnp.bfloat16)
    if swap:
        return dot(ones, high, ((1,), (1,))) + dot(ones, low, ((1,), (1,)))
    return dot(high, ones, ((1,), (1,))) + dot(low, ones, ((1,), (1,)))


def valid_kernel(where_ref, mine_ref, other_ref, valid_ref, hot_ref, sq_ref):
    steps, sides, _, embed = mine_ref.shape
    ones = jnp.ones((SUB, embed), jnp.bfloat16)
    class_ids = lax.broadcasted_iota(jnp.int32, (LANES, LANES), 0).astype(jnp.float32)
    for k in range(2 * steps * sides):
        core, z_pair, side = k // (steps * sides), k // sides % steps, k % sides
        back = lax.rem(where_ref[0] - z_pair + steps, steps)
        block = jnp.where(where_ref[2] == core, mine_ref[back, side], other_ref[back, side])
        here = slice(k * LANES, (k + 1) * LANES)
        points = block[:LANES, :]
        label_row = block[LANES:, :LANES].astype(jnp.float32)[:1, :]
        valid_ref[here, :] = points
        hot_ref[:, here] = jnp.where(class_ids == label_row, 1.0, 0.0).astype(jnp.bfloat16)
        sq_ref[:, here] = squared_sums(points, ones, True) * (1.0 / embed)


def start_kernel(
    train_ref, table_ref, valid_ref, hot_ref, sq_ref, cost_ref, partial_ref, left_ref, row_a, row_b, col_a, col_b
):
    embed = valid_ref.shape[1]
    packed = train_ref[...].reshape(cost_ref.shape[0], embed + LANES)
    train = packed[:, :embed]
    train_sq = squared_sums(train, jnp.ones((LANES, embed), jnp.bfloat16), False) * (1.0 / embed)
    labels = packed[:, embed:].astype(jnp.float32)
    lane_ids = lax.broadcasted_iota(jnp.int32, labels.shape, 1).astype(jnp.float32)
    train_hot = jnp.where(labels == lane_ids, 1.0, 0.0).astype(jnp.bfloat16)
    table_parts = split3(table_ref[...])
    table_rows = dot(train_hot, jnp.concatenate(table_parts, axis=1), ((1,), (0,))).astype(jnp.bfloat16)
    left_ref[...] = jnp.concatenate([train * jnp.bfloat16(-2.0 / embed), table_rows], axis=1)
    step = 2 * LANES
    train_sq = jnp.concatenate([train_sq] * 2, axis=1)
    for pair in range(valid_ref.shape[0] // step):
        here = slice(pair * step, (pair + 1) * step)
        cost = dot(left_ref[:, :embed], valid_ref[here, :], ((1,), (1,)))
        hot = jnp.concatenate([hot_ref[:, here]] * len(table_parts), axis=0)
        cost = cost + dot(left_ref[:, embed:], hot, ((1,), (0,)))
        cost_ref[:, here] = (cost + (train_sq + sq_ref[:1, here])) * (1.0 / UNIT)
    put_partials(partial_ref, row_partial(cost_ref, None, row_a, row_b), col_partial(cost_ref, None, col_a, col_b))


def put_partials(out_ref, row, col):
    unused = jnp.zeros((out_ref.shape[0] - col.shape[0] - row.shape[0], LANES), jnp.float32)
    out_ref[...] = jnp.concatenate([col, row, unused], axis=0)


def share_kernel(flags_ref, partials_ref, out_ref, *, row_chunks):
    _, chunks, _ = out_ref.shape
    rows = [partials_ref[core, chunks : chunks + row_chunks, :] for core in range(2)]
    unused = jnp.zeros((chunks - 2 * row_chunks, LANES), jnp.float32)
    row_side = jnp.concatenate(rows + [unused], axis=0)
    col_side = lse_lead(partials_ref[:, :chunks, :])
    first_core = jnp.concatenate([flags_ref[0]] * (chunks // SUB), axis=0) > 0.5
    out_ref[...] = jnp.broadcast_to(jnp.where(first_core, row_side, col_side)[None], out_ref.shape)


def settle_kernel(flags_ref, parts_ref, out_ref):
    repeats = parts_ref.shape[1] // SUB
    lines = flags_ref.shape[0] - 1
    wanted = [jnp.concatenate([flags_ref[1 + line]] * repeats, axis=0) > 0.5 for line in range(lines)]
    parts = [jnp.where(wanted[k % lines], parts_ref[k], -jnp.inf) for k in range(parts_ref.shape[0])]
    high = parts[0]
    for part in parts[1:]:
        high = jnp.maximum(high, part)
    total = jnp.exp2(parts[0] - high)
    for part in parts[1:]:
        total = total + jnp.exp2(part - high)
    out_ref[...] = high + jnp.log2(total)


def updated(pot_ref, lse, offset):
    return 0.5 * (pot_ref[...] + (offset - lse))


def both_updated(flags_ref, lse_ref, row_pot, col_pot, row_offset, col_offset):
    chunks = row_pot.shape[0]
    first_core = flags_ref[0, :chunks, :] > 0.5
    rows = jnp.where(first_core, lse_ref[0, :chunks, :], lse_ref[0, chunks : 2 * chunks, :])
    return updated(row_pot, rows, row_offset), updated(col_pot, lse_ref[1], col_offset)


def both_kernel(
    flags_ref, cost_ref, lse_ref, row_pot, col_pot, partial_ref, row_new, col_new, row_a, row_b, col_a, col_b, spread_ref,
    *, row_offset, col_offset
):
    row, col = both_updated(flags_ref, lse_ref, row_pot, col_pot, row_offset, col_offset)
    row_new[...] = row
    col_new[...] = col
    spread_rows(row, spread_ref)
    put_partials(
        partial_ref, row_partial(cost_ref, col, row_a, row_b), col_partial(cost_ref, spread_ref, col_a, col_b)
    )


def last_row_kernel(
    flags_ref, cost_ref, lse_ref, row_pot, col_pot, row_out, row_new, row_a, row_b, *, row_offset, col_offset
):
    row, col = both_updated(flags_ref, lse_ref, row_pot, col_pot, row_offset, col_offset)
    row_new[...] = row
    row_out[...] = jnp.broadcast_to(row_partial(cost_ref, col, row_a, row_b)[None], row_out.shape)


def last_kernel(parts_ref, pot_ref, out_ref, copies_ref, *, offset):
    pot = updated(pot_ref, lse_lead(parts_ref[...]), offset)
    out_ref[...] = pot
    copies_ref[...] = jnp.broadcast_to(pot[None], copies_ref.shape)


def calibrate_kernel(parts_ref, pot_ref, out_ref, *, count):
    total = jnp.sum(jnp.sum(parts_ref[...], axis=0), keepdims=True)
    out_ref[...] = (pot_ref[...] * count - total) * (UNIT / (count - 1))


def exchange(block, axis):
    copies = block if block.ndim == 3 else jnp.broadcast_to(block[None], (lax.axis_size(axis),) + block.shape)
    return lax.all_to_all(copies, axis, 0, 0, tiled=True)


def core_groups():
    z_size, y_size, x_size = lax.axis_size(ROW[:2]), lax.axis_size("y"), lax.axis_size("x")

    def index(z, core, y, x):
        return ((z * 2 + core) * y_size + y) * x_size + x

    ys, xs, zs = range(y_size), range(x_size), range(z_size)
    over_yx = [[index(z, 0, y, x) for y in ys for x in xs] for z in zs]
    over_zx = [[index(z, 1, y, x) for z in zs for x in xs] for y in ys]
    return over_yx + over_zx


def call(kernel, out_shape, scratch, *args, smem=(), hbm=(), limit=8, **static):
    body = kernel if not static else (lambda *refs: kernel(*refs, **static))
    smem_spec, hbm_spec = pl.BlockSpec(memory_space=pltpu.SMEM), pl.BlockSpec(memory_space=pl.ANY)
    specs = [smem_spec if i in smem else hbm_spec if i in hbm else VMEM for i in range(len(args))]
    return pl.pallas_call(
        body,
        out_shape=out_shape,
        in_specs=specs,
        out_specs=[VMEM] * len(out_shape),
        scratch_shapes=scratch,
        compiler_params=pltpu.CompilerParams(vmem_limit_bytes=limit * 2**20),
        cost_estimate=pl.CostEstimate(flops=2**24, bytes_accessed=4 * 2**20, transcendentals=2**20),
    )(*args)


def shards(train_embed, valid_embed, train_labels, valid_labels, pair_level, level_cost):
    row_size, col_size = lax.axis_size(ROW), lax.axis_size(COL)
    f32 = jnp.float32
    embed = train_embed.shape[1]
    train_copies, valid_pack = call(
        pack_kernel,
        (
            jax.ShapeDtypeStruct((col_size, train_embed.shape[0], embed + LANES), jnp.bfloat16),
            jax.ShapeDtypeStruct((valid_embed.shape[0] + 16, embed), jnp.bfloat16),
        ),
        [
            pltpu.SMEM(train_labels.shape, jnp.int32),
            pltpu.VMEM(train_embed.shape, train_embed.dtype),
            pltpu.VMEM((1,) + valid_labels.shape, jnp.int32),
            pltpu.SemaphoreType.DMA((4,)),
        ],
        train_labels,
        train_embed,
        valid_embed,
        valid_labels[None, :],
        hbm=(0, 1, 2, 3),
        limit=60,
    )
    train_all = exchange(train_copies, COL)
    pair = lax.all_gather(valid_pack, "zl", axis=0)
    steps = lax.axis_size("zh")
    turn = [[(i, (i + k) % steps) for i in range(steps)] for k in range(steps)]
    mine = jnp.stack([pair] + [lax.ppermute(pair, "zh", turn[k]) for k in range(1, steps)])
    other = lax.ppermute(mine, "core", [(0, 1), (1, 0)])
    where = jnp.stack([lax.axis_index(axis) for axis in ROW + ("x",)]).astype(jnp.int32)
    rows, cols = train_embed.shape[0] * col_size, valid_embed.shape[0] * row_size
    row_chunks, col_chunks = rows // LANES, cols // LANES
    classes = pair_level.shape[0]
    level_ids = jnp.arange(level_cost.shape[0], dtype=jnp.int32)
    chosen = (pair_level[:, :, None] == level_ids).astype(f32)
    table = jnp.pad(jnp.sum(chosen * level_cost, axis=2), ((0, LANES - classes), (0, LANES - classes)))
    tile = jax.ShapeDtypeStruct((rows, cols), f32)
    row_copies = jax.ShapeDtypeStruct((col_size, row_chunks, LANES), f32)
    part_shape = jax.ShapeDtypeStruct((-(-(row_chunks + col_chunks) // SUB) * SUB, LANES), f32)
    sent_shape = jax.ShapeDtypeStruct((col_size, col_chunks, LANES), f32)
    row_shape = jax.ShapeDtypeStruct((row_chunks, LANES), f32)
    col_shape = jax.ShapeDtypeStruct((col_chunks, LANES), f32)
    tall = [pltpu.VMEM((rows, LANES), f32)] * 2
    wide = [pltpu.VMEM((row_chunks * SUB, cols), f32)] * 2
    valid_side = call(
        valid_kernel,
        (
            jax.ShapeDtypeStruct((cols, embed), jnp.bfloat16),
            jax.ShapeDtypeStruct((LANES, cols), jnp.bfloat16),
            jax.ShapeDtypeStruct((SUB, cols), f32),
        ),
        [],
        where,
        mine,
        other,
        smem=(0,),
    )
    cost, partials = call(
        start_kernel,
        (tile, part_shape),
        [pltpu.VMEM((rows, embed + 3 * LANES), jnp.bfloat16)] + tall + wide,
        train_all,
        table,
        *valid_side,
        limit=16,
    )
    full_rows, full_cols = rows * row_size, cols * col_size
    offsets = {"row_offset": math.log2(full_cols), "col_offset": math.log2(full_rows)}
    row_pot = jnp.zeros(row_shape.shape, f32)
    col_pot = jnp.zeros(col_shape.shape, f32)
    groups = core_groups()
    lines = jnp.arange(lax.axis_size("x"), dtype=jnp.int32)
    counts = jnp.logical_or(where[2] == 0, lines == where[3])
    flags = jnp.concatenate([where[2:3] == 0, counts]).astype(f32)
    flags = jnp.broadcast_to(flags[:, None, None], (lines.shape[0] + 1, SUB, LANES))
    for iteration in range(ITERS - 1):
        both_cores = lax.all_gather(partials, "core")
        (sent,) = call(share_kernel, (sent_shape,), [], flags, both_cores, row_chunks=row_chunks)
        got = lax.all_to_all(sent, ROW + COL, 0, 0, tiled=True, axis_index_groups=groups)
        (lse,) = call(settle_kernel, (col_shape,), [], flags, got)
        given = (flags, cost, lax.all_gather(lse, "core"), row_pot, col_pot)
        if iteration < ITERS - 2:
            partials, row_pot, col_pot = call(
                both_kernel, (part_shape, row_shape, col_shape), tall + wide + tall[:1], *given, **offsets
            )
        else:
            row_part, row_pot = call(last_row_kernel, (row_copies, row_shape), tall, *given, **offsets)
    row_got = exchange(row_part, COL)
    final_shape = jax.ShapeDtypeStruct((row_size, row_chunks, LANES), f32)
    final, copies = call(
        last_kernel, (row_shape, final_shape), [], row_got, row_pot, offset=offsets["row_offset"]
    )
    (out,) = call(calibrate_kernel, (row_shape,), [], exchange(copies, ROW), final, count=full_rows)
    return out.reshape(rows)


def solution(mesh):
    row_size, col_size = mesh.shape["row"], mesh.shape["col"]
    finer = jax.sharding.Mesh(mesh.devices.reshape(row_size // 4, 2, 2, col_size // 4, 4), ROW + COL)
    both = ROW + COL
    placed = (P(both, None), P(both, None), P(both), P(both), P(), P())
    return jax.shard_map(shards, mesh=finer, in_specs=placed, out_specs=P(ROW), check_vma=False)
```

```python
import math

import jax
import jax.numpy as jnp
from jax import lax
from jax.experimental import pallas as pl
from jax.experimental.pallas import tpu as pltpu
from jax.sharding import PartitionSpec as P

ITERS = 4
LANES = 128
SUB = 8

entropy_scale = 0.05
UNIT = entropy_scale * math.log(2.0)

ROW = ("zh", "zl", "core")
COL = ("y", "x")

VMEM = pl.BlockSpec(memory_space=pltpu.VMEM)


def lse_lead(parts):
    high = jnp.max(parts, axis=0)
    return high + jnp.log2(jnp.sum(jnp.exp2(parts - high[None]), axis=0))


def merge(high, total):
    top = jnp.max(high, axis=0, keepdims=True)
    return top + jnp.log2(jnp.sum(total * jnp.exp2(high - top), axis=0, keepdims=True))


def spread_rows(values, out_ref):
    for a in range(values.shape[0]):
        block = jnp.broadcast_to(values[a : a + 1, :], (LANES, LANES))
        out_ref[a * LANES : (a + 1) * LANES, :] = block.T


def peak_and_sum(tiles):
    high = tiles[0]
    for tile in tiles[1:]:
        high = jnp.maximum(high, tile)
    total = jnp.exp2(tiles[0] - high)
    for tile in tiles[1:]:
        total = total + jnp.exp2(tile - high)
    return high, total


def col_partial(cost_ref, row_ref, high_ref, total_ref):
    rows, cols = cost_ref.shape
    blocks, chunks = rows // LANES, cols // LANES
    groups = LANES // SUB

    def block_step(q, carry):
        start = pl.multiple_of(q * LANES, LANES)
        bases = None if row_ref is None else [row_ref[pl.ds(start + g * SUB, SUB), :] for g in range(groups)]
        for k in range(chunks):
            cells = [cost_ref[pl.ds(start + g * SUB, SUB), k * LANES : (k + 1) * LANES] for g in range(groups)]
            tiles = [-cell for cell in cells] if bases is None else [base - cell for base, cell in zip(bases, cells)]
            high, total = peak_and_sum(tiles)
            here = (pl.ds(pl.multiple_of(q * SUB, SUB), SUB), slice(k * LANES, (k + 1) * LANES))
            high_ref[here] = high
            total_ref[here] = total
        return carry

    lax.fori_loop(0, blocks, block_step, 0, unroll=True)
    out = [merge(high_ref[:, k * LANES : (k + 1) * LANES], total_ref[:, k * LANES : (k + 1) * LANES]) for k in range(chunks)]
    return jnp.concatenate(out, axis=0)


def row_partial(cost_ref, col, high_ref, total_ref):
    rows, cols = cost_ref.shape
    chunks = cols // LANES
    bases = None if col is None else [jnp.broadcast_to(col[k : k + 1, :], (SUB, LANES)) for k in range(chunks)]

    def group_step(g, carry):
        here = pl.ds(pl.multiple_of(g * SUB, SUB), SUB)
        cells = [cost_ref[here, k * LANES : (k + 1) * LANES] for k in range(chunks)]
        tiles = [-cell for cell in cells] if bases is None else [base - cell for base, cell in zip(bases, cells)]
        high_ref[here, :], total_ref[here, :] = peak_and_sum(tiles)
        return carry

    lax.fori_loop(0, rows // SUB, group_step, 0, unroll=8)
    out = []
    for a in range(rows // LANES):
        block = slice(a * LANES, (a + 1) * LANES)
        out.append(merge(high_ref[block, :].T, total_ref[block, :].T))
    return jnp.concatenate(out, axis=0)


def split3(values):
    high = values.astype(jnp.bfloat16)
    rest = values - high.astype(jnp.float32)
    mid = rest.astype(jnp.bfloat16)
    low = (rest - mid.astype(jnp.float32)).astype(jnp.bfloat16)
    return high, mid, low


def dot(left, right, dims):
    return lax.dot_general(left, right, (dims, ((), ())), preferred_element_type=jnp.float32)


def pack_kernel(
    train_label_hbm, train_hbm, valid_hbm, valid_label_hbm, train_out, valid_out,
    train_label_ref, train_ref, valid_label_ref, sems
):
    count, embed = train_hbm.shape
    points = valid_hbm.shape[0]
    pairs = (
        (train_label_hbm, train_label_ref),
        (train_hbm, train_ref),
        (valid_label_hbm, valid_label_ref),
        (valid_hbm, valid_out.at[:points, :]),
    )
    copies = [pltpu.make_async_copy(source, target, sems.at[i]) for i, (source, target) in enumerate(pairs)]
    for copy in copies:
        copy.start()
    for copy in copies:
        copy.wait()
    row_ids = lax.broadcasted_iota(jnp.int32, (count, LANES), 0)
    shown = jnp.zeros((count, LANES), jnp.int32)
    for i in range(count):
        shown = jnp.where(row_ids == i, train_label_ref[i], shown)
    packed = jnp.concatenate([train_ref[...], shown.astype(jnp.float32).astype(jnp.bfloat16)], axis=1)
    train_out[...] = jnp.broadcast_to(packed[None], train_out.shape)
    row = jnp.broadcast_to(valid_label_ref[...].astype(jnp.float32), (valid_out.shape[0] - points, LANES))
    valid_out[points:, :] = jnp.concatenate([row] * (embed // LANES), axis=1).astype(jnp.bfloat16)


def squared_sums(rows, ones, swap):
    wide = rows.astype(jnp.float32)
    squares = wide * wide
    high = squares.astype(jnp.bfloat16)
    low = (squares - high.astype(jnp.float32)).astype(jnp.bfloat16)
    if swap:
        return dot(ones, high, ((1,), (1,))) + dot(ones, low, ((1,), (1,)))
    return dot(high, ones, ((1,), (1,))) + dot(low, ones, ((1,), (1,)))


def valid_kernel(where_ref, mine_ref, other_ref, valid_ref, hot_ref, sq_ref):
    steps, sides, _, embed = mine_ref.shape
    ones = jnp.ones((SUB, embed), jnp.bfloat16)
    class_ids = lax.broadcasted_iota(jnp.int32, (LANES, LANES), 0).astype(jnp.float32)
    for k in range(2 * steps * sides):
        core, z_pair, side = k // (steps * sides), k // sides % steps, k % sides
        back = lax.rem(where_ref[0] - z_pair + steps, steps)
        block = jnp.where(where_ref[2] == core, mine_ref[back, side], other_ref[back, side])
        here = slice(k * LANES, (k + 1) * LANES)
        points = block[:LANES, :]
        label_row = block[LANES:, :LANES].astype(jnp.float32)[:1, :]
        valid_ref[here, :] = points
        hot_ref[:, here] = jnp.where(class_ids == label_row, 1.0, 0.0).astype(jnp.bfloat16)
        sq_ref[:, here] = squared_sums(points, ones, True) * (1.0 / embed)


def start_kernel(
    train_ref, table_ref, valid_ref, hot_ref, sq_ref, cost_ref, partial_ref, left_ref, row_a, row_b, col_a, col_b
):
    embed = valid_ref.shape[1]
    packed = train_ref[...].reshape(cost_ref.shape[0], embed + LANES)
    train = packed[:, :embed]
    train_sq = squared_sums(train, jnp.ones((LANES, embed), jnp.bfloat16), False) * (1.0 / embed)
    labels = packed[:, embed:].astype(jnp.float32)
    lane_ids = lax.broadcasted_iota(jnp.int32, labels.shape, 1).astype(jnp.float32)
    train_hot = jnp.where(labels == lane_ids, 1.0, 0.0).astype(jnp.bfloat16)
    table_parts = split3(table_ref[...])
    table_rows = dot(train_hot, jnp.concatenate(table_parts, axis=1), ((1,), (0,))).astype(jnp.bfloat16)
    left_ref[...] = jnp.concatenate([train * jnp.bfloat16(-2.0 / embed), table_rows], axis=1)
    step = 2 * LANES
    train_sq = jnp.concatenate([train_sq] * 2, axis=1)
    for pair in range(valid_ref.shape[0] // step):
        here = slice(pair * step, (pair + 1) * step)
        cost = dot(left_ref[:, :embed], valid_ref[here, :], ((1,), (1,)))
        hot = jnp.concatenate([hot_ref[:, here]] * len(table_parts), axis=0)
        cost = cost + dot(left_ref[:, embed:], hot, ((1,), (0,)))
        cost_ref[:, here] = (cost + (train_sq + sq_ref[:1, here])) * (1.0 / UNIT)
    put_partials(partial_ref, row_partial(cost_ref, None, row_a, row_b), col_partial(cost_ref, None, col_a, col_b))


def put_partials(out_ref, row, col):
    unused = jnp.zeros((out_ref.shape[0] - col.shape[0] - row.shape[0], LANES), jnp.float32)
    out_ref[...] = jnp.concatenate([col, row, unused], axis=0)


def share_kernel(flags_ref, partials_ref, out_ref, *, row_chunks):
    _, chunks, _ = out_ref.shape
    rows = [partials_ref[core, chunks : chunks + row_chunks, :] for core in range(2)]
    unused = jnp.zeros((chunks - 2 * row_chunks, LANES), jnp.float32)
    row_side = jnp.concatenate(rows + [unused], axis=0)
    col_side = lse_lead(partials_ref[:, :chunks, :])
    first_core = jnp.concatenate([flags_ref[0]] * (chunks // SUB), axis=0) > 0.5
    out_ref[...] = jnp.broadcast_to(jnp.where(first_core, row_side, col_side)[None], out_ref.shape)


def settle_kernel(flags_ref, parts_ref, out_ref):
    repeats = parts_ref.shape[1] // SUB
    lines = flags_ref.shape[0] - 1
    wanted = [jnp.concatenate([flags_ref[1 + line]] * repeats, axis=0) > 0.5 for line in range(lines)]
    parts = [jnp.where(wanted[k % lines], parts_ref[k], -jnp.inf) for k in range(parts_ref.shape[0])]
    high = parts[0]
    for part in parts[1:]:
        high = jnp.maximum(high, part)
    total = jnp.exp2(parts[0] - high)
    for part in parts[1:]:
        total = total + jnp.exp2(part - high)
    out_ref[...] = high + jnp.log2(total)


def updated(pot_ref, lse, offset):
    return 0.5 * (pot_ref[...] + (offset - lse))


def both_updated(flags_ref, lse_ref, row_pot, col_pot, row_offset, col_offset):
    chunks = row_pot.shape[0]
    first_core = flags_ref[0, :chunks, :] > 0.5
    rows = jnp.where(first_core, lse_ref[0, :chunks, :], lse_ref[0, chunks : 2 * chunks, :])
    return updated(row_pot, rows, row_offset), updated(col_pot, lse_ref[1], col_offset)


def both_kernel(
    flags_ref, cost_ref, lse_ref, row_pot, col_pot, partial_ref, row_new, col_new, row_a, row_b, col_a, col_b, spread_ref,
    *, row_offset, col_offset
):
    row, col = both_updated(flags_ref, lse_ref, row_pot, col_pot, row_offset, col_offset)
    row_new[...] = row
    col_new[...] = col
    spread_rows(row, spread_ref)
    put_partials(
        partial_ref, row_partial(cost_ref, col, row_a, row_b), col_partial(cost_ref, spread_ref, col_a, col_b)
    )


def last_row_kernel(
    flags_ref, cost_ref, lse_ref, row_pot, col_pot, row_out, row_new, row_a, row_b, *, row_offset, col_offset
):
    row, col = both_updated(flags_ref, lse_ref, row_pot, col_pot, row_offset, col_offset)
    row_new[...] = row
    row_out[...] = jnp.broadcast_to(row_partial(cost_ref, col, row_a, row_b)[None], row_out.shape)


def last_kernel(parts_ref, pot_ref, out_ref, copies_ref, *, offset):
    pot = updated(pot_ref, lse_lead(parts_ref[...]), offset)
    out_ref[...] = pot
    copies_ref[...] = jnp.broadcast_to(pot[None], copies_ref.shape)


def calibrate_kernel(parts_ref, pot_ref, out_ref, *, count):
    total = jnp.sum(jnp.sum(parts_ref[...], axis=0), keepdims=True)
    out_ref[...] = (pot_ref[...] * count - total) * (UNIT / (count - 1))


def exchange(block, axis):
    copies = block if block.ndim == 3 else jnp.broadcast_to(block[None], (lax.axis_size(axis),) + block.shape)
    return lax.all_to_all(copies, axis, 0, 0, tiled=True)


def core_groups():
    z_size, y_size, x_size = lax.axis_size(ROW[:2]), lax.axis_size("y"), lax.axis_size("x")

    def index(z, core, y, x):
        return ((z * 2 + core) * y_size + y) * x_size + x

    ys, xs, zs = range(y_size), range(x_size), range(z_size)
    over_yx = [[index(z, 0, y, x) for y in ys for x in xs] for z in zs]
    over_zx = [[index(z, 1, y, x) for z in zs for x in xs] for y in ys]
    return over_yx + over_zx


def call(kernel, out_shape, scratch, *args, smem=(), hbm=(), limit=8, **static):
    body = kernel if not static else (lambda *refs: kernel(*refs, **static))
    smem_spec, hbm_spec = pl.BlockSpec(memory_space=pltpu.SMEM), pl.BlockSpec(memory_space=pl.ANY)
    specs = [smem_spec if i in smem else hbm_spec if i in hbm else VMEM for i in range(len(args))]
    return pl.pallas_call(
        body,
        out_shape=out_shape,
        in_specs=specs,
        out_specs=[VMEM] * len(out_shape),
        scratch_shapes=scratch,
        compiler_params=pltpu.CompilerParams(vmem_limit_bytes=limit * 2**20),
        cost_estimate=pl.CostEstimate(flops=2**24, bytes_accessed=4 * 2**20, transcendentals=2**20),
    )(*args)


def shards(train_embed, valid_embed, train_labels, valid_labels, pair_level, level_cost):
    row_size, col_size = lax.axis_size(ROW), lax.axis_size(COL)
    f32 = jnp.float32
    embed = train_embed.shape[1]
    train_copies, valid_pack = call(
        pack_kernel,
        (
            jax.ShapeDtypeStruct((col_size, train_embed.shape[0], embed + LANES), jnp.bfloat16),
            jax.ShapeDtypeStruct((valid_embed.shape[0] + 16, embed), jnp.bfloat16),
        ),
        [
            pltpu.SMEM(train_labels.shape, jnp.int32),
            pltpu.VMEM(train_embed.shape, train_embed.dtype),
            pltpu.VMEM((1,) + valid_labels.shape, jnp.int32),
            pltpu.SemaphoreType.DMA((4,)),
        ],
        train_labels,
        train_embed,
        valid_embed,
        valid_labels[None, :],
        hbm=(0, 1, 2, 3),
        limit=60,
    )
    train_all = exchange(train_copies, COL)
    pair = lax.all_gather(valid_pack, "zl", axis=0)
    steps = lax.axis_size("zh")
    turn = [[(i, (i + k) % steps) for i in range(steps)] for k in range(steps)]
    mine = jnp.stack([pair] + [lax.ppermute(pair, "zh", turn[k]) for k in range(1, steps)])
    other = lax.ppermute(mine, "core", [(0, 1), (1, 0)])
    where = jnp.stack([lax.axis_index(axis) for axis in ROW + ("x",)]).astype(jnp.int32)
    rows, cols = train_embed.shape[0] * col_size, valid_embed.shape[0] * row_size
    row_chunks, col_chunks = rows // LANES, cols // LANES
    classes = pair_level.shape[0]
    level_ids = jnp.arange(level_cost.shape[0], dtype=jnp.int32)
    chosen = (pair_level[:, :, None] == level_ids).astype(f32)
    table = jnp.pad(jnp.sum(chosen * level_cost, axis=2), ((0, LANES - classes), (0, LANES - classes)))
    tile = jax.ShapeDtypeStruct((rows, cols), f32)
    row_copies = jax.ShapeDtypeStruct((col_size, row_chunks, LANES), f32)
    part_shape = jax.ShapeDtypeStruct((-(-(row_chunks + col_chunks) // SUB) * SUB, LANES), f32)
    sent_shape = jax.ShapeDtypeStruct((col_size, col_chunks, LANES), f32)
    row_shape = jax.ShapeDtypeStruct((row_chunks, LANES), f32)
    col_shape = jax.ShapeDtypeStruct((col_chunks, LANES), f32)
    tall = [pltpu.VMEM((rows, LANES), f32)] * 2
    wide = [pltpu.VMEM((row_chunks * SUB, cols), f32)] * 2
    valid_side = call(
        valid_kernel,
        (
            jax.ShapeDtypeStruct((cols, embed), jnp.bfloat16),
            jax.ShapeDtypeStruct((LANES, cols), jnp.bfloat16),
            jax.ShapeDtypeStruct((SUB, cols), f32),
        ),
        [],
        where,
        mine,
        other,
        smem=(0,),
    )
    cost, partials = call(
        start_kernel,
        (tile, part_shape),
        [pltpu.VMEM((rows, embed + 3 * LANES), jnp.bfloat16)] + tall + wide,
        train_all,
        table,
        *valid_side,
        limit=16,
    )
    full_rows, full_cols = rows * row_size, cols * col_size
    offsets = {"row_offset": math.log2(full_cols), "col_offset": math.log2(full_rows)}
    row_pot = jnp.zeros(row_shape.shape, f32)
    col_pot = jnp.zeros(col_shape.shape, f32)
    groups = core_groups()
    lines = jnp.arange(lax.axis_size("x"), dtype=jnp.int32)
    counts = jnp.logical_or(where[2] == 0, lines == where[3])
    flags = jnp.concatenate([where[2:3] == 0, counts]).astype(f32)
    flags = jnp.broadcast_to(flags[:, None, None], (lines.shape[0] + 1, SUB, LANES))
    for iteration in range(ITERS - 1):
        both_cores = lax.all_gather(partials, "core")
        (sent,) = call(share_kernel, (sent_shape,), [], flags, both_cores, row_chunks=row_chunks)
        got = lax.all_to_all(sent, ROW + COL, 0, 0, tiled=True, axis_index_groups=groups)
        (lse,) = call(settle_kernel, (col_shape,), [], flags, got)
        given = (flags, cost, lax.all_gather(lse, "core"), row_pot, col_pot)
        if iteration < ITERS - 2:
            partials, row_pot, col_pot = call(
                both_kernel, (part_shape, row_shape, col_shape), tall + wide + tall[:1], *given, **offsets
            )
        else:
            row_part, row_pot = call(last_row_kernel, (row_copies, row_shape), tall, *given, **offsets)
    row_got = exchange(row_part, COL)
    final_shape = jax.ShapeDtypeStruct((row_size, row_chunks, LANES), f32)
    final, copies = call(
        last_kernel, (row_shape, final_shape), [], row_got, row_pot, offset=offsets["row_offset"]
    )
    (out,) = call(calibrate_kernel, (row_shape,), [], exchange(copies, ROW), final, count=full_rows)
    return out.reshape(rows)


def solution(mesh):
    row_size, col_size = mesh.shape["row"], mesh.shape["col"]
    finer = jax.sharding.Mesh(mesh.devices.reshape(row_size // 4, 2, 2, col_size // 4, 4), ROW + COL)
    both = ROW + COL
    placed = (P(both, None), P(both, None), P(both), P(both), P(), P())
    return jax.shard_map(shards, mesh=finer, in_specs=placed, out_specs=P(ROW), check_vma=False)
```
